32 devices in a mesh: dp: 16 (over z, x, core), seq: 2 (over y).
Axes of the slice: x: 2, y: 2, z: 4, core: 2. Of those that a mesh axis runs over, the one named last changes fastest.
Arguments:
- hidden_in: bfloat16 [16, 260, 1152], P('dp', 'seq'), may hold values from -6 to 6
- skip_in: bfloat16 [16, 260, 1152], P('dp', None, 'seq'), may hold values from -6 to 6
- cotangent: bfloat16 [16, 260, 1152], P('dp', 'seq'), may hold values from -6 to 6
- timesteps: int32 [16], P('dp'), may hold values from 0 to 999, as said below
- counts: int32 [16], P('dp'), may hold values from 1 to 1, as said below
- w_skip: bfloat16 [2304, 1152], replicated, may hold values from -0.125 to 0.125
- w_qkv: bfloat16 [1152, 3456], replicated, may hold values from -0.1875 to 0.1875
- w_proj: bfloat16 [1152, 1152], replicated, may hold values from -0.75 to 0.75
- w_fc1: bfloat16 [1152, 4608], replicated, may hold values from -0.1875 to 0.1875
- w_fc2: bfloat16 [4608, 1152], replicated, may hold values from -0.09375 to 0.09375
- gains: float32 [2, 1152], replicated, may hold values from 0.1 to 1.9
- biases: float32 [5, 1152], replicated, may hold values from -2 to 2
- fc1_bias: float32 [4608], replicated, may hold values from -3 to 3
Outputs:
- output: bfloat16 [16, 260, 1152], P('dp', 'seq')
- grad_hidden: bfloat16 [16, 260, 1152], P('dp', 'seq')
- grad_skip: bfloat16 [16, 260, 1152], P('dp', None, 'seq')
- grad_w_skip: float32 [2304, 1152], P('dp', 'seq')
- grad_w_qkv: float32 [1152, 3456], P('seq', 'dp')
- grad_w_proj: float32 [1152, 1152], P('dp', 'seq')
- grad_w_fc1: float32 [1152, 4608], P('seq', 'dp')
- grad_w_fc2: float32 [4608, 1152], P('dp', 'seq')
- grad_gains: float32 [2, 1152], replicated
- grad_biases: float32 [5, 1152], replicated
- grad_fc1_bias: float32 [4608], replicated
The draws below stay inside these ranges and needn't reach their ends.
Inputs may be any that keep to these rules, and one draw needn't show every extreme that they name: timesteps; larger ones are more frequent. The first counts[g] of the 1 slots of data group g hold live items, the others are empty; some group is full.
All inputs are finite; a program needn't handle non-finite values.
Results may differ from the reference program's by a relative error of at most 0.015.
Values may be sent and summed in bfloat16 or wider, within the bound.
No kernel may reach another device: no remote copies, remote signals or barrier semaphores. Data moves between devices by JAX's collectives and lax.ppermute only.
A program may use at most 384 MiB of HBM per device.

```python
import jax
import jax.numpy as jnp
from jax import lax

D = 1152
HEADS = 16
FF = 4608
POS = 260
PADDED = 2
TSTEPS = 1000
SLOTS = 1
ITEMS = 16
N_DP = 16


def draw_timesteps(key, part):
    key = jax.random.fold_in(key, 11)
    first_key, second_key = jax.random.split(key)
    first = jax.random.randint(first_key, (ITEMS,), 0, TSTEPS)
    second = jax.random.randint(second_key, (ITEMS,), 0, TSTEPS)
    return jnp.maximum(first, second).astype(jnp.int32)


def draw_counts(key, part):
    key = jax.random.fold_in(key, 23)
    base_key, full_key = jax.random.split(key)
    base = jax.random.randint(base_key, (N_DP,), 1, SLOTS + 1)
    full_group = jax.random.randint(full_key, (), 0, N_DP)
    return jnp.where(jnp.arange(N_DP) == full_group, SLOTS, base).astype(jnp.int32)


def shard_levels(key, extent, cuts, smallest, top_value):
    def one(dim, blocks):
        steps = jax.random.uniform(jax.random.fold_in(jax.random.fold_in(key, 6), dim), (blocks,), jnp.float32, smallest / len(cuts), top_value / len(cuts))
        return jnp.repeat(jnp.exp(steps), extent[dim] // blocks).reshape((-1,) + (1,) * (len(extent) - dim - 1))

    loudness = one(*cuts[0])
    for cut in cuts[1:]:
        loudness = loudness * one(*cut)
    return loudness


def noise(stream_key, extent, width, most, shards=(), dtype=jnp.bfloat16):
    values = jax.random.normal(stream_key, extent, jnp.float32) * width
    if len(shards) > 0:
        values = shard_levels(stream_key, extent, shards, -0.22, 0.18) * values
    return jnp.clip(values, min=-most, max=most).astype(dtype)


def setup_inputs(seed: int = 0) -> dict:
    arg_keys = jax.random.split(jax.random.key(seed), 14)
    hidden_in = noise(arg_keys[0], (ITEMS, POS, D), 1.0, 6.0, ((0, 16), (1, 2)))
    skip_in = noise(arg_keys[1], (ITEMS, POS, D), 1.0, 6.0, ((0, 16), (2, 2)))
    cotangent = noise(arg_keys[2], (ITEMS, POS, D), 1.0, 6.0, ((0, 16), (1, 2)))
    timesteps = draw_timesteps(jax.random.fold_in(arg_keys[13], 71), 0)
    counts = draw_counts(jax.random.fold_in(arg_keys[13], 71), 0)
    w_skip = noise(arg_keys[5], (2 * D, D), (2 * D) ** -0.5, 0.125)
    w_qkv = noise(arg_keys[6], (D, 3 * D), D ** -0.5, 0.1875)
    w_proj = noise(arg_keys[7], (D, D), (D // 16) ** -0.5, 0.75)
    w_fc1 = noise(arg_keys[8], (D, FF), D ** -0.5, 0.1875)
    w_fc2 = noise(arg_keys[9], (FF, D), FF ** -0.5, 0.09375)
    gains = jnp.clip(1.0 + 0.18 * jax.random.normal(arg_keys[10], (2, D), jnp.float32), 0.1, 1.9)
    biases = noise(arg_keys[11], (5, D), 0.3, 2.0, (), jnp.float32)
    fc1_bias = noise(arg_keys[12], (FF,), 0.5, 3.0, (), jnp.float32)
    return dict(hidden_in=hidden_in, skip_in=skip_in, cotangent=cotangent, timesteps=timesteps, counts=counts, w_skip=w_skip, w_qkv=w_qkv, w_proj=w_proj, w_fc1=w_fc1, w_fc2=w_fc2, gains=gains, biases=biases, fc1_bias=fc1_bias)


EPSILON = 1e-06
NEG_FILL = -1e+30
HIGH = lax.Precision.HIGHEST

@jax.custom_vjp
def low(v):
    return lax.optimization_barrier(v.astype(jnp.bfloat16)).astype(jnp.float32)

@jax.custom_vjp
def low_back(v):
    return v

def low_keep(v):
    return (low(v), None)

def low_pass(kept, grad):
    return (grad,)

def back_keep(v):
    return (v, None)

def back_low(kept, grad):
    return (low(grad),)
low.defvjp(low_keep, low_pass)
low_back.defvjp(back_keep, back_low)

def layer_norm(value, gain, shift):
    center = value - lax.optimization_barrier(jnp.mean(value, axis=-1, keepdims=True))
    spread = lax.optimization_barrier(jnp.mean(center * center, axis=-1, keepdims=True))
    return center * lax.rsqrt(spread + EPSILON) * gain + shift

def matmul(left, right):
    return jnp.dot(left, right, precision=HIGH)

def forward(params, hidden, skipped, row_mask):
    w_skip, w_qkv, w_proj, w_fc1, w_fc2, gains, biases, fc1_bias = params
    item_count = hidden.shape[0]
    row_count = item_count * POS
    head_dim = D // HEADS
    joined = jnp.concatenate([hidden, skipped], axis=-1).reshape(row_count, 2 * D)
    merged = low_back(matmul(joined, w_skip)) + biases[0]
    normed_one = low(layer_norm(merged, gains[0], biases[1]))
    project = low(low_back(matmul(normed_one, w_qkv)))
    queries = project[:, :D].reshape(item_count, POS, HEADS, head_dim)
    keys_all = project[:, D:2 * D].reshape(item_count, POS, HEADS, head_dim)
    values_all = project[:, 2 * D:].reshape(item_count, POS, HEADS, head_dim)
    scores = low_back(jnp.einsum('sqhd,skhd->shqk', queries, keys_all, precision=HIGH) * head_dim ** (-0.5))
    key_valid = jnp.arange(POS) < POS - PADDED
    scores = jnp.where(key_valid, scores, NEG_FILL)
    probs = jax.nn.softmax(scores, axis=-1)
    mixed = jnp.einsum('shqk,skhd->sqhd', low(probs), values_all, precision=HIGH).reshape(row_count, D)
    mixed = low(low_back(mixed))
    after_attn = merged + low_back(matmul(mixed, w_proj)) + biases[2]
    normed_two = low(layer_norm(after_attn, gains[1], biases[3]))
    inner = low_back(matmul(normed_two, w_fc1)) + fc1_bias
    activ = low(jax.nn.gelu(inner, approximate=False))
    result = after_attn + low_back(matmul(activ, w_fc2)) + biases[4]
    return result.reshape(item_count, POS, D) * row_mask[:, :, None]

def reference(hidden_in, skip_in, cotangent, timesteps, counts, w_skip, w_qkv, w_proj, w_fc1, w_fc2, gains, biases, fc1_bias):
    params = tuple((array.astype(jnp.float32) for array in (w_skip, w_qkv, w_proj, w_fc1, w_fc2, gains, biases, fc1_bias)))
    loss_weight = jax.nn.sigmoid(12.0 * timesteps.astype(jnp.float32) / TSTEPS - 6.0)

    def group_step(carry, group):
        hidden, skipped, cotan, weight_row, count = group
        slot_valid = jnp.arange(SLOTS) < count
        pos_valid = jnp.arange(POS) < POS - PADDED
        row_mask = jnp.logical_and(slot_valid[:, None], pos_valid[None, :]).astype(jnp.float32)

        def local_forward(params_in, hidden_val, skip_val):
            return forward(params_in, hidden_val, skip_val, row_mask)
        result, pullback = jax.vjp(local_forward, params, hidden.astype(jnp.float32), skipped.astype(jnp.float32))
        param_grads, hidden_grad, skip_grad = pullback(cotan.astype(jnp.float32) * weight_row[:, None, None])
        carry = jax.tree.map(jnp.add, carry, param_grads)
        return (carry, (result.astype(jnp.bfloat16), hidden_grad.astype(jnp.bfloat16), skip_grad.astype(jnp.bfloat16)))
    groups = (hidden_in.reshape(N_DP, SLOTS, POS, D), skip_in.reshape(N_DP, SLOTS, POS, D), cotangent.reshape(N_DP, SLOTS, POS, D), loss_weight.reshape(N_DP, SLOTS), counts)
    init = tuple((jnp.zeros_like(array) for array in params))
    totals, (outputs, hidden_grads, skip_grads) = lax.scan(group_step, init, groups)
    return (outputs.reshape(ITEMS, POS, D), hidden_grads.reshape(ITEMS, POS, D), skip_grads.reshape(ITEMS, POS, D), totals[0], totals[1], totals[2], totals[3], totals[4], totals[5], totals[6], totals[7])
```

```python
import jax
import jax.numpy as jnp
from jax import lax
from jax.sharding import PartitionSpec as P

HEADS = 16
PADDED = 2
TSTEPS = 1000

EPSILON = 1e-06
NEG_FILL = -1e30
BF = jnp.bfloat16
F32 = jnp.float32


def dot(left, right, dims):
    return lax.dot_general(left, right, ((dims[:1], dims[1:]), ((), ())), preferred_element_type=F32)


def norm(value):
    center = value - jnp.mean(value, axis=-1, keepdims=True)
    rstd = lax.rsqrt(jnp.mean(center * center, axis=-1, keepdims=True) + EPSILON)
    return center * rstd, rstd


def norm_back(grad, xhat, rstd, gain):
    scaled = grad * gain
    return rstd * (
        scaled
        - jnp.mean(scaled, axis=-1, keepdims=True)
        - xhat * jnp.mean(scaled * xhat, axis=-1, keepdims=True)
    )


def pick(array, index, axis):
    return lax.dynamic_index_in_dim(array, index, axis, keepdims=False)


def shards(
    hidden_in,
    skip_in,
    cotangent,
    timesteps,
    counts,
    w_skip,
    w_qkv,
    w_proj,
    w_fc1,
    w_fc2,
    gains,
    biases,
    fc1_bias,
):
    rows, width = hidden_in.shape[1:]
    half = width // 2
    ff = w_fc1.shape[1]
    head_dim = width // HEADS
    scale = head_dim ** (-0.5)
    n_dp = lax.axis_size("dp")
    bits = n_dp.bit_length() - 1
    pairs = n_dp // 2
    place = lax.axis_index("dp")
    core = place % 2
    seq = lax.axis_index("seq")

    def flat(dp, s):
        return 2 * dp + s

    mirror_perm = [
        (flat(2 * k + c, s), flat(2 * k + s, c)) for k in range(pairs) for c in range(2) for s in range(2)
    ]
    turn = {(0, 0): (1, 0), (1, 0): (1, 1), (1, 1): (0, 1), (0, 1): (0, 0)}
    turn_perm = [
        (flat(2 * k + c, s), flat(2 * k + d[0], d[1])) for k in range(pairs) for (c, s), d in turn.items()
    ]
    turn_back_perm = [(b, a) for a, b in turn_perm]

    def mirror(x):
        return lax.ppermute(x, ("dp", "seq"), mirror_perm)

    def across_seq(x):
        return lax.ppermute(x, "seq", [(0, 1), (1, 0)])

    def across_bit(x, bit):
        return lax.ppermute(x, "dp", [(i, i ^ (1 << bit)) for i in range(n_dp)])

    def across_core(x):
        return across_bit(x, 0)

    def swap_if(flag, a, b, axis):
        return jnp.where(flag, jnp.concatenate([b, a], axis), jnp.concatenate([a, b], axis))

    hidden = mirror(hidden_in[0])
    skip_rows = skip_in[0].reshape(2, rows, half)
    skip_a = mirror(pick(skip_rows, seq, 0))
    skip_b = lax.ppermute(pick(skip_rows, 1 - seq, 0), ("dp", "seq"), turn_perm)
    joined = jnp.concatenate([hidden, swap_if(core == 1, skip_a, skip_b, 1)], axis=1)

    live = (counts[0] > 0).astype(F32)
    home_pos = seq * rows + jnp.arange(rows)[:, None]
    home_mask = jnp.where(home_pos < 2 * rows - PADDED, live, 0.0)
    loss_weight = jax.nn.sigmoid(12.0 * timesteps[0].astype(F32) / TSTEPS - 6.0)
    grad_out_home = cotangent[0].astype(F32) * loss_weight * home_mask
    sum_grad_out = jnp.sum(grad_out_home, axis=0)
    g_home = grad_out_home.astype(BF)
    g_far = across_seq(g_home)
    g_other = across_core(jnp.concatenate([g_home, g_far], 0))
    same = core == seq
    g0, g1, g2, g3 = g_home, g_far, g_other[:rows], g_other[rows:]
    g_all = jnp.where(
        same, jnp.concatenate([g0, g2, g1, g3], 0), jnp.concatenate([g3, g1, g2, g0], 0)
    )
    grad_out = g_all[:rows].astype(F32)

    piece = ff // (4 * pairs)
    quarter = pairs * piece
    w1 = pick(pick(w_fc1.reshape(width, pairs, 2, 2, piece), core, 2), seq, 2).reshape(width, quarter)
    w2 = pick(pick(w_fc2.reshape(pairs, 2, 2, piece, width), core, 1), seq, 1).reshape(quarter, width)
    b1 = pick(pick(fc1_bias.reshape(pairs, 2, 2, piece), core, 1), seq, 1).reshape(quarter)

    merged = dot(joined, w_skip, (1, 0)) + biases[0]
    xhat_one, rstd_one = norm(merged)
    normed_one = (xhat_one * gains[0] + biases[1]).astype(BF)
    project = dot(normed_one, w_qkv, (1, 0)).astype(BF)
    kv_other = across_core(project[:, width:])
    kv = jnp.concatenate([project[:, width:], kv_other], 0)
    queries = project[:, :width].reshape(rows, HEADS, head_dim)
    keys = kv[:, :width].reshape(2 * rows, HEADS, head_dim)
    values = kv[:, width:].reshape(2 * rows, HEADS, head_dim)
    spot = jnp.arange(2 * rows)
    last_half = jnp.where(core == 1, spot < rows, spot >= rows)
    key_valid = jnp.logical_not(jnp.logical_and(last_half, spot % rows >= rows - PADDED))
    scores = jnp.einsum("qhd,khd->hqk", queries, keys, preferred_element_type=F32) * scale
    scores = jnp.where(key_valid, scores, NEG_FILL)
    top = jnp.max(scores, axis=-1, keepdims=True)
    expo = jnp.exp(scores - top)
    probs = expo / jnp.sum(expo, axis=-1, keepdims=True)
    probs_low = probs.astype(BF)
    mixed = jnp.einsum("hqk,khd->qhd", probs_low, values, preferred_element_type=F32)
    mixed = mixed.reshape(rows, width).astype(BF)
    after_attn = merged + dot(mixed, w_proj, (1, 0)) + biases[2]
    xhat_two, rstd_two = norm(after_attn)
    normed_two = (xhat_two * gains[1] + biases[3]).astype(BF)

    n_far = across_seq(normed_two)
    n_other = across_core(normed_two)
    n_other_far = across_core(n_far)
    n_all = jnp.concatenate([normed_two, n_far, n_other, n_other_far], 0)
    inner = dot(n_all, w1, (1, 0)) + b1
    cdf = 0.5 * lax.erfc(-inner * (0.5**0.5))
    activ = (inner * cdf).astype(BF)
    grad_w_fc2 = dot(activ, g_all, (0, 0)).astype(BF)
    grad_activ = dot(g_all, w2, (1, 1))
    grad_inner = grad_activ * (cdf + inner * jnp.exp(-0.5 * inner * inner) * (0.5 / jnp.pi) ** 0.5)
    grad_inner_low = grad_inner.astype(BF)
    grad_w_fc1 = dot(grad_inner_low, n_all, (0, 0)).astype(BF)
    sum_grad_inner = jnp.sum(grad_inner, axis=0)

    def sum_rows(partial):
        low = partial.astype(BF)
        mine = partial[: 2 * rows] + across_core(low[2 * rows :]).astype(F32)
        return mine[:rows] + across_seq(mine[rows:].astype(BF)).astype(F32)

    gn_two = sum_rows(dot(grad_inner_low, w1, (1, 1)))
    mlp_out = sum_rows(dot(activ, w2, (1, 0)))
    result = (after_attn + mlp_out + biases[4]).astype(BF)
    output = mirror(result) * home_mask.astype(BF)

    grad_after = grad_out + norm_back(gn_two, xhat_two, rstd_two, gains[1])
    grad_after_low = grad_after.astype(BF)
    grad_mixed = dot(grad_after_low, w_proj, (1, 1)).astype(BF).reshape(rows, HEADS, head_dim)
    grad_probs = jnp.einsum("qhd,khd->hqk", grad_mixed, values, preferred_element_type=F32)
    grad_scores = probs * (grad_probs - jnp.sum(grad_probs * probs, axis=-1, keepdims=True))
    grad_scores = grad_scores.astype(BF)
    grad_q = jnp.einsum("hqk,khd->qhd", grad_scores, keys, preferred_element_type=F32) * scale
    grad_k = jnp.einsum("hqk,qhd->khd", grad_scores, queries, preferred_element_type=F32) * scale
    grad_v = jnp.einsum("hqk,qhd->khd", probs_low, grad_mixed, preferred_element_type=F32)
    grad_kv = jnp.concatenate([grad_k.reshape(2 * rows, width), grad_v.reshape(2 * rows, width)], 1)
    grad_kv = grad_kv[:rows] + across_core(grad_kv[rows:].astype(BF)).astype(F32)
    grad_project = jnp.concatenate([grad_q.reshape(rows, width), grad_kv], 1).astype(BF)
    gn_one = dot(grad_project, w_qkv, (1, 1))
    grad_merged = grad_after + norm_back(gn_one, xhat_one, rstd_one, gains[0])
    grad_merged_low = grad_merged.astype(BF)
    grad_joined = dot(grad_merged_low, w_skip, (1, 1)).astype(BF)
    grad_hidden = mirror(grad_joined[:, :width])
    grad_skip_halves = grad_joined[:, width:].reshape(rows, 2, half)
    back_a = mirror(pick(grad_skip_halves, core, 1))
    back_b = lax.ppermute(pick(grad_skip_halves, 1 - core, 1), ("dp", "seq"), turn_back_perm)
    grad_skip = swap_if(seq == 1, back_a, back_b, 0)

    def own_half(x):
        return lax.dynamic_slice_in_dim(x, seq * half, half, 1)

    def far_half(x):
        return lax.dynamic_slice_in_dim(x, (1 - seq) * half, half, 1)

    def both(x):
        return jnp.concatenate([x, across_seq(x)], 0)

    def both_half(x):
        return jnp.concatenate([own_half(x), across_seq(far_half(x))], 0)

    grad_w_skip = dot(both(joined), both_half(grad_merged_low), (0, 0)).astype(BF)
    grad_w_qkv = dot(both(grad_project), both_half(normed_one), (0, 0)).astype(BF)
    grad_w_proj = dot(both(mixed), both_half(grad_after_low), (0, 0)).astype(BF)

    def halve(array, bit_list):
        left = list(range(bits - 1, -1, -1))[: array.ndim - 2]
        for bit in bit_list:
            axis = left.index(bit)
            mine = (place >> bit) & 1
            keep = pick(array, mine, axis)
            got = across_bit(pick(array, 1 - mine, axis), bit)
            array = keep.astype(F32) + got.astype(F32)
            left.remove(bit)
            if left:
                array = array.astype(BF)
        return array

    order = list(range(bits))

    def blocks(array, count_bits):
        return array.reshape((2,) * count_bits + (array.shape[0] >> count_bits, array.shape[1]))

    def halve_ff(array):
        left = list(range(bits - 1, 0, -1))
        array = blocks(array, bits - 1)
        for bit in order[1:]:
            axis = left.index(bit)
            mine = (place >> bit) & 1
            keep = pick(array, mine, axis)
            got = across_bit(pick(array, 1 - mine, axis), bit)
            array = keep.astype(F32) + got.astype(F32)
            left.remove(bit)
            if left:
                array = array.astype(BF)
        here = own_half(array)
        there = across_seq(far_half(array).astype(BF)).astype(F32)
        return swap_if(seq == 1, here, there, 0)

    out_w_fc2 = halve_ff(grad_w_fc2)
    out_w_fc1 = halve_ff(grad_w_fc1).T
    out_w_proj = halve(blocks(grad_w_proj, bits), order)
    out_w_qkv = halve(blocks(grad_w_qkv, bits), order).T
    out_w_skip = halve(blocks(grad_w_skip, bits), order)

    fc1_part = jnp.zeros((pairs, 2, 2, piece), F32)
    fc1_part = lax.dynamic_update_slice(
        fc1_part, sum_grad_inner.reshape(pairs, 1, 1, piece), (0, core, seq, 0)
    )
    small = jnp.concatenate(
        [
            jnp.sum(gn_one * xhat_one, axis=0),
            jnp.sum(gn_two * xhat_two, axis=0),
            jnp.sum(grad_merged, axis=0),
            jnp.sum(gn_one, axis=0),
            jnp.sum(grad_after, axis=0),
            jnp.sum(gn_two, axis=0),
            sum_grad_out,
            fc1_part.reshape(ff),
        ]
    ).reshape(-1, 128)
    small = small + across_seq(small)
    for bit in order:
        small = small + across_bit(small, bit)
    small = small.reshape(-1)
    return (
        output[None],
        grad_hidden[None],
        grad_skip[None],
        out_w_skip,
        out_w_qkv,
        out_w_proj,
        out_w_fc1,
        out_w_fc2,
        small[: 2 * width].reshape(2, width),
        small[2 * width : 7 * width].reshape(5, width),
        small[7 * width :],
    )


def solution(mesh):
    return jax.shard_map(
        shards,
        mesh=mesh,
        in_specs=(
            P("dp", "seq", None),
            P("dp", None, "seq"),
            P("dp", "seq", None),
            P("dp"),
            P("dp"),
            P(),
            P(),
            P(),
            P(),
            P(),
            P(),
            P(),
            P(),
        ),
        out_specs=(
            P("dp", "seq", None),
            P("dp", "seq", None),
            P("dp", None, "seq"),
            P("dp", "seq"),
            P("seq", "dp"),
            P("dp", "seq"),
            P("seq", "dp"),
            P("dp", "seq"),
            P(),
            P(),
            P(),
        ),
        check_vma=False,
    )
```

```python
import functools

import jax
import jax.numpy as jnp
from jax import lax
from jax.experimental import pallas as pl
from jax.experimental.pallas import tpu as pltpu
from jax.sharding import PartitionSpec as P

HEADS = 16
PADDED = 2
TSTEPS = 1000

EPSILON = 1e-06
NEG_FILL = -1e30
BF = jnp.bfloat16
F32 = jnp.float32
MIB = 1 << 20
LANES = 128
GAP = 16


def dot(left, right, dims):
    return lax.dot_general(left, right, ((dims[:1], dims[1:]), ((), ())), preferred_element_type=F32)


def norm(value):
    center = value - jnp.mean(value, axis=-1, keepdims=True)
    rstd = lax.rsqrt(jnp.mean(center * center, axis=-1, keepdims=True) + EPSILON)
    return center * rstd, rstd


def norm_back(grad, xhat, rstd, gain):
    scaled = grad * gain
    return rstd * (
        scaled
        - jnp.mean(scaled, axis=-1, keepdims=True)
        - xhat * jnp.mean(scaled * xhat, axis=-1, keepdims=True)
    )


def pick(array, index, axis):
    return lax.dynamic_index_in_dim(array, index, axis, keepdims=False)


def shape(dims, dtype):
    return jax.ShapeDtypeStruct(dims, dtype)


IN_VMEM = pl.BlockSpec(memory_space=pltpu.VMEM)
IN_SMEM = pl.BlockSpec(memory_space=pltpu.SMEM)
IN_ANY = pl.BlockSpec(memory_space=pl.ANY)


def call(kernel, name, operands, outs, scratch, mib, flops):
    moved = sum(a.size * a.dtype.itemsize for a, _ in operands)
    moved += sum(o.size * o.dtype.itemsize for o in outs)
    return pl.pallas_call(
        kernel,
        out_shape=outs,
        in_specs=[spec for _, spec in operands],
        out_specs=[IN_VMEM] * len(outs),
        scratch_shapes=scratch,
        compiler_params=pltpu.CompilerParams(vmem_limit_bytes=mib * MIB),
        cost_estimate=pl.CostEstimate(flops=flops, bytes_accessed=moved, transcendentals=0),
        name=name,
    )(*[a for a, _ in operands])


def fetch(pairs, sems):
    copies = [pltpu.make_async_copy(src, dst, sems.at[i]) for i, (src, dst) in enumerate(pairs)]
    for copy in copies:
        copy.start()
    return copies


def gather_kernel(ids, left, right, out):
    m = pl.program_id(0)
    core, seq, piece = ids[0], ids[1], ids[2]
    start = (4 * m + 2 * core + seq) * piece % LANES
    base = pl.multiple_of(m * piece // LANES * LANES, LANES)
    into = m * piece % LANES
    wide = jnp.concatenate([left[...], right[...]], axis=1).astype(F32)
    wide = pltpu.roll(wide, (into - start + 2 * LANES) % (2 * LANES), 1).astype(BF)
    lane = lax.broadcasted_iota(jnp.int32, (wide.shape[0], LANES), 1)
    first = pl.ds(base, LANES)
    out[:, first] = jnp.where(lane >= into, wide[:, :LANES].astype(F32), out[:, first].astype(F32)).astype(BF)
    out[:, pl.ds(pl.multiple_of(base + LANES, LANES), LANES)] = wide[:, LANES:]


def gather_columns(weight, ids, pairs, piece):
    width = weight.shape[0]

    def spot(extra):
        def index(m, ids):
            return 0, (4 * m + 2 * ids[0] + ids[1]) * piece // LANES + extra

        return index

    return pl.pallas_call(
        gather_kernel,
        out_shape=shape((width, pairs * piece), BF),
        grid_spec=pltpu.PrefetchScalarGridSpec(
            num_scalar_prefetch=1,
            grid=(pairs,),
            in_specs=[pl.BlockSpec((width, LANES), spot(0)), pl.BlockSpec((width, LANES), spot(1))],
            out_specs=pl.BlockSpec((width, pairs * piece), lambda m, ids: (0, 0)),
        ),
        compiler_params=pltpu.CompilerParams(vmem_limit_bytes=16 * MIB),
        name="gather_columns",
    )(ids, weight, weight)


def first_kernel(ids, hidden, skip_a, skip_b, w_skip, w_qkv, gains, biases, merged, normed, q, kv, ws, wq, sems):
    width = hidden.shape[1]
    half = width // 2
    parts = [(0, width), (width, half), (width + half, half)]
    copies = fetch(
        [(w_skip.at[pl.ds(a, n)], ws.at[pl.ds(a, n)]) for a, n in parts]
        + [(w_qkv.at[:, pl.ds(i * width, width)], wq.at[i]) for i in range(3)],
        sems,
    )
    core = ids[0]
    a, b = skip_a[...].astype(F32), skip_b[...].astype(F32)
    low = jnp.where(core == 0, a, b).astype(BF)
    high = jnp.where(core == 0, b, a).astype(BF)
    copies[0].wait()
    total = dot(hidden[...], ws[:width], (1, 0)) + biases[0:1]
    copies[1].wait()
    total += dot(low, ws[width : width + half], (1, 0))
    copies[2].wait()
    total += dot(high, ws[width + half :], (1, 0))
    merged[...] = total
    xhat, _ = norm(total)
    one = (xhat * gains[0:1] + biases[1:2]).astype(BF)
    normed[...] = one
    copies[3].wait()
    q[...] = dot(one, wq[0], (1, 0)).astype(BF)
    copies[4].wait()
    kv[:, :width] = dot(one, wq[1], (1, 0)).astype(BF)
    copies[5].wait()
    kv[:, width:] = dot(one, wq[2], (1, 0)).astype(BF)


def head_windows(width):
    size = width // HEADS
    spans = []
    for h in range(HEADS):
        low, high = h * size, (h + 1) * size
        t0, t1 = low // LANES, (high - 1) // LANES + 1
        spans.append((h, low, high, t0 * LANES, t1 * LANES))
    return spans


def lane_mask(low, high, first, last):
    lane = lax.broadcasted_iota(jnp.int32, (1, last - first), 1) + first
    return jnp.logical_and(lane >= low, lane < high)


def key_mask(core, rows, pitch):
    spot = lax.broadcasted_iota(jnp.int32, (1, 2 * pitch), 1)
    other = spot >= pitch
    here = jnp.where(other, spot - pitch, spot)
    last_half = jnp.where(other, 1 - core, core) == 1
    limit = jnp.where(last_half, rows - PADDED, rows)
    return here < limit


def lay_keys(keys, values, kv_own, kv_other, rows, pitch, width):
    for buf, at in ((keys, 0), (values, width)):
        buf[...] = jnp.zeros_like(buf)
        buf[0:rows] = kv_own[:, at : at + width]
        buf[pitch : pitch + rows] = kv_other[:, at : at + width]


def attend_kernel(ids, q, kv_own, kv_other, merged, w_proj, gains, biases, mixed, after, normed, log_total, keys, values, wp, sems):
    rows, width = q.shape
    pitch = keys.shape[0] // 2
    copies = fetch([(w_proj, wp)], sems)
    lay_keys(keys, values, kv_own, kv_other, rows, pitch, width)
    valid = key_mask(ids[0], rows, pitch)
    scale = (width // HEADS) ** (-0.5)
    lane = lax.broadcasted_iota(jnp.int32, (rows, LANES), 1)
    tiles = [jnp.zeros((rows, LANES), F32) for _ in range(width // LANES)]
    logs = jnp.zeros((rows, LANES), F32)
    for h, low, high, first, last in head_windows(width):
        mask = lane_mask(low, high, first, last)
        mine = q[:, first:last] * mask.astype(F32).astype(BF)
        scores = jnp.where(valid, dot(mine, keys[:, first:last], (1, 1)) * scale, NEG_FILL)
        top = jnp.max(scores, axis=-1, keepdims=True)
        expo = jnp.exp(scores - top)
        total = jnp.sum(expo, axis=-1, keepdims=True)
        probs = (expo * (1.0 / total)).astype(BF)
        logs = jnp.where(lane == h, top + jnp.log(total), logs)
        part = dot(probs, values[:, first:last], (1, 0))
        for t in range(first, last, LANES):
            tiles[t // LANES] = jnp.where(
                mask[:, t - first : t - first + LANES], part[:, t - first : t - first + LANES], tiles[t // LANES]
            )
    log_total[...] = logs
    for t, tile in enumerate(tiles):
        mixed[:, t * LANES : (t + 1) * LANES] = tile.astype(BF)
    copies[0].wait()
    value = merged[...] + dot(mixed[...], wp[...], (1, 0)) + biases[2:3]
    after[...] = value
    xhat, _ = norm(value)
    normed[...] = (xhat * gains[1:2] + biases[3:4]).astype(BF)


def attend_back_kernel(
    ids, gn_mine, gn_core, gn_far, g_out, after, q, kv_own, kv_other, log_total, w_proj, gains,
    grad_after, grad_low, ga_own, ga_far, grad_q, gkv_own, gkv_other, sums,
    keys, values, wp, gk, gv, sems,
):
    rows, width = q.shape
    half = width // 2
    pitch = keys.shape[0] // 2
    copies = fetch([(w_proj, wp)], sems)
    gn = gn_mine[...] + gn_core[...].astype(F32) + gn_far[...].astype(F32)
    xhat, rstd = norm(after[...])
    value = g_out[...].astype(F32) + norm_back(gn, xhat, rstd, gains[1:2])
    grad_after[...] = value
    low = value.astype(BF)
    grad_low[...] = low
    halves = value[:, :half], value[:, half:]
    ga_own[...] = jnp.where(ids[1] == 0, halves[0], halves[1]).astype(BF)
    ga_far[...] = jnp.where(ids[1] == 0, halves[1], halves[0]).astype(BF)
    sums[...] = jnp.concatenate(
        [
            jnp.sum(gn * xhat, axis=0, keepdims=True),
            jnp.sum(gn, axis=0, keepdims=True),
            jnp.sum(value, axis=0, keepdims=True),
            jnp.zeros((5, width), F32),
        ],
        0,
    )
    lay_keys(keys, values, kv_own, kv_other, rows, pitch, width)
    valid = key_mask(ids[0], rows, pitch)
    scale = (width // HEADS) ** (-0.5)
    copies[0].wait()
    grad_mixed = dot(low, wp[...], (1, 1)).astype(BF)
    gk[...] = jnp.zeros_like(gk)
    gv[...] = jnp.zeros_like(gv)
    lane = lax.broadcasted_iota(jnp.int32, (rows, LANES), 1)
    tiles = [jnp.zeros((rows, LANES), F32) for _ in range(width // LANES)]
    logs = log_total[...]
    for h, start, stop, first, last in head_windows(width):
        mask = lane_mask(start, stop, first, last)
        low_mask = mask.astype(F32).astype(BF)
        mine = q[:, first:last] * low_mask
        gm = grad_mixed[:, first:last] * low_mask
        log = jnp.sum(jnp.where(lane == h, logs, 0.0), axis=-1, keepdims=True)
        scores = jnp.where(valid, dot(mine, keys[:, first:last], (1, 1)) * scale, NEG_FILL)
        probs = jnp.exp(scores - log)
        gp = dot(gm, values[:, first:last], (1, 1))
        gs = (probs * (gp - jnp.sum(gp * probs, axis=-1, keepdims=True))).astype(BF)
        part = dot(gs, keys[:, first:last], (1, 0))
        for t in range(first, last, LANES):
            tiles[t // LANES] = jnp.where(
                mask[:, t - first : t - first + LANES], part[:, t - first : t - first + LANES], tiles[t // LANES]
            )
        gk[:, first:last] += dot(gs, mine, (0, 0))
        gv[:, first:last] += dot(probs.astype(BF), gm, (0, 0))
    for t, tile in enumerate(tiles):
        grad_q[:, t * LANES : (t + 1) * LANES] = (tile * scale).astype(BF)
    gkv_own[:, :width] = gk[0:rows] * scale
    gkv_own[:, width:] = gv[0:rows]
    gkv_other[:, :width] = (gk[pitch : pitch + rows] * scale).astype(BF)
    gkv_other[:, width:] = gv[pitch : pitch + rows].astype(BF)


def lay_rows(buf, blocks):
    rows = blocks[0].shape[0]
    pitch = buf.shape[0] // len(blocks)
    buf[...] = jnp.zeros_like(buf)
    for i, block in enumerate(blocks):
        buf[i * pitch : i * pitch + rows] = block[...]


def mlp_kernel(n0, n1, n2, n3, g0, g1, g2, g3, w1, b1, w2, activ, grad_inner, n_all, g_all, gn_mine, gn_other, sum_inner, w2_out, inner_v, grad_v, sems):
    rows, width = n0.shape
    units = w1.shape[1]
    pieces = w2.shape[0]
    per = units // pieces
    lay_rows(n_all, (n0, n1, n2, n3))
    lay_rows(g_all, (g0, g1, g2, g3))
    height = n_all.shape[0]
    pitch = height // 4
    step = 3 * LANES
    chunk = 48
    root = 0.5**0.5
    bell = (0.5 / jnp.pi) ** 0.5
    w2_out[...] = w2[...].reshape(units, width)
    for j in range(units // step):
        cols = slice(j * step, (j + 1) * step)
        inner_v[...] = dot(n_all[...], w1[:, cols], (1, 0))
        grad_v[...] = dot(g_all[...], w2_out[cols, :], (1, 1))
        bias = b1[0:1, cols]

        def body(i, total):
            at = pl.ds(pl.multiple_of(i * chunk, chunk), chunk)
            x = inner_v[at] + bias
            cdf = 0.5 + 0.5 * lax.erf(x * root)
            activ[at, cols] = (x * cdf).astype(BF)
            g = grad_v[at] * (cdf + x * jnp.exp(-0.5 * x * x) * bell)
            grad_inner[at, cols] = g.astype(BF)
            return total + jnp.sum(g, axis=0, keepdims=True)

        sum_inner[0:1, cols] = lax.fori_loop(0, height // chunk, body, jnp.zeros((1, step), F32))
    low = grad_inner[...]
    for j in range(width // step):
        cols = slice(j * step, (j + 1) * step)
        part = dot(low, w1[cols, :], (1, 1))
        for b in range(2):
            gn_mine[b, :, cols] = part[b * pitch : b * pitch + rows]
            gn_other[b, :, cols] = part[(2 + b) * pitch : (2 + b) * pitch + rows].astype(BF)


def mlp_out_kernel(activ, w2, mine, other):
    rows = mine.shape[1]
    pitch = activ.shape[0] // 4
    step = 3 * LANES
    for j in range(w2.shape[1] // step):
        cols = slice(j * step, (j + 1) * step)
        part = dot(activ[...], w2[:, cols], (1, 0))
        for b in range(2):
            mine[b, :, cols] = part[b * pitch : b * pitch + rows]
            other[b, :, cols] = part[(2 + b) * pitch : (2 + b) * pitch + rows].astype(BF)


def split_blocks(total, keep, send, mine, stride):
    count, rows, _ = keep.shape
    slot = 0
    for i in range(2 * count):
        if i // stride % 2:
            continue
        a = total[i * rows : (i + 1) * rows]
        b = total[(i + stride) * rows : (i + stride + 1) * rows]
        keep[slot] = jnp.where(mine == 0, a, b).astype(BF)
        send[slot] = jnp.where(mine == 0, b, a).astype(BF)
        slot += 1


def outer_kernel(stride, ids, left, right, keep, send, total):
    step = 3 * LANES
    for j in range(left.shape[1] // step):
        cols = slice(j * step, (j + 1) * step)
        total[cols, :] = dot(left[:, cols], right[...], (0, 0))
    if stride:
        split_blocks(total, keep, send, ids[2], stride)
    else:
        keep[...] = total[...].astype(BF)


def outer_pair_kernel(stride, ids, own, far, right_own, right_far, keep, send, total, left, right):
    lay_rows(left, (own, far))
    lay_rows(right, (right_own, right_far))
    outer_kernel(stride, ids, left, right, keep, send, total)


def outer(left, right, blocks, bit, mine, name):
    pair = isinstance(left, tuple)
    n = (left[0] if pair else left).shape[1]
    cols = (right[0] if pair else right).shape[1]
    rows = n // blocks
    inside = rows % 8 == 0
    stride = (1 << bit) if inside else 0
    if inside:
        outs = [shape((blocks // 2, rows, cols), BF)] * 2
    else:
        outs = [shape((n, cols), BF), shape((8, LANES), BF)]
    ids = jnp.stack([mine * 0, mine * 0, mine]).astype(jnp.int32)
    scratch = [pltpu.VMEM((n, cols), F32)]
    height = left[0].shape[0] if pair else left.shape[0]
    if pair:
        pitch = -(-height // GAP) * GAP
        height = 2 * pitch
        scratch += [pltpu.VMEM((height, n), BF), pltpu.VMEM((height, cols), BF)]
        operands = [(a, IN_VMEM) for a in (*left, *right)]
        kernel = outer_pair_kernel
    else:
        operands = [(left, IN_VMEM), (right, IN_VMEM)]
        kernel = outer_kernel
    keep, send = call(
        functools.partial(kernel, stride), name, [(ids, IN_SMEM)] + operands, outs, scratch, 32, 2 * height * n * cols
    )
    if inside:
        return keep, send
    parted = keep.reshape(blocks >> (bit + 1), 2, 1 << bit, rows, cols)
    return [pick(parted, i, 1).reshape(blocks // 2, rows, cols) for i in (mine, 1 - mine)]


def last_kernel(
    ids, gq, gkv, merged, grad_after, w_skip, w_qkv, gains,
    gm_own, gm_far, grad_hidden, back_a, back_b, sums, ws, wq, sems,
):
    width = gq.shape[1]
    half = width // 2
    copies = fetch(
        [(w_qkv.at[:, pl.ds(i * width, width)], wq.at[i]) for i in range(3)] + [(w_skip, ws)], sems
    )
    xhat, rstd = norm(merged[...])
    copies[0].wait()
    gn = dot(gq[...], wq[0], (1, 1))
    copies[1].wait()
    gn += dot(gkv[:, :width], wq[1], (1, 1))
    copies[2].wait()
    gn += dot(gkv[:, width:], wq[2], (1, 1))
    value = grad_after[...] + norm_back(gn, xhat, rstd, gains[0:1])
    sums[...] = jnp.concatenate(
        [
            jnp.sum(gn * xhat, axis=0, keepdims=True),
            jnp.sum(gn, axis=0, keepdims=True),
            jnp.sum(value, axis=0, keepdims=True),
            jnp.zeros((5, width), F32),
        ],
        0,
    )
    halves = value[:, :half], value[:, half:]
    gm_own[...] = jnp.where(ids[1] == 0, halves[0], halves[1]).astype(BF)
    gm_far[...] = jnp.where(ids[1] == 0, halves[1], halves[0]).astype(BF)
    low = value.astype(BF)
    copies[3].wait()
    grad_hidden[...] = dot(low, ws[:width], (1, 1)).astype(BF)
    a = dot(low, ws[width : width + half], (1, 1))
    b = dot(low, ws[width + half :], (1, 1))
    back_a[...] = jnp.where(ids[0] == 0, a, b).astype(BF)
    back_b[...] = jnp.where(ids[0] == 0, b, a).astype(BF)


def shards(
    hidden_in,
    skip_in,
    cotangent,
    timesteps,
    counts,
    w_skip,
    w_qkv,
    w_proj,
    w_fc1,
    w_fc2,
    gains,
    biases,
    fc1_bias,
):
    rows, width = hidden_in.shape[1:]
    half = width // 2
    ff = w_fc1.shape[1]
    n_dp = lax.axis_size("dp")
    bits = n_dp.bit_length() - 1
    pairs = n_dp // 2
    place = lax.axis_index("dp")
    core = place % 2
    seq = lax.axis_index("seq")
    piece = ff // (4 * pairs)
    quarter = pairs * piece
    ids = jnp.stack([core, seq, core * 0 + piece]).astype(jnp.int32)
    pitch = -(-rows // GAP) * GAP

    def flat(dp, s):
        return 2 * dp + s

    mirror_perm = [
        (flat(2 * k + c, s), flat(2 * k + s, c)) for k in range(pairs) for c in range(2) for s in range(2)
    ]
    turn = {(0, 0): (1, 0), (1, 0): (1, 1), (1, 1): (0, 1), (0, 1): (0, 0)}
    turn_perm = [
        (flat(2 * k + c, s), flat(2 * k + d[0], d[1])) for k in range(pairs) for (c, s), d in turn.items()
    ]
    turn_back_perm = [(b, a) for a, b in turn_perm]

    def mirror(x):
        return lax.ppermute(x, ("dp", "seq"), mirror_perm)

    def across_seq(x):
        return lax.ppermute(x, "seq", [(0, 1), (1, 0)])

    def across_bit(x, bit):
        return lax.ppermute(x, "dp", [(i, i ^ (1 << bit)) for i in range(n_dp)])

    def across_core(x):
        return across_bit(x, 0)

    def swap_if(flag, a, b, axis):
        return jnp.where(flag, jnp.concatenate([b, a], axis), jnp.concatenate([a, b], axis))

    hidden = mirror(hidden_in[0])
    skip_rows = skip_in[0].reshape(2, rows, half)
    skip_a = mirror(pick(skip_rows, seq, 0))
    skip_b = lax.ppermute(pick(skip_rows, 1 - seq, 0), ("dp", "seq"), turn_perm)

    live = (counts[0] > 0).astype(F32)
    home_pos = seq * rows + jnp.arange(rows)[:, None]
    home_mask = jnp.where(home_pos < 2 * rows - PADDED, live, 0.0)
    loss_weight = jax.nn.sigmoid(12.0 * timesteps[0].astype(F32) / TSTEPS - 6.0)
    grad_out_home = cotangent[0].astype(F32) * loss_weight * home_mask
    sum_grad_out = jnp.sum(grad_out_home, axis=0)
    g_home = grad_out_home.astype(BF)
    g_far = across_seq(g_home)
    g_other, g_other_far = across_core(g_home), across_core(g_far)
    same = core == seq
    g_blocks = [
        jnp.where(same, a, b)
        for a, b in ((g_home, g_other_far), (g_other, g_far), (g_far, g_other), (g_other_far, g_home))
    ]

    if piece % GAP == 0 and piece <= 2 * LANES - 7 * GAP:
        w1 = gather_columns(w_fc1, ids, pairs, piece)
    else:
        w1 = pick(pick(w_fc1.reshape(width, pairs, 2, 2, piece), core, 2), seq, 2).reshape(width, quarter)
    w2 = pick(pick(w_fc2.reshape(pairs, 2, 2, piece, width), core, 1), seq, 1)
    w2 = w2.reshape(1, quarter, width)
    b1 = pick(pick(fc1_bias.reshape(pairs, 2, 2, piece), core, 1), seq, 1).reshape(1, quarter)

    token = shape((rows, width), BF)
    merged, normed_one, q, kv = call(
        first_kernel,
        "first",
        [(ids, IN_SMEM), (hidden, IN_VMEM), (skip_a, IN_VMEM), (skip_b, IN_VMEM), (w_skip, IN_ANY), (w_qkv, IN_ANY)]
        + [(gains, IN_VMEM), (biases, IN_VMEM)],
        [shape((rows, width), F32), token, token, shape((rows, 2 * width), BF)],
        [
            pltpu.VMEM(w_skip.shape, BF),
            pltpu.VMEM((3, width, width), BF),
            pltpu.SemaphoreType.DMA((6,)),
        ],
        28,
        2 * rows * width * 5 * width,
    )
    kv_other = across_core(kv)
    key_buf = pltpu.VMEM((2 * pitch, width), BF)
    proj_buf = [pltpu.VMEM((width, width), BF), pltpu.SemaphoreType.DMA((1,))]
    mixed, after_attn, normed_two, log_total = call(
        attend_kernel,
        "attend",
        [(ids, IN_SMEM), (q, IN_VMEM), (kv, IN_VMEM), (kv_other, IN_VMEM), (merged, IN_VMEM), (w_proj, IN_ANY)]
        + [(gains, IN_VMEM), (biases, IN_VMEM)],
        [token, shape((rows, width), F32), token, shape((rows, LANES), F32)],
        [key_buf, key_buf, *proj_buf],
        20,
        2 * rows * width * 2 * width,
    )

    n_far = across_seq(normed_two)
    n_other = across_core(normed_two)
    n_other_far = across_core(n_far)
    tall = shape((4 * pitch, quarter), BF)
    activ, grad_inner, n_all, g_all, gn_mine, gn_other, sum_inner, w2 = call(
        mlp_kernel,
        "mlp",
        [(a, IN_VMEM) for a in (normed_two, n_far, n_other, n_other_far, *g_blocks, w1, b1, w2)],
        [tall, tall, shape((4 * pitch, width), BF), shape((4 * pitch, width), BF)]
        + [shape((2, rows, width), F32), shape((2, rows, width), BF), shape((8, quarter), F32), shape((quarter, width), BF)],
        [
            pltpu.VMEM((4 * pitch, 3 * LANES), F32),
            pltpu.VMEM((4 * pitch, 3 * LANES), F32),
            pltpu.SemaphoreType.DMA((1,)),
        ],
        40,
        6 * 4 * rows * width * quarter,
    )

    def my_bit(bit):
        return (place >> bit) & 1

    ff_bits = bits - 1
    order_two = [1, 2, 3] + list(range(4, bits))
    order_one = [2, 1, 3] + list(range(4, bits))
    order_two = order_two[:ff_bits]
    order_one = order_one[:ff_bits]

    gn_core = across_core(gn_other)
    fc2_keep, fc2_send = outer(activ, g_all, pairs, order_two[0] - 1, my_bit(order_two[0]), "outer_fc2")
    gn_far = across_seq((gn_mine[1] + gn_core[1].astype(F32)).astype(BF))
    fc1_keep, fc1_send = outer(grad_inner, n_all, pairs, order_one[0] - 1, my_bit(order_one[0]), "outer_fc1")

    out_mine, out_other = call(
        mlp_out_kernel,
        "mlp_out",
        [(activ, IN_VMEM), (w2, IN_VMEM)],
        [shape((2, rows, width), F32), shape((2, rows, width), BF)],
        [],
        24,
        2 * 4 * rows * width * quarter,
    )
    out_core = across_core(out_other)
    out_far = across_seq((out_mine[1] + out_core[1].astype(F32)).astype(BF))
    result = after_attn + biases[4] + out_mine[0] + out_core[0].astype(F32) + out_far.astype(F32)
    output = mirror(result.astype(BF)) * home_mask.astype(BF)

    half_token = shape((rows, half), BF)
    grad_after, grad_after_low, ga_own, ga_far, grad_q, gkv_own, gkv_other, sums_two = call(
        attend_back_kernel,
        "attend_back",
        [(ids, IN_SMEM)]
        + [
            (a, IN_VMEM)
            for a in (gn_mine[0], gn_core[0], gn_far, g_blocks[0], after_attn, q, kv, kv_other, log_total)
        ]
        + [(w_proj, IN_ANY), (gains, IN_VMEM)],
        [shape((rows, width), F32), token, half_token, half_token, token]
        + [shape((rows, 2 * width), F32), shape((rows, 2 * width), BF), shape((8, width), F32)],
        [key_buf, key_buf, proj_buf[0], pltpu.VMEM((2 * pitch, width), F32), pltpu.VMEM((2 * pitch, width), F32), proj_buf[1]],
        32,
        2 * rows * width * 3 * width,
    )
    gkv = (gkv_own + across_core(gkv_other).astype(F32)).astype(BF)
    gm_own, gm_far, grad_hidden, back_a, back_b, sums_one = call(
        last_kernel,
        "last",
        [(ids, IN_SMEM)]
        + [(a, IN_VMEM) for a in (grad_q, gkv, merged, grad_after)]
        + [(w_skip, IN_ANY), (w_qkv, IN_ANY), (gains, IN_VMEM)],
        [half_token, half_token, token, half_token, half_token, shape((8, width), F32)],
        [
            pltpu.VMEM(w_skip.shape, BF),
            pltpu.VMEM((3, width, width), BF),
            pltpu.SemaphoreType.DMA((4,)),
        ],
        32,
        2 * rows * width * 5 * width,
    )
    grad_hidden = mirror(grad_hidden)
    back_a = mirror(back_a)
    back_b = lax.ppermute(back_b, ("dp", "seq"), turn_back_perm)
    grad_skip = swap_if(seq == 1, back_a, back_b, 0)

    joined = jnp.concatenate([hidden, swap_if(core == 1, skip_a, skip_b, 1)], axis=1)

    def own_half(x):
        return lax.dynamic_slice_in_dim(x, seq * half, half, 1)

    def far_half(x):
        return lax.dynamic_slice_in_dim(x, (1 - seq) * half, half, 1)

    def finish(keep, send, order, far_first):
        left = [b for b in range(bits - 1, -1, -1) if b in order]
        left.remove(order[0])
        block = keep.shape[1:]
        keep = keep.reshape((2,) * len(left) + block)
        send = send.reshape(keep.shape)
        for at, bit in enumerate(order):
            got = across_bit(send, bit)
            if at + 1 == len(order):
                return keep.astype(F32) + got.astype(F32)
            axis = left.index(order[at + 1])
            mine = my_bit(order[at + 1])

            def part(index):
                return (pick(keep, index, axis).astype(F32) + pick(got, index, axis).astype(F32)).astype(BF)

            send, keep = part(1 - mine), part(mine)
            left.remove(order[at + 1])

    def finish_ff(keep, send, order):
        array = finish(keep, send, order, False)
        there = across_seq(far_half(array).astype(BF)).astype(F32)
        return swap_if(seq == 1, own_half(array), there, 0)

    out_w_fc2 = finish_ff(fc2_keep, fc2_send, order_two)
    out_w_fc1 = finish_ff(fc1_keep, fc1_send, order_one).T

    order_rest = list(range(bits))
    n1_own, n1_far = own_half(normed_one), across_seq(far_half(normed_one))
    grad_project = jnp.concatenate([grad_q, gkv], 1)

    def summed(left, right, name):
        keep, send = outer((left, across_seq(left)), right, n_dp, 0, core, name)
        return finish(keep, send, order_rest, False)

    out_w_proj = summed(mixed, (ga_own, across_seq(ga_far)), "outer_proj")
    out_w_qkv = summed(grad_project, (n1_own, n1_far), "outer_qkv").T
    out_w_skip = summed(joined, (gm_own, across_seq(gm_far)), "outer_skip")

    fc1_part = jnp.zeros((pairs, 2, 2, piece), F32)
    fc1_part = lax.dynamic_update_slice(
        fc1_part, sum_inner[0].reshape(pairs, 1, 1, piece), (0, core, seq, 0)
    )
    small = jnp.concatenate(
        [
            sums_one[0],
            sums_two[0],
            sums_one[2],
            sums_one[1],
            sums_two[2],
            sums_two[1],
            sum_grad_out,
            fc1_part.reshape(ff),
        ]
    ).reshape(-1, 128)
    small = small + across_seq(small)
    for bit in range(bits):
        small = small + across_bit(small, bit)
    small = small.reshape(-1)
    return (
        output[None],
        grad_hidden[None],
        grad_skip[None],
        out_w_skip,
        out_w_qkv,
        out_w_proj,
        out_w_fc1,
        out_w_fc2,
        small[: 2 * width].reshape(2, width),
        small[2 * width : 7 * width].reshape(5, width),
        small[7 * width :],
    )


def solution(mesh):
    return jax.shard_map(
        shards,
        mesh=mesh,
        in_specs=(
            P("dp", "seq", None),
            P("dp", None, "seq"),
            P("dp", "seq", None),
            P("dp"),
            P("dp"),
            P(),
            P(),
            P(),
            P(),
            P(),
            P(),
            P(),
            P(),
        ),
        out_specs=(
            P("dp", "seq", None),
            P("dp", "seq", None),
            P("dp", None, "seq"),
            P("dp", "seq"),
            P("seq", "dp"),
            P("dp", "seq"),
            P("seq", "dp"),
            P("dp", "seq"),
            P(),
            P(),
            P(),
        ),
        check_vma=False,
    )
```

```python
import functools

import jax
import jax.numpy as jnp
from jax import lax
from jax.experimental import pallas as pl
from jax.experimental.pallas import tpu as pltpu
from jax.sharding import PartitionSpec as P

HEADS = 16
PADDED = 2
TSTEPS = 1000

EPSILON = 1e-06
NEG_FILL = -1e30
BF = jnp.bfloat16
F32 = jnp.float32
MIB = 1 << 20
LANES = 128
GAP = 16


def dot(left, right, dims):
    return lax.dot_general(left, right, ((dims[:1], dims[1:]), ((), ())), preferred_element_type=F32)


def norm(value):
    center = value - jnp.mean(value, axis=-1, keepdims=True)
    rstd = lax.rsqrt(jnp.mean(center * center, axis=-1, keepdims=True) + EPSILON)
    return center * rstd, rstd


def norm_back(grad, xhat, rstd, gain):
    scaled = grad * gain
    return rstd * (
        scaled
        - jnp.mean(scaled, axis=-1, keepdims=True)
        - xhat * jnp.mean(scaled * xhat, axis=-1, keepdims=True)
    )


def pick(array, index, axis):
    return lax.dynamic_index_in_dim(array, index, axis, keepdims=False)


def shape(dims, dtype):
    return jax.ShapeDtypeStruct(dims, dtype)


def padded(dims, dtype):
    dims = (1,) * (2 - len(dims)) + tuple(dims)
    size = -(-dims[-2] // 16) * 16 * -(-dims[-1] // LANES) * LANES
    for dim in dims[:-2]:
        size *= dim
    return size * jnp.dtype(dtype).itemsize


IN_VMEM = pl.BlockSpec(memory_space=pltpu.VMEM)
IN_SMEM = pl.BlockSpec(memory_space=pltpu.SMEM)
IN_ANY = pl.BlockSpec(memory_space=pl.ANY)
IN_HBM = pl.BlockSpec(memory_space=pltpu.HBM)


def call(kernel, name, operands, outs, scratch, mib, flops, after=()):
    moved = sum(a.size * a.dtype.itemsize for a, _ in operands)
    moved += sum(o.size * o.dtype.itemsize for o in outs)
    outs = [*outs, shape((8, LANES), F32)]
    inputs = len(operands)
    marks = len(after)
    if not mib:
        need = sum(padded(a.shape, a.dtype) for a, spec in operands if spec is IN_VMEM)
        need += sum(padded(o.shape, o.dtype) for o in outs)
        need += sum(padded(b.shape, b.dtype) for b in scratch if b.memory_space == pltpu.VMEM)
        mib = need * 9 // 8 // MIB + 4

    def body(*refs):
        mark = refs[inputs + marks + len(outs) - 1]
        mark[...] = jnp.zeros_like(mark)
        kernel(*refs[:inputs], *refs[inputs + marks : inputs + marks + len(outs) - 1], *refs[inputs + marks + len(outs) :])

    return pl.pallas_call(
        body,
        out_shape=outs,
        in_specs=[spec for _, spec in operands] + [IN_ANY] * marks,
        out_specs=[IN_VMEM] * len(outs),
        scratch_shapes=scratch,
        compiler_params=pltpu.CompilerParams(vmem_limit_bytes=mib * MIB),
        cost_estimate=pl.CostEstimate(flops=1, bytes_accessed=1, transcendentals=0),
        name=name,
    )(*[a for a, _ in operands], *after)


def fetch(pairs, sems):
    copies = [pltpu.make_async_copy(src, dst, sems.at[i]) for i, (src, dst) in enumerate(pairs)]
    for copy in copies:
        copy.start()
    return copies


def gather_kernel(ids, w_fc1, w_fc2, bias, w1, w2, b1, windows, sems):
    pieces = windows.shape[0]
    core, seq = ids[1], ids[0]
    piece_size = w1.shape[1] // pieces
    which = [4 * m + 2 * core + seq for m in range(pieces)]
    spots = [w * piece_size for w in which]
    copies = fetch(
        [
            (w_fc1.at[:, pl.ds(pl.multiple_of(s // LANES * LANES, LANES), 2 * LANES)], windows.at[m])
            for m, s in enumerate(spots)
        ]
        + [(w_fc2.at[w], w2.at[m]) for m, w in enumerate(which)],
        sems,
    )
    lane = lax.broadcasted_iota(jnp.int32, (8, LANES), 1)
    for m in range(pieces):
        base, into = m * piece_size // LANES * LANES, m * piece_size % LANES
        window = bias[:, pl.ds(pl.multiple_of(spots[m] // LANES * LANES, LANES), 2 * LANES)]
        turn = (into - spots[m] % LANES + 2 * LANES) % (2 * LANES)
        window = pltpu.roll(jnp.broadcast_to(window, (8, 2 * LANES)), turn, 1)
        left = window[:, :LANES]
        if into:
            left = jnp.where(lane >= into, left, b1[:, base : base + LANES])
        b1[:, base : base + LANES] = left
        b1[:, base + LANES : base + 2 * LANES] = window[:, LANES:]
    source = lax.broadcasted_iota(jnp.int32, (2 * LANES, LANES), 0)
    target = lax.broadcasted_iota(jnp.int32, (2 * LANES, LANES), 1)
    arrived = 0
    for tile in range(w1.shape[1] // LANES):
        total = None
        for m in range(pieces):
            low = max(m * piece_size, tile * LANES)
            if low >= min((m + 1) * piece_size, (tile + 1) * LANES):
                continue
            while arrived <= m:
                copies[arrived].wait()
                arrived += 1
            column = target + (tile * LANES - m * piece_size)
            take = jnp.logical_and(column >= 0, column < piece_size)
            take = jnp.logical_and(take, source == column + spots[m] % LANES)
            part = dot(windows[m], take.astype(F32).astype(BF), (1, 0))
            total = part if total is None else total + part
        w1[:, tile * LANES : (tile + 1) * LANES] = total.astype(BF)
    for copy in copies[pieces:]:
        copy.wait()


def pack_kernel(ids, timesteps, counts, skip, cotangent, skip_a, skip_b, g_home, sums):
    rows, width = cotangent.shape
    seq = ids[0]
    whole = skip[...].astype(F32)
    top, bottom = whole[:rows], whole[rows:]
    skip_a[...] = jnp.where(seq == 0, top, bottom).astype(BF)
    skip_b[...] = jnp.where(seq == 0, bottom, top).astype(BF)
    time = jnp.zeros((1, 1), F32) + timesteps[0].astype(F32)
    weight = jax.nn.sigmoid(12.0 * time / TSTEPS - 6.0)
    spot = lax.broadcasted_iota(jnp.int32, (rows, 1), 0) + seq * rows
    live = jnp.logical_and(spot < 2 * rows - PADDED, counts[0] > 0)
    g = cotangent[...].astype(F32) * jnp.where(live, weight, 0.0)
    g_home[...] = g.astype(BF)
    sums[...] = jnp.concatenate([jnp.sum(g, axis=0, keepdims=True), jnp.zeros((7, width), F32)], 0)


def first_kernel(ids, hidden, skip_a, skip_b, w_skip, w_qkv, gains, biases, merged, early, normed_own, q, kv):
    width = hidden.shape[1]
    half = width // 2
    core, seq = ids[1], ids[0]
    a, b = skip_a[...].astype(F32), skip_b[...].astype(F32)
    low = jnp.where(core == 0, a, b).astype(BF)
    high = jnp.where(core == 0, b, a).astype(BF)
    early[:, :width] = hidden[...]
    early[:, width : width + half] = low
    early[:, width + half : 2 * width] = high
    total = dot(hidden[...], w_skip[:width], (1, 0)) + biases[0:1]
    total += dot(low, w_skip[width : width + half], (1, 0))
    total += dot(high, w_skip[width + half :], (1, 0))
    merged[...] = total
    xhat, _ = norm(total)
    one = xhat * gains[0:1] + biases[1:2]
    left, right = one[:, :half], one[:, half:]
    normed_own[...] = jnp.where(seq == 0, left, right).astype(BF)
    early[:, 2 * width :] = jnp.where(seq == 0, right, left).astype(BF)
    one = one.astype(BF)
    q[...] = dot(one, w_qkv[:, :width], (1, 0)).astype(BF)
    kv[...] = dot(one, w_qkv[:, width:], (1, 0)).astype(BF)


def head_windows(width):
    size = width // HEADS
    spans = []
    for h in range(HEADS):
        low, high = h * size, (h + 1) * size
        t0, t1 = low // LANES, (high - 1) // LANES + 1
        spans.append((h, low, high, t0 * LANES, t1 * LANES))
    return spans


def lane_mask(low, high, first, last):
    lane = lax.broadcasted_iota(jnp.int32, (1, last - first), 1) + first
    return jnp.logical_and(lane >= low, lane < high)


def key_mask(core, rows, pitch):
    spot = lax.broadcasted_iota(jnp.int32, (1, 2 * pitch), 1)
    other = spot >= pitch
    here = jnp.where(other, spot - pitch, spot)
    last_half = jnp.where(other, 1 - core, core) == 1
    limit = jnp.where(last_half, rows - PADDED, rows)
    return here < limit


def lay_keys(keys, values, kv_own, kv_other, rows, pitch, width):
    for buf, at in ((keys, 0), (values, width)):
        buf[...] = jnp.zeros_like(buf)
        buf[0:rows] = kv_own[:, at : at + width]
        buf[pitch : pitch + rows] = kv_other[:, at : at + width]


def attend_kernel(ids, q, kv_own, kv_other, merged, w_proj, gains, biases, mixed, after, normed, log_total, keys, values, wp, sems):
    rows, width = q.shape
    pitch = keys.shape[0] // 2
    copies = fetch([(w_proj, wp)], sems)
    lay_keys(keys, values, kv_own, kv_other, rows, pitch, width)
    valid = key_mask(ids[1], rows, pitch)
    scale = (width // HEADS) ** (-0.5)
    lane = lax.broadcasted_iota(jnp.int32, (rows, LANES), 1)
    tiles = [jnp.zeros((rows, LANES), F32) for _ in range(width // LANES)]
    logs = jnp.zeros((rows, LANES), F32)
    for h, low, high, first, last in head_windows(width):
        mask = lane_mask(low, high, first, last)
        mine = q[:, first:last] * mask.astype(F32).astype(BF)
        scores = jnp.where(valid, dot(mine, keys[:, first:last], (1, 1)) * scale, NEG_FILL)
        top = jnp.max(scores, axis=-1, keepdims=True)
        expo = jnp.exp(scores - top)
        total = jnp.sum(expo, axis=-1, keepdims=True)
        probs = (expo * (1.0 / total)).astype(BF)
        logs = jnp.where(lane == h, top + jnp.log(total), logs)
        part = dot(probs, values[:, first:last], (1, 0))
        for t in range(first, last, LANES):
            tiles[t // LANES] = jnp.where(
                mask[:, t - first : t - first + LANES], part[:, t - first : t - first + LANES], tiles[t // LANES]
            )
    log_total[...] = logs
    for t, tile in enumerate(tiles):
        mixed[:, t * LANES : (t + 1) * LANES] = tile.astype(BF)
    copies[0].wait()
    value = merged[...] + dot(mixed[...], wp[...], (1, 0)) + biases[2:3]
    after[...] = value
    xhat, _ = norm(value)
    normed[...] = (xhat * gains[1:2] + biases[3:4]).astype(BF)


def attend_back_kernel(
    ids, gn_mine, gn_core, gn_far, g_home, g_cross, after, q, kv_own, kv_other, log_total, w_proj, gains,
    grad_after, ga_own, ga_far, grad_q, gkv_own, gkv_other, sums,
    keys, values, wp, gk, gv, sems,
):
    rows, width = q.shape
    half = width // 2
    pitch = keys.shape[0] // 2
    copies = fetch([(w_proj, wp)], sems)
    gn = gn_mine[...] + gn_core[...].astype(F32) + gn_far[...].astype(F32)
    xhat, rstd = norm(after[...])
    g_out = jnp.where(ids[0] == ids[1], g_home[...].astype(F32), g_cross[...].astype(F32))
    value = g_out + norm_back(gn, xhat, rstd, gains[1:2])
    grad_after[...] = value
    low = value.astype(BF)
    halves = value[:, :half], value[:, half:]
    ga_own[...] = jnp.where(ids[0] == 0, halves[0], halves[1]).astype(BF)
    ga_far[...] = jnp.where(ids[0] == 0, halves[1], halves[0]).astype(BF)
    sums[...] = jnp.concatenate(
        [
            jnp.sum(gn * xhat, axis=0, keepdims=True),
            jnp.sum(gn, axis=0, keepdims=True),
            jnp.sum(value, axis=0, keepdims=True),
            jnp.zeros((5, width), F32),
        ],
        0,
    )
    lay_keys(keys, values, kv_own, kv_other, rows, pitch, width)
    valid = key_mask(ids[1], rows, pitch)
    scale = (width // HEADS) ** (-0.5)
    copies[0].wait()
    grad_mixed = dot(low, wp[...], (1, 1)).astype(BF)
    gk[...] = jnp.zeros_like(gk)
    gv[...] = jnp.zeros_like(gv)
    lane = lax.broadcasted_iota(jnp.int32, (rows, LANES), 1)
    tiles = [jnp.zeros((rows, LANES), F32) for _ in range(width // LANES)]
    logs = log_total[...]
    for h, start, stop, first, last in head_windows(width):
        mask = lane_mask(start, stop, first, last)
        low_mask = mask.astype(F32).astype(BF)
        mine = q[:, first:last] * low_mask
        gm = grad_mixed[:, first:last] * low_mask
        log = jnp.sum(jnp.where(lane == h, logs, 0.0), axis=-1, keepdims=True)
        scores = jnp.where(valid, dot(mine, keys[:, first:last], (1, 1)) * scale, NEG_FILL)
        probs = jnp.exp(scores - log)
        gp = dot(gm, values[:, first:last], (1, 1))
        gs = (probs * (gp - jnp.sum(gp * probs, axis=-1, keepdims=True))).astype(BF)
        part = dot(gs, keys[:, first:last], (1, 0))
        for t in range(first, last, LANES):
            tiles[t // LANES] = jnp.where(
                mask[:, t - first : t - first + LANES], part[:, t - first : t - first + LANES], tiles[t // LANES]
            )
        gk[:, first:last] += dot(gs, mine, (0, 0))
        gv[:, first:last] += dot(probs.astype(BF), gm, (0, 0))
    for t, tile in enumerate(tiles):
        grad_q[:, t * LANES : (t + 1) * LANES] = (tile * scale).astype(BF)
    gkv_own[:, :width] = gk[0:rows] * scale
    gkv_own[:, width:] = gv[0:rows]
    gkv_other[:, :width] = (gk[pitch : pitch + rows] * scale).astype(BF)
    gkv_other[:, width:] = gv[pitch : pitch + rows].astype(BF)


def lay_rows(buf, blocks):
    rows = blocks[0].shape[0]
    pitch = buf.shape[0] // len(blocks)
    if pitch > rows:
        buf[...] = jnp.zeros_like(buf)
    for i, block in enumerate(blocks):
        buf[i * pitch : i * pitch + rows] = block[...]


def lay_chosen(buf, flag, pairs):
    rows = pairs[0][0].shape[0]
    pitch = buf.shape[0] // len(pairs)
    buf[...] = jnp.zeros_like(buf)
    for way, chosen in enumerate((flag, jnp.logical_not(flag))):

        @pl.when(chosen)
        def _(way=way):
            for i, pair in enumerate(pairs):
                buf[i * pitch : i * pitch + rows] = pair[way][...]


def mlp_kernel(ids, n0, n1, g0a, g0b, g1a, g1b, w1, b1, w2, activ, grad_inner, n_all, g_all, gn_mine, gn_other, sums, inner_v, grad_v):
    rows, width = n0.shape
    units = w1.shape[1]
    lay_rows(n_all, (n0, n1))
    lay_chosen(g_all, ids[0] == ids[1], ((g0a, g0b), (g1a, g1b)))
    height = n_all.shape[0]
    pitch = height // 2
    step = 3 * LANES
    chunk = 48
    root = 0.5**0.5
    bell = (0.5 / jnp.pi) ** 0.5
    for j in range(units // step):
        cols = slice(j * step, (j + 1) * step)
        inner_v[...] = dot(n_all[...], w1[:, cols], (1, 0))
        grad_v[...] = dot(g_all[...], w2[cols, :], (1, 1))
        bias = b1[0:1, cols]

        def body(i, total):
            at = pl.ds(pl.multiple_of(i * chunk, chunk), chunk)
            x = inner_v[at] + bias
            cdf = 0.5 + 0.5 * lax.erf(x * root)
            activ[at, cols] = (x * cdf).astype(BF)
            g = grad_v[at] * (cdf + x * jnp.exp(-0.5 * x * x) * bell)
            grad_inner[at, cols] = g.astype(BF)
            return total + jnp.sum(g, axis=0, keepdims=True)

        sums[0:1, cols] = lax.fori_loop(0, height // chunk, body, jnp.zeros((1, step), F32))
    for j in range(width // step):
        cols = slice(j * step, (j + 1) * step)
        part = dot(grad_inner[...], w1[cols, :], (1, 1))
        gn_mine[:, cols] = part[:rows]
        gn_other[:, cols] = part[pitch : pitch + rows].astype(BF)


def mlp_out_kernel(activ_own, activ_far, w2, own, far, own_core, far_core):
    rows = own.shape[0]
    pitch = activ_own.shape[0] // 2
    step = 3 * LANES
    for activ, mine, other in ((activ_far, far, far_core), (activ_own, own, own_core)):
        for j in range(w2.shape[1] // step):
            cols = slice(j * step, (j + 1) * step)
            part = dot(activ[...], w2[:, cols], (1, 0))
            mine[:, cols] = part[:rows]
            other[:, cols] = part[pitch : pitch + rows].astype(BF)


def split_blocks(total, keep, send, at, mine, stride):
    count = keep.shape[0]
    rows = total.shape[0] // (2 * count)
    slot = 0
    for i in range(2 * count):
        if i // stride % 2:
            continue
        a = total[i * rows : (i + 1) * rows]
        b = total[(i + stride) * rows : (i + stride + 1) * rows]
        keep[slot, at : at + rows] = jnp.where(mine == 0, a, b).astype(BF)
        send[slot, at : at + rows] = jnp.where(mine == 0, b, a).astype(BF)
        slot += 1


def outer_kernel(stride, bit, layout, ids, *refs):
    spots = iter(refs)
    operands = [[([(next(spots), n) for n in left], next(spots)) for left in parts] for parts in layout]
    outs = [next(spots) for _ in range(2 if stride else len(layout))]
    at = 0
    for i, parts in enumerate(operands):
        total, left, right = next(spots), next(spots), next(spots)
        pitch = left.shape[0] // len(parts)
        cols = right.shape[1]
        for p, (lefts, y) in enumerate(parts):
            rows = y.shape[0]
            if pitch > rows:
                left[p * pitch : (p + 1) * pitch] = jnp.zeros((pitch, left.shape[1]), BF)
                right[p * pitch : (p + 1) * pitch] = jnp.zeros((pitch, cols), BF)
            right[p * pitch : p * pitch + rows] = y[:, y.shape[1] - cols :]
            spot = 0
            for x, n in lefts:
                left[p * pitch : p * pitch + rows, spot : spot + n] = x[:, :n]
                spot += n
        step = 3 * LANES
        for j in range(left.shape[1] // step):
            span = slice(j * step, (j + 1) * step)
            total[span, :] = dot(left[:, span], right[...], (0, 0))
        if stride:
            split_blocks(total, outs[0], outs[1], at, ids[1 + bit], stride)
            at += left.shape[1] // (2 * outs[0].shape[0])
        else:
            outs[i][...] = total[...].astype(BF)


def combine_kernel(stride, bit, ids, keep, got, kept, send):
    slot = 0
    for i in range(keep.shape[0]):
        if i // stride % 2:
            continue
        a = keep[i].astype(F32) + got[i].astype(F32)
        b = keep[i + stride].astype(F32) + got[i + stride].astype(F32)
        kept[slot] = jnp.where(ids[1 + bit] == 0, a, b).astype(BF)
        send[slot] = jnp.where(ids[1 + bit] == 0, b, a).astype(BF)
        slot += 1


def add_kernel(ids, *refs):
    total = refs[0][...].astype(F32)
    for ref in refs[1:-1]:
        total += ref[...].astype(F32)
    refs[-1][...] = total.astype(refs[-1].dtype)


def result_kernel(ids, biases, *refs):
    total = biases[4:5]
    for ref in refs[:-1]:
        total = total + ref[...].astype(F32)
    refs[-1][...] = total.astype(BF)


def half_kernel(ids, keep_two, got_two, keep_one, got_one, own, far):
    half = own.shape[2]
    for i, (keep, got) in enumerate(((keep_two, got_two), (keep_one, got_one))):
        total = keep[0].astype(F32) + got[0].astype(F32)
        left, right = total[:, :half], total[:, half:]
        own[i] = jnp.where(ids[0] == 0, left, right)
        far[i] = jnp.where(ids[0] == 0, right, left).astype(BF)


def join_kernel(ids, own, far, two, one):
    rows = own.shape[1]
    for i in range(2):
        here, there = own[i], far[i].astype(F32)
        first, second = jnp.where(ids[0] == 0, here, there), jnp.where(ids[0] == 0, there, here)
        if i == 0:
            two[:rows] = first
            two[rows:] = second
        else:
            one[...] = jnp.concatenate([first, second], 0).T


def ends_kernel(split, ids, keep_two, got_two, proj, skip):
    total = keep_two[0].astype(F32) + got_two[0].astype(F32)
    proj[...] = total[:split]
    skip[...] = total[split:]


def turn_kernel(ids, keep, got, out):
    out[...] = (keep[0].astype(F32) + got[0].astype(F32)).T


def home_kernel(ids, counts, result, back_a, back_b, output, grad_skip):
    rows = result.shape[0]
    seq = ids[0]
    spot = lax.broadcasted_iota(jnp.int32, (rows, 1), 0) + seq * rows
    live = jnp.logical_and(spot < 2 * rows - PADDED, counts[0] > 0)
    output[...] = jnp.where(live, result[...].astype(F32), 0.0).astype(BF)
    a, b = back_a[...].astype(F32), back_b[...].astype(F32)
    grad_skip[:rows] = jnp.where(seq == 0, a, b).astype(BF)
    grad_skip[rows:] = jnp.where(seq == 0, b, a).astype(BF)


def last_kernel(
    ids, gq, gkv, merged, grad_after, w_skip, w_qkv, gains, sums_two, sums_out, units_own, units_far,
    gm_own, gm_far, grad_hidden, back_a, back_b, small,
):
    width = gq.shape[1]
    half = width // 2
    xhat, rstd = norm(merged[...])
    gn = dot(gq[...], w_qkv[:, :width], (1, 1))
    gn += dot(gkv[...], w_qkv[:, width:], (1, 1))
    value = grad_after[...] + norm_back(gn, xhat, rstd, gains[0:1])
    units = units_own[0:1] + units_far[0:1]
    spot = 2 * ids[1] + ids[0]
    small[...] = jnp.concatenate(
        [
            jnp.sum(gn * xhat, axis=0, keepdims=True),
            sums_two[0:1],
            jnp.sum(value, axis=0, keepdims=True),
            jnp.sum(gn, axis=0, keepdims=True),
            sums_two[2:3],
            sums_two[1:2],
            sums_out[0:1],
            jnp.zeros((1, width), F32),
        ]
        + [jnp.where(spot == i, units, 0.0) for i in range(4)]
        + [jnp.zeros((4, width), F32)],
        0,
    )
    halves = value[:, :half], value[:, half:]
    gm_own[...] = jnp.where(ids[0] == 0, halves[0], halves[1]).astype(BF)
    gm_far[...] = jnp.where(ids[0] == 0, halves[1], halves[0]).astype(BF)
    low = value.astype(BF)
    grad_hidden[...] = dot(low, w_skip[:width], (1, 1)).astype(BF)
    a = dot(low, w_skip[width : width + half], (1, 1))
    b = dot(low, w_skip[width + half :], (1, 1))
    back_a[...] = jnp.where(ids[1] == 0, a, b).astype(BF)
    back_b[...] = jnp.where(ids[1] == 0, b, a).astype(BF)


def shards(
    hidden_in,
    skip_in,
    cotangent,
    timesteps,
    counts,
    w_skip,
    w_qkv,
    w_proj,
    w_fc1,
    w_fc2,
    gains,
    biases,
    fc1_bias,
):
    rows, width = hidden_in.shape[1:]
    half = width // 2
    ff = w_fc1.shape[1]
    n_dp = lax.axis_size("dp")
    bits = n_dp.bit_length() - 1
    pairs = n_dp // 2
    place = lax.axis_index("dp")
    core = place % 2
    seq = lax.axis_index("seq")
    piece = ff // (4 * pairs)
    quarter = pairs * piece
    ids = jnp.stack([seq] + [(place >> b) & 1 for b in range(bits)]).astype(jnp.int32)
    ids = lax.optimization_barrier(ids)
    pitch = -(-rows // GAP) * GAP

    def flat(dp, s):
        return 2 * dp + s

    mirror_perm = [
        (flat(2 * k + c, s), flat(2 * k + s, c)) for k in range(pairs) for c in range(2) for s in range(2)
    ]
    turn = {(0, 0): (1, 0), (1, 0): (1, 1), (1, 1): (0, 1), (0, 1): (0, 0)}
    turn_perm = [
        (flat(2 * k + c, s), flat(2 * k + d[0], d[1])) for k in range(pairs) for (c, s), d in turn.items()
    ]
    turn_back_perm = [(b, a) for a, b in turn_perm]

    def mirror(x):
        return lax.ppermute(x, ("dp", "seq"), mirror_perm)

    def across_seq(x):
        return lax.ppermute(x, "seq", [(0, 1), (1, 0)])

    def across_bit(x, bit):
        return lax.ppermute(x, "dp", [(i, i ^ (1 << bit)) for i in range(n_dp)])

    def across_core(x):
        return across_bit(x, 0)

    def swap_if(flag, a, b, axis):
        return jnp.where(flag, jnp.concatenate([b, a], axis), jnp.concatenate([a, b], axis))

    def my_bit(bit):
        return (place >> bit) & 1

    marks = []

    def run(kernel, name, operands, outs, scratch, mib, flops):
        results = call(
            kernel,
            name,
            [(ids, IN_SMEM)] + [a if isinstance(a, tuple) else (a, IN_VMEM) for a in operands],
            outs,
            scratch,
            mib,
            flops,
            marks[-1:],
        )
        marks.append(results[-1])
        return results[:-1]

    def later(x):
        return lax.optimization_barrier((x, marks[-1]))[0]

    token = shape((rows, width), BF)
    token32 = shape((rows, width), F32)
    half_token = shape((rows, half), BF)
    sums = shape((8, width), F32)
    work = 2 * rows * width * width

    hidden = mirror(hidden_in[0])
    skip_a, skip_b, g_home, sum_grad_out = run(
        pack_kernel,
        "pack",
        [(timesteps, IN_SMEM), (counts, IN_SMEM), skip_in[0], cotangent[0]],
        [half_token, half_token, token, sums],
        [],
        0,
        work // 100,
    )
    skip_a = mirror(skip_a)
    skip_b = lax.ppermute(skip_b, ("dp", "seq"), turn_perm)
    g_far = across_seq(g_home)
    g_other = across_core(g_home)

    if piece % GAP == 0 and piece <= 2 * LANES - 7 * GAP:
        w1, w2, b1 = run(
            gather_kernel,
            "gather",
            [(w_fc1, IN_HBM), (w_fc2.reshape(4 * pairs, piece, width), IN_HBM), fc1_bias.reshape(1, ff)],
            [shape((width, quarter), BF), shape((pairs, piece, width), BF), shape((8, quarter), F32)],
            [pltpu.VMEM((pairs, width, 2 * LANES), BF), pltpu.SemaphoreType.DMA((2 * pairs,))],
            56,
            work // 100,
        )
    else:
        w1 = pick(pick(w_fc1.reshape(width, pairs, 2, 2, piece), core, 2), seq, 2).reshape(width, quarter)
        w2 = pick(pick(w_fc2.reshape(pairs, 2, 2, piece, width), core, 1), seq, 1)
        b1 = pick(pick(fc1_bias.reshape(pairs, 2, 2, piece), core, 1), seq, 1).reshape(1, quarter)
        b1 = jnp.broadcast_to(b1, (8, quarter))
    w2 = w2.reshape(quarter, width)

    merged, early, normed_own, q, kv = run(
        first_kernel,
        "first",
        [hidden, skip_a, skip_b, w_skip, w_qkv, gains, biases],
        [token32, shape((rows, 2 * width + half), BF), half_token, token, shape((rows, 2 * width), BF)],
        [],
        0,
        5 * work,
    )
    kv_other = across_core(kv)
    key_buf = pltpu.VMEM((2 * pitch, width), BF)
    proj_buf = [pltpu.VMEM((width, width), BF), pltpu.SemaphoreType.DMA((1,))]
    mixed, after_attn, normed_two, log_total = run(
        attend_kernel,
        "attend",
        [q, kv, kv_other, merged, (w_proj, IN_ANY), gains, biases],
        [token, token32, token, shape((rows, LANES), F32)],
        [key_buf, key_buf, *proj_buf],
        0,
        2 * work,
    )

    n_far = across_seq(normed_two)
    n_other = across_core(normed_two)
    g_other_far = across_core(later(g_far))

    def mlp(name, n0, n1, *g):
        tall = shape((2 * pitch, quarter), BF)
        wide = shape((2 * pitch, width), BF)
        return run(
            mlp_kernel,
            name,
            [n0, n1, *g, w1, b1, w2],
            [tall, tall, wide, wide, token32, token, shape((8, quarter), F32)],
            [pltpu.VMEM((2 * pitch, 3 * LANES), F32), pltpu.VMEM((2 * pitch, 3 * LANES), F32)],
            0,
            6 * 2 * rows * width * quarter,
        )

    act_own, gi_own, nn_own, gg_own, gn_own, gn_own_core, si_own = mlp(
        "mlp_own", normed_two, n_other, g_home, g_other_far, g_far, g_other
    )
    n_other_far = across_core(later(n_far))
    early_far = across_seq(later(early))
    act_far, gi_far, nn_far, gg_far, gn_far, gn_far_core, si_far = mlp(
        "mlp_far", n_far, n_other_far, g_other, g_far, g_other_far, g_home
    )
    gn_far_core = across_core(gn_far_core)
    gn_own_core = across_core(gn_own_core)

    def outer(name, products, blocks, bit, shift):
        lefts = [sum(n for _, n in parts[0][0]) for _, parts in products]
        rows_of = [n // blocks for n in lefts]
        inside = all(r % 8 == 0 for r in rows_of)
        cols = products[0][0]
        stride = (1 << (bit - shift)) if inside else 0
        scratch, operands = [], []
        for n, (c, parts) in zip(lefts, products):
            height = -(-parts[0][1].shape[0] // GAP) * GAP * len(parts)
            scratch += [pltpu.VMEM((n, c), F32), pltpu.VMEM((height, n), BF), pltpu.VMEM((height, c), BF)]
            for left, right in parts:
                operands += [x for x, _ in left] + [right]
        if inside:
            outs = [shape((blocks // 2, sum(rows_of), cols), BF)] * 2
        else:
            outs = [shape((n, cols), BF) for n in lefts]
        layout = [[[n for _, n in left] for left, _ in parts] for _, parts in products]
        results = run(
            functools.partial(outer_kernel, stride, bit, layout),
            name,
            operands,
            outs,
            scratch,
            0,
            sum(2 * n * cols * 4 * rows for n in lefts),
        )
        if inside:
            return results
        whole = jnp.concatenate([x.reshape(blocks, r, cols) for x, r in zip(results, rows_of)], 1)
        whole = whole.reshape(blocks >> (bit - shift + 1), 2, 1 << (bit - shift), sum(rows_of), cols)
        flat_shape = (blocks // 2, sum(rows_of), cols)
        return [pick(whole, i, 1).reshape(flat_shape) for i in (my_bit(bit), 1 - my_bit(bit))]

    def combine(name, keep, got, left, bit):
        count, r, cols = keep.shape
        stride = 1 << left.index(bit)
        if r % 8 == 0:
            return run(
                functools.partial(combine_kernel, stride, bit),
                name,
                [keep, got],
                [shape((count // 2, r, cols), BF)] * 2,
                [],
                0,
                work // 100,
            )
        both = (keep.astype(F32) + got.astype(F32)).astype(BF).reshape(count // (2 * stride), 2, stride, r, cols)
        return [pick(both, i, 1).reshape(count // 2, r, cols) for i in (my_bit(bit), 1 - my_bit(bit))]

    class Chain:
        def __init__(self, name, order, parts):
            self.name, self.order = name, order
            self.keep, send = parts
            self.step = 0
            self.left = sorted(order[1:])
            self.got = across_bit(send, order[0])

        def advance(self):
            self.step += 1
            if self.step >= len(self.order):
                return
            bit = self.order[self.step]
            self.keep, send = combine(f"{self.name}_{self.step}", self.keep, self.got, self.left, bit)
            self.left.remove(bit)
            self.got = across_bit(send, bit)

    def order_of(first):
        return first + list(range(4, bits))

    def add(name, out, *terms):
        return run(add_kernel, name, list(terms), [out], [], 0, work // 100)[0]

    fc2 = Chain(
        "fc2",
        order_of([1, 2, 3]),
        outer("outer_fc2", [(width, [([(act_own, quarter)], gg_own), ([(act_far, quarter)], gg_far)])], pairs, 1, 1),
    )
    gn_far = across_seq(add("gn_add", token, gn_far, gn_far_core))
    fc1 = Chain(
        "fc1",
        order_of([2, 1, 3]),
        outer("outer_fc1", [(width, [([(gi_own, quarter)], nn_own), ([(gi_far, quarter)], nn_far)])], pairs, 2, 1),
    )

    grad_after, ga_own, ga_far, grad_q, gkv_own, gkv_other, sums_two = run(
        attend_back_kernel,
        "attend_back",
        [gn_own, gn_own_core, gn_far, g_home, g_other_far, after_attn, q, kv, kv_other, log_total]
        + [(w_proj, IN_ANY), gains],
        [token32, half_token, half_token, token]
        + [shape((rows, 2 * width), F32), shape((rows, 2 * width), BF), sums],
        [key_buf, key_buf, proj_buf[0], pltpu.VMEM((2 * pitch, width), F32), pltpu.VMEM((2 * pitch, width), F32), proj_buf[1]],
        0,
        3 * work,
    )
    gkv_core = across_core(gkv_other)
    gq_far = across_seq(grad_q)
    out_own, out_far, out_own_core, out_far_core = run(
        lambda ids, *refs: mlp_out_kernel(*refs),
        "mlp_out",
        [act_own, act_far, w2],
        [token32, token32, token, token],
        [],
        0,
        2 * 4 * rows * width * quarter,
    )
    gkv = add("gkv_add", shape((rows, 2 * width), BF), gkv_own, gkv_core)
    gkv_far = across_seq(gkv)
    ga_far = across_seq(ga_far)
    out_own_core, out_far_core = across_core(out_own_core), across_core(out_far_core)
    gm_own, gm_far, grad_hidden, back_a, back_b, small = run(
        last_kernel,
        "last",
        [grad_q, gkv, merged, grad_after, w_skip, w_qkv, gains, sums_two, sum_grad_out, si_own, si_far],
        [half_token, half_token, token, half_token, half_token, shape((16, width), F32)],
        [],
        0,
        5 * work,
    )
    gm_far = across_seq(gm_far)
    mixed_far = across_seq(later(mixed))

    fc2.advance()
    fc1.advance()
    small = add("small_0", shape(small.shape, F32), small, across_core(small))
    out_far = across_seq(add("out_add", token, out_far, out_far_core))
    second = Chain(
        "second",
        order_of([0, 2, 1, 3]),
        outer(
            "outer_second",
            [
                (half, [([(mixed, width)], ga_own), ([(mixed_far, width)], ga_far)]),
                (half, [([(early, 2 * width)], gm_own), ([(early_far, 2 * width)], gm_far)]),
            ],
            n_dp,
            0,
            0,
        ),
    )
    small = add("small_1", shape(small.shape, F32), small, across_seq(small))
    second.advance()
    fc2.advance()
    fc1.advance()
    third = Chain(
        "third",
        order_of([0, 1, 2, 3]),
        outer(
            "outer_third",
            [
                (
                    half,
                    [
                        ([(grad_q, width), (gkv, 2 * width)], normed_own),
                        ([(gq_far, width), (gkv_far, 2 * width)], early_far),
                    ],
                )
            ],
            n_dp,
            0,
            0,
        ),
    )
    small = add("small_2", shape(small.shape, F32), small, across_bit(small, 1))
    result = run(
        result_kernel,
        "result",
        [biases, after_attn, out_own, out_own_core, out_far],
        [token],
        [],
        0,
        work // 100,
    )[0]
    third.advance()
    grad_hidden = mirror(later(grad_hidden))
    back_a = mirror(later(back_a))
    back_b = lax.ppermute(later(back_b), ("dp", "seq"), turn_back_perm)
    result = mirror(result)
    small = add("small_3", shape(small.shape, F32), small, across_bit(small, 2))
    while fc2.step + 1 < len(fc2.order):
        fc2.advance()
        fc1.advance()
    own, far = run(
        half_kernel,
        "half",
        [fc2.keep, fc2.got, fc1.keep, fc1.got],
        [shape((2, piece, half), F32), shape((2, piece, half), BF)],
        [],
        0,
        work // 100,
    )
    far = across_seq(far)
    for bit in range(3, bits):
        small = add(f"small_{bit + 1}", shape(small.shape, F32), small, across_bit(small, bit))
    while second.step + 1 < len(second.order):
        second.advance()
        third.advance()
    output, grad_skip = run(
        home_kernel,
        "home",
        [(counts, IN_SMEM), result, back_a, back_b],
        [token, shape((2 * rows, half), BF)],
        [],
        0,
        work // 100,
    )
    out_w_fc2, out_w_fc1 = run(
        join_kernel,
        "join",
        [own, far],
        [shape((2 * piece, half), F32), shape((half, 2 * piece), F32)],
        [],
        0,
        work // 100,
    )
    split = width // n_dp
    out_w_proj, out_w_skip = run(
        functools.partial(ends_kernel, split),
        "ends",
        [second.keep, second.got],
        [shape((split, half), F32), shape((2 * split, half), F32)],
        [],
        0,
        work // 100,
    )
    (out_w_qkv,) = run(
        turn_kernel,
        "turn",
        [third.keep, third.got],
        [shape((half, 3 * split), F32)],
        [],
        0,
        work // 100,
    )
    fc1_bias_grad = small[8:12].reshape(2, 2, pairs, piece).transpose(2, 0, 1, 3).reshape(ff)
    return (
        output[None],
        grad_hidden[None],
        grad_skip[None],
        out_w_skip,
        out_w_qkv,
        out_w_proj,
        out_w_fc1,
        out_w_fc2,
        small[:2],
        small[2:7],
        fc1_bias_grad,
    )


def solution(mesh):
    return jax.shard_map(
        shards,
        mesh=mesh,
        in_specs=(
            P("dp", "seq", None),
            P("dp", None, "seq"),
            P("dp", "seq", None),
            P("dp"),
            P("dp"),
            P(),
            P(),
            P(),
            P(),
            P(),
            P(),
            P(),
            P(),
        ),
        out_specs=(
            P("dp", "seq", None),
            P("dp", "seq", None),
            P("dp", None, "seq"),
            P("dp", "seq"),
            P("seq", "dp"),
            P("dp", "seq"),
            P("seq", "dp"),
            P("dp", "seq"),
            P(),
            P(),
            P(),
        ),
        check_vma=False,
    )
```

```python
import functools

import jax
import jax.numpy as jnp
from jax import lax
from jax.experimental import pallas as pl
from jax.experimental.pallas import tpu as pltpu
from jax.sharding import PartitionSpec as P

HEADS = 16
PADDED = 2
TSTEPS = 1000

EPSILON = 1e-06
NEG_FILL = -1e30
BF = jnp.bfloat16
F32 = jnp.float32
MIB = 1 << 20
LANES = 128
GAP = 16


def dot(left, right, dims):
    return lax.dot_general(left, right, ((dims[:1], dims[1:]), ((), ())), preferred_element_type=F32)


def norm(value):
    center = value - jnp.mean(value, axis=-1, keepdims=True)
    rstd = lax.rsqrt(jnp.mean(center * center, axis=-1, keepdims=True) + EPSILON)
    return center * rstd, rstd


def norm_back(grad, xhat, rstd, gain):
    scaled = grad * gain
    return rstd * (
        scaled
        - jnp.mean(scaled, axis=-1, keepdims=True)
        - xhat * jnp.mean(scaled * xhat, axis=-1, keepdims=True)
    )


def pick(array, index, axis):
    return lax.dynamic_index_in_dim(array, index, axis, keepdims=False)


def shape(dims, dtype):
    return jax.ShapeDtypeStruct(dims, dtype)


def padded(dims, dtype):
    dims = (1,) * (2 - len(dims)) + tuple(dims)
    size = -(-dims[-2] // 16) * 16 * -(-dims[-1] // LANES) * LANES
    for dim in dims[:-2]:
        size *= dim
    return size * jnp.dtype(dtype).itemsize


GATHER_MIB = 55
FIRST_MIB = 50
PIECES = 4
UNROLL = True
SCALE = 0.3
TAKES = {
    "pack": 12.0,
    "gather": 8.0,
    "first": 4.4,
    "attend": 6.6,
    "mlp": 6.0,
    "outer": 3.2,
    "attend_back": 10.3,
    "last": 6.3,
}


IN_VMEM = pl.BlockSpec(memory_space=pltpu.VMEM)
IN_SMEM = pl.BlockSpec(memory_space=pltpu.SMEM)
IN_ANY = pl.BlockSpec(memory_space=pl.ANY)
IN_HBM = pl.BlockSpec(memory_space=pltpu.HBM)


def call(kernel, name, operands, outs, scratch, mib, flops, after=()):
    takes = TAKES.get(name, TAKES.get(name.split("_")[0], 1.0)) * SCALE
    outs = [*outs, shape((8, LANES), F32)]
    inputs = len(operands)
    marks = len(after)
    if not mib:
        need = sum(padded(a.shape, a.dtype) for a, spec in operands if spec is IN_VMEM)
        need += sum(padded(o.shape, o.dtype) for o in outs)
        need += sum(padded(b.shape, b.dtype) for b in scratch if b.memory_space == pltpu.VMEM)
        mib = need * 9 // 8 // MIB + 4

    def body(*refs):
        mark = refs[inputs + marks + len(outs) - 1]
        mark[...] = jnp.zeros_like(mark)
        kernel(*refs[:inputs], *refs[inputs + marks : inputs + marks + len(outs) - 1], *refs[inputs + marks + len(outs) :])

    return pl.pallas_call(
        body,
        out_shape=outs,
        in_specs=[spec for _, spec in operands] + [IN_ANY] * marks,
        out_specs=[IN_VMEM] * len(outs),
        scratch_shapes=scratch,
        compiler_params=pltpu.CompilerParams(vmem_limit_bytes=mib * MIB),
        cost_estimate=pl.CostEstimate(flops=int(takes * 1e9), bytes_accessed=int(takes * 3.6e6), transcendentals=0),
        name=name,
    )(*[a for a, _ in operands], *after)


def fetch(pairs, sems):
    copies = [pltpu.make_async_copy(src, dst, sems.at[i]) for i, (src, dst) in enumerate(pairs)]
    for copy in copies:
        copy.start()
    return copies


def gather_kernel(ids, w_fc1, bias, w1, b1, windows, sems):
    pieces = windows.shape[0]
    core, seq = ids[1], ids[0]
    piece_size = w1.shape[1] // pieces
    which = [4 * m + 2 * core + seq for m in range(pieces)]
    spots = [w * piece_size for w in which]
    copies = fetch(
        [
            (w_fc1.at[:, pl.ds(pl.multiple_of(s // LANES * LANES, LANES), 2 * LANES)], windows.at[m])
            for m, s in enumerate(spots)
        ],
        sems,
    )
    lane = lax.broadcasted_iota(jnp.int32, (8, LANES), 1)
    for m in range(pieces):
        base, into = m * piece_size // LANES * LANES, m * piece_size % LANES
        window = [bias[pl.ds(spots[m] // LANES + i, 1), :] for i in range(2)]
        window = jnp.concatenate([jnp.broadcast_to(x, (8, LANES)) for x in window], 1)
        turn = (into - spots[m] % LANES + 2 * LANES) % (2 * LANES)
        window = pltpu.roll(window, turn, 1)
        left = window[:, :LANES]
        if into:
            left = jnp.where(lane >= into, left, b1[:, base : base + LANES])
        b1[:, base : base + LANES] = left
        b1[:, base + LANES : base + 2 * LANES] = window[:, LANES:]
    source = lax.broadcasted_iota(jnp.int32, (2 * LANES, 2 * LANES), 0)
    target = lax.broadcasted_iota(jnp.int32, (2 * LANES, 2 * LANES), 1)
    before = {}
    for m in range(pieces):
        base = m * piece_size // LANES * LANES
        copies[m].wait()
        column = target + (base - m * piece_size)
        take = jnp.logical_and(column >= 0, column < piece_size)
        take = jnp.logical_and(take, source == column + spots[m] % LANES)
        part = dot(windows[m], take.astype(F32).astype(BF), (1, 0))
        for at, half in ((base, part[:, :LANES]), (base + LANES, part[:, LANES:])):
            before[at] = before[at] + half if at in before else half
        for at in [x for x in before if x <= base]:
            w1[:, at : at + LANES] = before.pop(at).astype(BF)
    for at, half in before.items():
        w1[:, at : at + LANES] = half.astype(BF)


def pack_kernel(ids, skip_in, skip_a, skip_b, skip, sems):
    rows = skip_a.shape[0]
    seq = ids[0]
    fetch([(skip_in, skip)], sems)[0].wait()
    whole = skip[...].astype(F32)
    top, bottom = whole[:rows], whole[rows:]
    skip_a[...] = jnp.where(seq == 0, top, bottom).astype(BF)
    skip_b[...] = jnp.where(seq == 0, bottom, top).astype(BF)


def grad_out_kernel(ids, timesteps, counts, cotangent_in, g_home, sums, cotangent, sems):
    rows, width = cotangent.shape
    fetch([(cotangent_in, cotangent)], sems)[0].wait()
    time = jnp.zeros((1, 1), F32) + timesteps[0].astype(F32)
    weight = jax.nn.sigmoid(12.0 * time / TSTEPS - 6.0)
    spot = lax.broadcasted_iota(jnp.int32, (rows, 1), 0) + ids[0] * rows
    live = jnp.logical_and(spot < 2 * rows - PADDED, counts[0] > 0)
    g = cotangent[...].astype(F32) * jnp.where(live, weight, 0.0)
    g_home[...] = g.astype(BF)
    sums[...] = jnp.concatenate([jnp.sum(g, axis=0, keepdims=True), jnp.zeros((7, width), F32)], 0)


def first_kernel(ids, hidden, skip_a, skip_b, w_skip_far, w_qkv, gains, biases, merged, early_a, early_b, q, kv, w_skip, sems):
    parts = [(0, hidden.shape[1]), (hidden.shape[1], skip_a.shape[1]), (hidden.shape[1] + skip_a.shape[1], skip_a.shape[1])]
    copies = fetch([(w_skip_far.at[pl.ds(a, n)], w_skip.at[pl.ds(a, n)]) for a, n in parts], sems)
    width = hidden.shape[1]
    half = width // 2
    core = ids[1]
    a, b = skip_a[...].astype(F32), skip_b[...].astype(F32)
    low = jnp.where(core == 0, a, b).astype(BF)
    high = jnp.where(core == 0, b, a).astype(BF)
    early_a[:, :width] = hidden[...]
    early_a[:, width:] = low
    early_b[:, width:] = high
    copies[0].wait()
    total = dot(hidden[...], w_skip[:width], (1, 0)) + biases[0:1]
    copies[1].wait()
    total += dot(low, w_skip[width : width + half], (1, 0))
    copies[2].wait()
    total += dot(high, w_skip[width + half :], (1, 0))
    merged[...] = total
    xhat, _ = norm(total)
    one = (xhat * gains[0:1] + biases[1:2]).astype(BF)
    early_b[:, :width] = one
    kv[...] = dot(one, w_qkv[:, width:], (1, 0)).astype(BF)
    q[...] = dot(one, w_qkv[:, :width], (1, 0)).astype(BF)


def head_windows(width):
    size = width // HEADS
    spans = []
    for h in range(HEADS):
        low, high = h * size, (h + 1) * size
        t0, t1 = low // LANES, (high - 1) // LANES + 1
        spans.append((h, low, high, t0 * LANES, t1 * LANES))
    return spans


def lane_mask(low, high, first, last):
    lane = lax.broadcasted_iota(jnp.int32, (1, last - first), 1) + first
    return jnp.logical_and(lane >= low, lane < high)


def key_mask(core, rows, pitch):
    spot = lax.broadcasted_iota(jnp.int32, (1, 2 * pitch), 1)
    other = spot >= pitch
    here = jnp.where(other, spot - pitch, spot)
    last_half = jnp.where(other, 1 - core, core) == 1
    limit = jnp.where(last_half, rows - PADDED, rows)
    return here < limit


def lay_keys(keys, values, kv_own, kv_other, rows, pitch, width):
    for buf, at in ((keys, 0), (values, width)):
        buf[...] = jnp.zeros_like(buf)
        buf[0:rows] = kv_own[:, at : at + width]
        buf[pitch : pitch + rows] = kv_other[:, at : at + width]


def attend_kernel(ids, q, kv_own, kv_other, merged, early, w_proj, gains, biases, early_b, after, normed, log_total, keys, values, wp, sems):
    rows, width = q.shape
    pitch = keys.shape[0] // 2
    copies = fetch([(w_proj, wp)], sems)
    lay_keys(keys, values, kv_own, kv_other, rows, pitch, width)
    valid = key_mask(ids[1], rows, pitch)
    scale = (width // HEADS) ** (-0.5)
    lane = lax.broadcasted_iota(jnp.int32, (rows, LANES), 1)
    tiles = [jnp.zeros((rows, LANES), F32) for _ in range(width // LANES)]
    logs = jnp.zeros((rows, LANES), F32)
    for h, low, high, first, last in head_windows(width):
        mask = lane_mask(low, high, first, last)
        mine = q[:, first:last] * mask.astype(F32).astype(BF)
        scores = jnp.where(valid, dot(mine, keys[:, first:last], (1, 1)) * scale, NEG_FILL)
        top = jnp.max(scores, axis=-1, keepdims=True)
        expo = jnp.exp(scores - top)
        total = jnp.sum(expo, axis=-1, keepdims=True)
        probs = (expo * (1.0 / total)).astype(BF)
        logs = jnp.where(lane == h, top + jnp.log(total), logs)
        part = dot(probs, values[:, first:last], (1, 0))
        for t in range(first, last, LANES):
            tiles[t // LANES] = jnp.where(
                mask[:, t - first : t - first + LANES], part[:, t - first : t - first + LANES], tiles[t // LANES]
            )
    log_total[...] = logs
    for t, tile in enumerate(tiles):
        early_b[:, width + t * LANES : width + (t + 1) * LANES] = tile.astype(BF)
    copies[0].wait()
    early_b[:, :width] = early[:, :width]
    early_b[:, 2 * width :] = early[:, width:]
    value = merged[...] + dot(early_b[:, width : 2 * width], wp[...], (1, 0)) + biases[2:3]
    after[...] = value
    xhat, _ = norm(value)
    normed[...] = (xhat * gains[1:2] + biases[3:4]).astype(BF)


def attend_back_kernel(
    ids, gn_mine, gn_core, gn_far, g_home, g_cross, after, q, kv_own, kv_other, log_total, w_proj, gains,
    grad_after, ga_own, ga_far, grad_q, gkv_own, gk_other, gv_other, sums,
    keys, values, wp, gk, gv, sems,
):
    rows, width = q.shape
    half = width // 2
    pitch = keys.shape[0] // 2
    copies = fetch([(w_proj, wp)], sems)
    gn = gn_mine[...] + gn_core[...].astype(F32) + gn_far[...].astype(F32)
    xhat, rstd = norm(after[...])
    g_out = jnp.where(ids[0] == ids[1], g_home[...].astype(F32), g_cross[...].astype(F32))
    value = g_out + norm_back(gn, xhat, rstd, gains[1:2])
    grad_after[...] = value
    low = value.astype(BF)
    halves = value[:, :half], value[:, half:]
    ga_own[...] = jnp.where(ids[0] == 0, halves[0], halves[1]).astype(BF)
    ga_far[...] = jnp.where(ids[0] == 0, halves[1], halves[0]).astype(BF)
    sums[...] = jnp.concatenate(
        [
            jnp.sum(gn * xhat, axis=0, keepdims=True),
            jnp.sum(gn, axis=0, keepdims=True),
            jnp.sum(value, axis=0, keepdims=True),
            jnp.zeros((5, width), F32),
        ],
        0,
    )
    lay_keys(keys, values, kv_own, kv_other, rows, pitch, width)
    valid = key_mask(ids[1], rows, pitch)
    scale = (width // HEADS) ** (-0.5)
    copies[0].wait()
    grad_mixed = dot(low, wp[...], (1, 1)).astype(BF)
    gk[...] = jnp.zeros_like(gk)
    gv[...] = jnp.zeros_like(gv)
    lane = lax.broadcasted_iota(jnp.int32, (rows, LANES), 1)
    tiles = [jnp.zeros((rows, LANES), F32) for _ in range(width // LANES)]
    logs = log_total[...]
    for h, start, stop, first, last in head_windows(width):
        mask = lane_mask(start, stop, first, last)
        low_mask = mask.astype(F32).astype(BF)
        mine = q[:, first:last] * low_mask
        gm = grad_mixed[:, first:last] * low_mask
        log = jnp.sum(jnp.where(lane == h, logs, 0.0), axis=-1, keepdims=True)
        scores = jnp.where(valid, dot(mine, keys[:, first:last], (1, 1)) * scale, NEG_FILL)
        probs = jnp.exp(scores - log)
        gp = dot(gm, values[:, first:last], (1, 1))
        gs = (probs * (gp - jnp.sum(gp * probs, axis=-1, keepdims=True))).astype(BF)
        part = dot(gs, keys[:, first:last], (1, 0))
        for t in range(first, last, LANES):
            tiles[t // LANES] = jnp.where(
                mask[:, t - first : t - first + LANES], part[:, t - first : t - first + LANES], tiles[t // LANES]
            )
        gk[:, first:last] += dot(gs, mine, (0, 0))
        gv[:, first:last] += dot(probs.astype(BF), gm, (0, 0))
    for t, tile in enumerate(tiles):
        grad_q[:, t * LANES : (t + 1) * LANES] = (tile * scale).astype(BF)
    gkv_own[:, :width] = gk[0:rows] * scale
    gkv_own[:, width:] = gv[0:rows]
    gk_other[...] = (gk[pitch : pitch + rows] * scale).astype(BF)
    gv_other[...] = gv[pitch : pitch + rows].astype(BF)


def lay_rows(buf, blocks):
    rows = blocks[0].shape[0]
    pitch = buf.shape[0] // len(blocks)
    if pitch > rows:
        buf[...] = jnp.zeros_like(buf)
    for i, block in enumerate(blocks):
        buf[i * pitch : i * pitch + rows] = block[...]


def lay_chosen(buf, flag, pairs):
    rows = pairs[0][0].shape[0]
    pitch = buf.shape[0] // len(pairs)
    buf[...] = jnp.zeros_like(buf)
    for way, chosen in enumerate((flag, jnp.logical_not(flag))):

        @pl.when(chosen)
        def _(way=way):
            for i, pair in enumerate(pairs):
                buf[i * pitch : i * pitch + rows] = pair[way][...]


def mlp_first_kernel(ids, n0, n1, g0a, g0b, g1a, g1b, w1, b1, w_fc2, *refs):
    outs, (w2, buf_a, buf_b, sems) = refs[:7], refs[7:]
    pieces = sems.shape[0]
    piece = w2.shape[0] // pieces
    copies = fetch(
        [
            (w_fc2.at[4 * m + 2 * ids[1] + ids[0]], w2.at[pl.ds(m * piece, piece)])
            for m in range(pieces)
        ],
        sems,
    )
    mlp_kernel(ids, n0, n1, g0a, g0b, g1a, g1b, w1, b1, w2, *outs, buf_a, buf_b, copies=copies)


def mlp_kernel(ids, n0, n1, g0a, g0b, g1a, g1b, w1, b1, w2, activ, grad_inner, n_all, g_all, gn_mine, gn_other, sums, inner_v, grad_v, copies=()):
    rows, width = n0.shape
    units = w1.shape[1]
    lay_rows(n_all, (n0, n1))
    lay_chosen(g_all, ids[0] == ids[1], ((g0a, g0b), (g1a, g1b)))
    height = n_all.shape[0]
    pitch = height // 2
    step = 3 * LANES
    chunk = 48
    root = 0.5**0.5
    bell = (0.5 / jnp.pi) ** 0.5
    for j in range(units // step):
        cols = slice(j * step, (j + 1) * step)
        inner_v[...] = dot(n_all[...], w1[:, cols], (1, 0))
        for copy in copies:
            copy.wait()
        copies = ()
        grad_v[...] = dot(g_all[...], w2[cols, :], (1, 1))
        bias = b1[0:1, cols]

        def body(i, total):
            at = pl.ds(pl.multiple_of(i * chunk, chunk), chunk)
            x = inner_v[at] + bias
            cdf = 0.5 + 0.5 * lax.erf(x * root)
            activ[at, cols] = (x * cdf).astype(BF)
            g = grad_v[at] * (cdf + x * jnp.exp(-0.5 * x * x) * bell)
            grad_inner[at, cols] = g.astype(BF)
            return total + jnp.sum(g, axis=0, keepdims=True)

        sums[0:1, cols] = lax.fori_loop(0, height // chunk, body, jnp.zeros((1, step), F32), unroll=UNROLL)
    for j in range(width // step):
        cols = slice(j * step, (j + 1) * step)
        part = dot(grad_inner[...], w1[cols, :], (1, 1))
        gn_mine[:, cols] = part[:rows]
        gn_other[:, cols] = part[pitch : pitch + rows].astype(BF)


def mlp_out_kernel(activ_own, activ_far, w2, own, far, own_core, far_core):
    rows = own.shape[0]
    pitch = activ_own.shape[0] // 2
    step = 3 * LANES
    for activ, mine, other in ((activ_far, far, far_core), (activ_own, own, own_core)):
        for j in range(w2.shape[1] // step):
            cols = slice(j * step, (j + 1) * step)
            part = dot(activ[...], w2[:, cols], (1, 0))
            mine[:, cols] = part[:rows]
            other[:, cols] = part[pitch : pitch + rows].astype(BF)


def split_blocks(total, keep, sends, at, mine, stride):
    count = keep.shape[0]
    rows = total.shape[0] // (2 * count)
    slot = 0
    for i in range(2 * count):
        if i // stride % 2:
            continue
        a = total[i * rows : (i + 1) * rows]
        b = total[(i + stride) * rows : (i + stride + 1) * rows]
        keep[slot, at : at + rows] = jnp.where(mine == 0, a, b).astype(BF)
        per = sends[0].shape[0]
        sends[slot // per][slot % per, at : at + rows, : keep.shape[2]] = jnp.where(mine == 0, b, a).astype(BF)
        slot += 1


def outer_kernel(stride, bit, layout, pieces, ids, *refs):
    spots = iter(refs)
    operands = [
        [([(next(spots), *span) for span in left], (next(spots), right)) for left, right in parts] for parts in layout
    ]
    outs = [next(spots) for _ in range(1 + pieces if stride else len(layout))]
    at = 0
    for i, parts in enumerate(operands):
        total, left, right = next(spots), next(spots), next(spots)
        pitch = left.shape[0] // len(parts)
        cols = right.shape[1]
        for p, (lefts, (y, first)) in enumerate(parts):
            rows = lefts[0][0].shape[0]
            if pitch > rows:
                left[p * pitch : (p + 1) * pitch] = jnp.zeros((pitch, left.shape[1]), BF)
                right[p * pitch : (p + 1) * pitch] = jnp.zeros((pitch, cols), BF)
            right[p * pitch : p * pitch + rows] = y[:rows, first : first + cols]
            spot = 0
            for x, start, n in lefts:
                left[p * pitch : p * pitch + rows, spot : spot + n] = x[:, start : start + n]
                spot += n
        step = 3 * LANES
        for j in range(0, left.shape[1], step):
            span = slice(j, min(j + step, left.shape[1]))
            total[span, :] = dot(left[:, span], right[...], (0, 0))
        if stride:
            split_blocks(total, outs[0], outs[1:], at, ids[1 + bit], stride)
            at += left.shape[1] // (2 * outs[0].shape[0])
        else:
            outs[i][...] = total[...].astype(BF)


def combine_kernel(stride, bit, ids, keep, *refs):
    gots, kept, send = refs[:-2], refs[-2], refs[-1]
    slot = 0
    cols = keep.shape[2]
    per = gots[0].shape[0]

    def total(i):
        return keep[i].astype(F32) + gots[i // per][i % per, :, :cols].astype(F32)

    for i in range(keep.shape[0]):
        if i // stride % 2:
            continue
        a, b = total(i), total(i + stride)
        kept[slot] = jnp.where(ids[1 + bit] == 0, a, b).astype(BF)
        send[slot, :, :cols] = jnp.where(ids[1 + bit] == 0, b, a).astype(BF)
        slot += 1


def ride_outer_kernel(stride, bit, layout, pieces, ids, *refs):
    inputs = sum(len(left) + 1 for parts in layout for left, _ in parts)
    operands, small, outs, scratch = refs[:inputs], refs[inputs], refs[inputs + 1 : inputs + 3 + pieces], refs[inputs + 3 + pieces :]
    keep, sends, riding = outs[0], outs[1:-1], outs[-1]
    outer_kernel(stride, bit, layout, pieces, ids, *operands, keep, *sends, *scratch)
    far = operands[-1]
    half = small.shape[1] // 2
    low = far[far.shape[0] - 32 :, :].astype(F32)
    total = small[...] + jnp.concatenate([low[:16], low[16:]], 1)
    cols = keep.shape[2]
    extra = sends[0].shape[2] - cols
    for j in range(small.shape[1] // extra):
        riding[12 * j : 12 * j + 12, :] = total[:12, extra * j : extra * (j + 1)]
    for send in sends:
        send[:, :, cols:] = jnp.zeros((send.shape[0], send.shape[1], extra), BF)
    sends[0][0, :, cols:] = riding[...].astype(BF)


def ride_combine_kernel(stride, bit, ids, keep, riding, *refs):
    gots, (kept, send, rode) = refs[:-3], refs[-3:]
    combine_kernel(stride, bit, ids, keep, *gots, kept, send)
    cols = keep.shape[2]
    total = riding[...] + gots[0][0, :, cols:].astype(F32)
    rode[...] = total
    if send.shape[0] > 1:
        send[1:, :, cols:] = jnp.zeros((send.shape[0] - 1, send.shape[1], send.shape[2] - cols), BF)
    send[0, :, cols:] = total.astype(BF)


def ride_ends_kernel(split, pieces, ids, keep, got, riding, proj, skip, gains, biases, units, buf):
    cols = keep.shape[2]
    total = keep[0].astype(F32) + got[0, :, :cols].astype(F32)
    proj[...] = total[:split]
    skip[...] = total[split:]
    extra = riding.shape[1]
    small = riding[...] + got[0, :, cols:].astype(F32)
    for j in range(buf.shape[1] // extra):
        buf[:12, extra * j : extra * (j + 1)] = small[12 * j : 12 * j + 12]
    gains[...] = buf[:2]
    biases[...] = buf[2:7]
    piece = buf.shape[1] // pieces
    for m in range(pieces):
        for i in range(4):
            at = (4 * m + i) * piece
            units[:, at : at + piece] = buf[7 + i : 8 + i, piece * m : piece * (m + 1)]


def add_kernel(ids, *refs):
    total = refs[0][...].astype(F32)
    for ref in refs[1:-1]:
        total += ref[...].astype(F32)
    refs[-1][...] = total.astype(refs[-1].dtype)


def project_kernel(blocks, ids, grad_q, gkv_own, gk_core, gv_core, ga_far, gkv, own, late):
    total = gkv_own[...] + jnp.concatenate([gk_core[...], gv_core[...]], 1).astype(F32)
    gkv[...] = total.astype(BF)
    whole = jnp.concatenate([grad_q[...].astype(F32), total], 1)
    size = whole.shape[1] // (2 * blocks)
    parts = [
        jnp.concatenate([whole[:, (2 * j + s) * size : (2 * j + s + 1) * size] for j in range(blocks)], 1)
        for s in range(2)
    ]
    own[...] = jnp.where(ids[0] == 0, parts[0], parts[1]).astype(BF)
    late[:, : blocks * size] = jnp.where(ids[0] == 0, parts[1], parts[0]).astype(BF)
    late[:, blocks * size :] = ga_far[...]


def result_kernel(ids, biases, grad_hidden, back_a, *refs):
    total = biases[4:5]
    for ref in refs[:-1]:
        total = total + ref[...].astype(F32)
    width = grad_hidden.shape[1]
    refs[-1][:, :width] = total.astype(BF)
    refs[-1][:, width : 2 * width] = grad_hidden[...]
    refs[-1][:, 2 * width :] = back_a[...]


def half_kernel(ids, keep_two, got_two, keep_one, got_one, own, far):
    half = own.shape[2]
    for i, (keep, got) in enumerate(((keep_two, got_two), (keep_one, got_one))):
        total = keep[0].astype(F32) + got[0].astype(F32)
        left, right = total[:, :half], total[:, half:]
        own[i] = jnp.where(ids[0] == 0, left, right)
        far[i] = jnp.where(ids[0] == 0, right, left).astype(BF)


def join_kernel(ids, own, far, two, one):
    rows = own.shape[1]
    for i in range(2):
        here, there = own[i], far[i].astype(F32)
        first, second = jnp.where(ids[0] == 0, here, there), jnp.where(ids[0] == 0, there, here)
        if i == 0:
            two[:rows] = first
            two[rows:] = second
        else:
            one[...] = jnp.concatenate([first, second], 0).T


def ends_kernel(split, ids, keep_two, got_two, proj, skip):
    total = keep_two[0].astype(F32) + got_two[0].astype(F32)
    proj[...] = total[:split]
    skip[...] = total[split:]


def third_half_kernel(ids, keep, got, own, far):
    half = own.shape[1]
    total = keep[0].astype(F32) + got[0].astype(F32)
    left, right = total[:, :half], total[:, half:]
    own[...] = jnp.where(ids[0] == 0, left, right)
    far[...] = jnp.where(ids[0] == 0, right, left).astype(BF)


def third_join_kernel(ids, own, far, out):
    here, there = own[...], far[...].astype(F32)
    first, second = jnp.where(ids[0] == 0, here, there), jnp.where(ids[0] == 0, there, here)
    out[...] = jnp.concatenate([first, second], 0).T


def home_kernel(ids, counts, back, back_b, output, grad_hidden, grad_skip):
    rows, width = output.shape
    grad_hidden[...] = back[:, width : 2 * width]
    seq = ids[0]
    spot = lax.broadcasted_iota(jnp.int32, (rows, 1), 0) + seq * rows
    live = jnp.logical_and(spot < 2 * rows - PADDED, counts[0] > 0)
    output[...] = jnp.where(live, back[:, :width].astype(F32), 0.0).astype(BF)
    a, b = back[:, 2 * width :].astype(F32), back_b[...].astype(F32)
    grad_skip[:rows] = jnp.where(seq == 0, a, b).astype(BF)
    grad_skip[rows:] = jnp.where(seq == 0, b, a).astype(BF)


def last_kernel(
    ids, grad_q, gkv, merged, grad_after, w_skip, w_qkv, gains, sums_two, sums_out, units_own, units_far,
    gm_own, gm_far, grad_hidden, back_a, back_b, small,
):
    width = merged.shape[1]
    half = width // 2
    xhat, rstd = norm(merged[...])
    gn = dot(grad_q[...], w_qkv[:, :width], (1, 1))
    gn += dot(gkv[...], w_qkv[:, width:], (1, 1))
    value = grad_after[...] + norm_back(gn, xhat, rstd, gains[0:1])
    units = units_own[0:1] + units_far[0:1]
    spot = 2 * ids[1] + ids[0]
    sums = jnp.concatenate(
        [
            jnp.sum(gn * xhat, axis=0, keepdims=True),
            sums_two[0:1],
            jnp.sum(value, axis=0, keepdims=True),
            jnp.sum(gn, axis=0, keepdims=True),
            sums_two[2:3],
            sums_two[1:2],
            sums_out[0:1],
        ]
        + [jnp.where(spot == i, units, 0.0) for i in range(4)]
        + [jnp.zeros((5, width), F32)],
        0,
    )
    small[...] = sums
    halves = value[:, :half], value[:, half:]
    rows = value.shape[0]
    gm_own[...] = jnp.where(ids[0] == 0, halves[0], halves[1]).astype(BF)
    gm_far[:rows] = jnp.where(ids[0] == 0, halves[1], halves[0]).astype(BF)
    gm_far[gm_far.shape[0] - 32 :] = jnp.concatenate([sums[:, :half], sums[:, half:]], 0).astype(BF)
    low = value.astype(BF)
    grad_hidden[...] = dot(low, w_skip[:width], (1, 1)).astype(BF)
    a = dot(low, w_skip[width : width + half], (1, 1))
    b = dot(low, w_skip[width + half :], (1, 1))
    back_a[...] = jnp.where(ids[1] == 0, a, b).astype(BF)
    back_b[...] = jnp.where(ids[1] == 0, b, a).astype(BF)


def shards(
    hidden_in,
    skip_in,
    cotangent,
    timesteps,
    counts,
    w_skip,
    w_qkv,
    w_proj,
    w_fc1,
    w_fc2,
    gains,
    biases,
    fc1_bias,
):
    rows, width = hidden_in.shape[1:]
    half = width // 2
    ff = w_fc1.shape[1]
    n_dp = lax.axis_size("dp")
    bits = n_dp.bit_length() - 1
    pairs = n_dp // 2
    place = lax.axis_index("dp")
    core = place % 2
    seq = lax.axis_index("seq")
    piece = ff // (4 * pairs)
    quarter = pairs * piece
    ids = jnp.stack([seq] + [(place >> b) & 1 for b in range(bits)]).astype(jnp.int32)
    ids = lax.optimization_barrier(ids)
    pitch = -(-rows // GAP) * GAP

    def flat(dp, s):
        return 2 * dp + s

    mirror_perm = [
        (flat(2 * k + c, s), flat(2 * k + s, c)) for k in range(pairs) for c in range(2) for s in range(2)
    ]
    turn = {(0, 0): (1, 0), (1, 0): (1, 1), (1, 1): (0, 1), (0, 1): (0, 0)}
    turn_perm = [
        (flat(2 * k + c, s), flat(2 * k + d[0], d[1])) for k in range(pairs) for (c, s), d in turn.items()
    ]
    turn_back_perm = [(b, a) for a, b in turn_perm]

    def mirror(x):
        return lax.ppermute(x, ("dp", "seq"), mirror_perm)

    def across_seq(x):
        return lax.ppermute(x, "seq", [(0, 1), (1, 0)])

    def across_bit(x, bit):
        return lax.ppermute(x, "dp", [(i, i ^ (1 << bit)) for i in range(n_dp)])

    def across_core(x):
        return across_bit(x, 0)

    def swap_if(flag, a, b, axis):
        return jnp.where(flag, jnp.concatenate([b, a], axis), jnp.concatenate([a, b], axis))

    def my_bit(bit):
        return (place >> bit) & 1

    marks = []

    def run(kernel, name, operands, outs, scratch, mib, flops, after=()):
        results = call(
            kernel,
            name,
            [(ids, IN_SMEM)] + [a if isinstance(a, tuple) else (a, IN_VMEM) for a in operands],
            outs,
            scratch,
            mib,
            flops,
            [*marks[-1:], *after],
        )
        marks.append(results[-1])
        return results[:-1]

    def tie(x, *others):
        return lax.optimization_barrier((x, *others))[0]

    def later(x):
        return lax.optimization_barrier((x, marks[-1]))[0]

    token = shape((rows, width), BF)
    token32 = shape((rows, width), F32)
    half_token = shape((rows, half), BF)
    wide_token = shape((rows, width + half), BF)
    sums = shape((8, width), F32)
    work = 2 * rows * width * width

    hidden = mirror(hidden_in[0])
    skip_a, skip_b = run(
        pack_kernel,
        "pack",
        [(skip_in[0], IN_ANY)],
        [half_token, half_token],
        [pltpu.VMEM((2 * rows, half), BF), pltpu.SemaphoreType.DMA((1,))],
        0,
        work // 100,
    )
    skip_a = mirror(skip_a)
    skip_b = lax.ppermute(skip_b, ("dp", "seq"), turn_perm)
    if piece % GAP == 0 and piece <= 2 * LANES - 7 * GAP:
        w1, b1 = run(
            gather_kernel,
            "gather",
            [(w_fc1, IN_HBM), fc1_bias.reshape(ff // LANES, LANES)],
            [shape((width, quarter), BF), shape((8, quarter), F32)],
            [pltpu.VMEM((pairs, width, 2 * LANES), BF), pltpu.SemaphoreType.DMA((pairs,))],
            GATHER_MIB,
            work // 100,
        )
    else:
        w1 = pick(pick(w_fc1.reshape(width, pairs, 2, 2, piece), core, 2), seq, 2).reshape(width, quarter)
        b1 = pick(pick(fc1_bias.reshape(pairs, 2, 2, piece), core, 1), seq, 1).reshape(1, quarter)
        b1 = jnp.broadcast_to(b1, (8, quarter))

    merged, early_a, early, q, kv = run(
        first_kernel,
        "first",
        [hidden, skip_a, skip_b, (w_skip, IN_ANY), w_qkv, gains, biases],
        [token32, wide_token, wide_token, token, shape((rows, 2 * width), BF)],
        [pltpu.VMEM(w_skip.shape, BF), pltpu.SemaphoreType.DMA((3,))],
        FIRST_MIB,
        5 * work,
    )
    kv_other = across_core(kv)
    g_home, sum_grad_out = run(
        grad_out_kernel,
        "grad_out",
        [(timesteps, IN_SMEM), (counts, IN_SMEM), (cotangent[0], IN_ANY)],
        [token, sums],
        [pltpu.VMEM((rows, width), BF), pltpu.SemaphoreType.DMA((1,))],
        0,
        work // 100,
    )
    g_far = across_seq(g_home)
    g_other = across_core(g_home)

    key_buf = pltpu.VMEM((2 * pitch, width), BF)
    proj_buf = [pltpu.VMEM((width, width), BF), pltpu.SemaphoreType.DMA((1,))]
    early_b, after_attn, normed_two, log_total = run(
        attend_kernel,
        "attend",
        [q, kv, kv_other, merged, early, (w_proj, IN_ANY), gains, biases],
        [shape((rows, 2 * width + half), BF), token32, token, shape((rows, LANES), F32)],
        [key_buf, key_buf, *proj_buf],
        0,
        2 * work,
    )

    n_far = across_seq(normed_two)
    n_other = across_core(normed_two)
    g_other_far = across_core(later(g_far))

    def mlp(name, n0, n1, *g, w2):
        tall = shape((2 * pitch, quarter), BF)
        wide = shape((2 * pitch, width), BF)
        loads = w2 is None
        return run(
            mlp_first_kernel if loads else mlp_kernel,
            name,
            [n0, n1, *g, w1, b1, (w_fc2.reshape(4 * pairs, piece, width), IN_HBM) if loads else w2],
            [tall, tall, wide, wide, token32, token, shape((8, quarter), F32)] + [shape((quarter, width), BF)] * loads,
            [pltpu.VMEM((2 * pitch, 3 * LANES), F32), pltpu.VMEM((2 * pitch, 3 * LANES), F32)]
            + [pltpu.SemaphoreType.DMA((pairs,))] * loads,
            0,
            6 * 2 * rows * width * quarter,
        )

    w2 = None
    if piece % GAP:
        w2 = pick(pick(w_fc2.reshape(pairs, 2, 2, piece, width), core, 1), seq, 1).reshape(quarter, width)
    act_own, gi_own, nn_own, gg_own, gn_own, gn_own_core, si_own, *loaded = mlp(
        "mlp_own", normed_two, n_other, g_home, g_other_far, g_far, g_other, w2=w2
    )
    w2 = loaded[0] if loaded else w2
    n_other_far = across_core(later(n_far))
    early_a_far = across_seq(tie(early_a, n_far))
    act_far, gi_far, nn_far, gg_far, gn_far, gn_far_core, si_far = mlp(
        "mlp_far", n_far, n_other_far, g_other, g_far, g_other_far, g_home, w2=w2
    )
    gn_far_core = across_core(gn_far_core)
    gn_own_core = across_core(gn_own_core)

    def outer(name, products, blocks, bit, shift, riding=None):
        pieces = PIECES if shift == 0 and n_dp // 2 % PIECES == 0 else 1
        lefts = [sum(n for _, _, n in parts[0][0]) for _, parts in products]
        rows_of = [n // blocks for n in lefts]
        inside = all(r % 4 == 0 for r in rows_of)
        cols = products[0][0]
        stride = (1 << (bit - shift)) if inside else 0
        scratch, operands = [], []
        for n, (c, parts) in zip(lefts, products):
            height = -(-parts[0][0][0][0].shape[0] // GAP) * GAP * len(parts)
            scratch += [pltpu.VMEM((n, c), F32), pltpu.VMEM((height, n), BF), pltpu.VMEM((height, c), BF)]
            for left, (right, _) in parts:
                operands += [x for x, _, _ in left] + [right]
        r = sum(rows_of)
        if inside:
            outs = [shape((blocks // 2, r, cols), BF)] + [shape((blocks // 2 // pieces, r, cols), BF)] * pieces
        else:
            outs = [shape((n, cols), BF) for n in lefts]
        layout = [[([span for _, *span in left], right[1]) for left, right in parts] for _, parts in products]
        if riding is not None:
            outs = [outs[0], *[shape((blocks // 2 // pieces, r, cols + extra), BF)] * pieces, shape((r, extra), F32)]
            operands.append(riding)
        results = run(
            functools.partial(outer_kernel if riding is None else ride_outer_kernel, stride, bit, layout, pieces),
            name,
            operands,
            outs,
            scratch,
            0,
            sum(2 * n * cols * 4 * rows for n in lefts),
        )
        if inside:
            return results[0], results[1 : 1 + pieces], results[1 + pieces :]
        whole = jnp.concatenate([x.reshape(blocks, r, cols) for x, r in zip(results, rows_of)], 1)
        whole = whole.reshape(blocks >> (bit - shift + 1), 2, 1 << (bit - shift), sum(rows_of), cols)
        flat_shape = (blocks // 2, sum(rows_of), cols)
        keep, send = [pick(whole, i, 1).reshape(flat_shape) for i in (my_bit(bit), 1 - my_bit(bit))]
        return keep, [send], []

    def combine(name, keep, gots, left, bit, riding=(), after=()):
        count, r, cols = keep.shape
        stride = 1 << left.index(bit)
        if r % 4 == 0:
            results = run(
                functools.partial(ride_combine_kernel if riding else combine_kernel, stride, bit),
                name,
                [keep, *riding, *gots],
                [shape((count // 2, r, cols), BF), shape((count // 2, r, gots[0].shape[2]), BF)]
                + [shape(x.shape, F32) for x in riding],
                [],
                0,
                work // 100,
                after,
            )
            return results[0], [results[1]], results[2:]
        both = (keep.astype(F32) + gots[0].astype(F32)).astype(BF).reshape(count // (2 * stride), 2, stride, r, cols)
        keep, send = [pick(both, i, 1).reshape(count // 2, r, cols) for i in (my_bit(bit), 1 - my_bit(bit))]
        return keep, [send], []

    class Chain:
        def __init__(self, name, order, parts):
            self.name, self.order = name, order
            self.keep, sends, self.riding = parts
            self.step = 0
            self.left = sorted(order[1:])
            self.got = [across_bit(send, order[0]) for send in sends]

        def advance(self, *after):
            self.step += 1
            if self.step >= len(self.order):
                return
            bit = self.order[self.step]
            self.keep, sends, self.riding = combine(
                f"{self.name}_{self.step}", self.keep, self.got, self.left, bit, self.riding, after
            )
            self.left.remove(bit)
            self.got = [across_bit(send, bit) for send in sends]

    def order_of(first):
        return first + list(range(4, bits))

    def add(name, out, *terms):
        return run(add_kernel, name, list(terms), [out], [], 0, work // 100)[0]

    fc2 = Chain(
        "fc2",
        order_of([1, 2, 3]),
        outer("outer_fc2", [(width, [([(act_own, 0, quarter)], (gg_own, 0)), ([(act_far, 0, quarter)], (gg_far, 0))])], pairs, 1, 1),
    )
    gn_far = across_seq(add("gn_add", token, gn_far, gn_far_core))
    fc1 = Chain(
        "fc1",
        order_of([2, 1, 3]),
        outer("outer_fc1", [(width, [([(gi_own, 0, quarter)], (nn_own, 0)), ([(gi_far, 0, quarter)], (nn_far, 0))])], pairs, 2, 1),
    )

    split = width // n_dp
    extra = -half % LANES
    rides = 3 * split % 8 == 0 and extra and 3 * split * extra == 12 * width
    early_b_far = across_seq(tie(early_b, gn_far))
    grad_after, ga_own, ga_far, grad_q, gkv_own, gk_other, gv_other, sums_two = run(
        attend_back_kernel,
        "attend_back",
        [gn_own, gn_own_core, gn_far, g_home, g_other_far, after_attn, q, kv, kv_other, log_total]
        + [(w_proj, IN_ANY), gains],
        [token32, half_token, half_token, token]
        + [shape((rows, 2 * width), F32), token, token, sums],
        [key_buf, key_buf, proj_buf[0], pltpu.VMEM((2 * pitch, width), F32), pltpu.VMEM((2 * pitch, width), F32), proj_buf[1]],
        0,
        3 * work,
        (early_a_far,),
    )
    gk_core, gv_core = across_core(gk_other), across_core(gv_other)
    even = 3 * split % 8 == 0
    if even:
        gkv, project_own, late = run(
            functools.partial(project_kernel, n_dp),
            "project",
            [grad_q, gkv_own, gk_core, gv_core, ga_far],
            [shape((rows, 2 * width), BF), wide_token, shape((rows, 2 * width), BF)],
            [],
            0,
            work // 100,
        )
        third_cols, normed, normed_far = width, early_b, early_b_far
    else:
        gkv = (gkv_own + jnp.concatenate([gk_core, gv_core], 1).astype(F32)).astype(BF)
        project_own = jnp.concatenate([grad_q, gkv], 1)
        late = jnp.concatenate([project_own, ga_far], 1)
        third_cols = half
        normed, normed_far = [lax.dynamic_slice_in_dim(x, seq * half, half, 1) for x in (early_b, early_b_far)]
    third_wide = project_own.shape[1]
    late_far = across_seq(late)
    gm_own, gm_far, grad_hidden, back_a, back_b, small = run(
        last_kernel,
        "last",
        [grad_q, gkv, merged, grad_after, w_skip, w_qkv, gains, sums_two, sum_grad_out, si_own, si_far],
        [half_token, shape((pitch + 32, half), BF), token, half_token, half_token, shape((16, width), F32)],
        [],
        0,
        5 * work,
        (early_b_far,),
    )
    gm_far = across_seq(gm_far)

    fc2.advance()
    out_own, out_far, out_own_core, out_far_core = run(
        lambda ids, *refs: mlp_out_kernel(*refs),
        "mlp_out",
        [act_own, act_far, w2],
        [token32, token32, token, token],
        [],
        0,
        2 * 4 * rows * width * quarter,
    )
    out_own_core, out_far_core = across_core(out_own_core), across_core(out_far_core)
    fc1.advance()
    third = Chain(
        "third",
        order_of([0, 2, 1, 3]),
        outer(
            "outer_third",
            [
                (
                    third_cols,
                    [
                        ([(project_own, 0, third_wide)], (normed, 0)),
                        ([(late_far, 0, third_wide)], (normed_far, 0)),
                    ],
                )
            ],
            n_dp,
            0,
            0,
        ),
    )
    second = Chain(
        "second",
        order_of([0, 1, 2, 3]),
        outer(
            "outer_second",
            [
                (half, [([(early_b, width, width)], (ga_own, 0)), ([(early_b_far, width, width)], (late_far, third_wide))]),
                (
                    half,
                    [
                        ([(early_a, 0, width + half), (early_b, 2 * width, half)], (gm_own, 0)),
                        ([(early_a_far, 0, width + half), (early_b_far, 2 * width, half)], (gm_far, 0)),
                    ],
                ),
            ],
            n_dp,
            0,
            0,
            small if rides else None,
        ),
    )
    third.advance()
    second.advance()
    fc2.advance()
    fc1.advance()
    out_far = across_seq(add("out_add", token, out_far, out_far_core))
    back = run(
        result_kernel,
        "result",
        [biases, grad_hidden, back_a, after_attn, out_own, out_own_core, out_far],
        [shape((rows, 2 * width + half), BF)],
        [],
        0,
        work // 100,
    )[0]
    back = mirror(back)
    back_b = lax.ppermute(later(back_b), ("dp", "seq"), turn_back_perm)
    if not rides:
        small = small[:12]
        small = small + across_seq(small)
        for bit in range(bits):
            small = small + across_bit(small, bit)
    while fc2.step + 1 < len(fc2.order):
        fc2.advance()
        fc1.advance()
    own, far = run(
        half_kernel,
        "half",
        [fc2.keep, *fc2.got, fc1.keep, *fc1.got],
        [shape((2, piece, half), F32), shape((2, piece, half), BF)],
        [],
        0,
        work // 100,
    )
    far = across_seq(far)
    third.advance()
    second.advance()
    output, grad_hidden, grad_skip = run(
        home_kernel,
        "home",
        [(counts, IN_SMEM), back, back_b],
        [token, token, shape((2 * rows, half), BF)],
        [],
        0,
        work // 100,
    )
    while third.step + 1 < len(third.order):
        third.advance()
        second.advance()
    out_w_fc2, out_w_fc1 = run(
        join_kernel,
        "join",
        [own, far],
        [shape((2 * piece, half), F32), shape((half, 2 * piece), F32)],
        [],
        0,
        work // 100,
    )
    if even:
        third_rows = 3 * split // 2
        third_own, third_far = run(
            third_half_kernel,
            "third_half",
            [third.keep, *third.got],
            [shape((third_rows, half), F32), shape((third_rows, half), BF)],
            [],
            0,
            work // 100,
        )
        third_far = across_seq(third_far)
    ends = [shape((split, half), F32), shape((2 * split, half), F32)]
    if rides:
        out_w_proj, out_w_skip, grad_gains, grad_biases, grad_fc1_bias = run(
            functools.partial(ride_ends_kernel, split, pairs),
            "ends",
            [second.keep, *second.got, *second.riding],
            ends + [shape((2, width), F32), shape((5, width), F32), shape((1, ff), F32)],
            [pltpu.VMEM((16, width), F32)],
            0,
            work // 100,
        )
        grad_fc1_bias = grad_fc1_bias.reshape(ff)
    else:
        out_w_proj, out_w_skip = run(
            functools.partial(ends_kernel, split), "ends", [second.keep, *second.got], ends, [], 0, work // 100
        )
        grad_gains, grad_biases = small[:2], small[2:7]
        grad_fc1_bias = small[7:11].reshape(2, 2, pairs, piece).transpose(2, 0, 1, 3).reshape(ff)
    if even:
        (out_w_qkv,) = run(
            third_join_kernel,
            "third_join",
            [third_own, third_far],
            [shape((half, 2 * third_rows), F32)],
            [],
            0,
            work // 100,
        )
    else:
        out_w_qkv = (third.keep[0].astype(F32) + third.got[0][0].astype(F32)).T
    return (
        output[None],
        grad_hidden[None],
        grad_skip[None],
        out_w_skip,
        out_w_qkv,
        out_w_proj,
        out_w_fc1,
        out_w_fc2,
        grad_gains,
        grad_biases,
        grad_fc1_bias,
    )


def solution(mesh):
    return jax.shard_map(
        shards,
        mesh=mesh,
        in_specs=(
            P("dp", "seq", None),
            P("dp", None, "seq"),
            P("dp", "seq", None),
            P("dp"),
            P("dp"),
            P(),
            P(),
            P(),
            P(),
            P(),
            P(),
            P(),
            P(),
        ),
        out_specs=(
            P("dp", "seq", None),
            P("dp", "seq", None),
            P("dp", None, "seq"),
            P("dp", "seq"),
            P("seq", "dp"),
            P("dp", "seq"),
            P("seq", "dp"),
            P("dp", "seq"),
            P(),
            P(),
            P(),
        ),
        check_vma=False,
    )
```

```python
import functools

import jax
import jax.numpy as jnp
from jax import lax
from jax.experimental import pallas as pl
from jax.experimental.pallas import tpu as pltpu
from jax.sharding import PartitionSpec as P

HEADS = 16
PADDED = 2
TSTEPS = 1000

EPSILON = 1e-06
NEG_FILL = -1e30
BF = jnp.bfloat16
F32 = jnp.float32
MIB = 1 << 20
LANES = 128
GAP = 16


def dot(left, right, dims):
    return lax.dot_general(left, right, ((dims[:1], dims[1:]), ((), ())), preferred_element_type=F32)


def norm(value):
    center = value - jnp.mean(value, axis=-1, keepdims=True)
    rstd = lax.rsqrt(jnp.mean(center * center, axis=-1, keepdims=True) + EPSILON)
    return center * rstd, rstd


def norm_back(grad, xhat, rstd, gain):
    scaled = grad * gain
    return rstd * (
        scaled
        - jnp.mean(scaled, axis=-1, keepdims=True)
        - xhat * jnp.mean(scaled * xhat, axis=-1, keepdims=True)
    )


def pick(array, index, axis):
    return lax.dynamic_index_in_dim(array, index, axis, keepdims=False)


def shape(dims, dtype):
    return jax.ShapeDtypeStruct(dims, dtype)


def padded(dims, dtype):
    dims = (1,) * (2 - len(dims)) + tuple(dims)
    size = -(-dims[-2] // 16) * 16 * -(-dims[-1] // LANES) * LANES
    for dim in dims[:-2]:
        size *= dim
    return size * jnp.dtype(dtype).itemsize


COMPUTE = ("gather",)
PIECES = 4
UNROLL = True
GATHER_MIB = 34
SCALE = 0.3
TAKES = {
    "pack": 12.0,
    "gather": 8.0,
    "first": 4.4,
    "attend": 6.6,
    "mlp": 6.0,
    "outer": 3.2,
    "attend_back": 10.3,
    "last": 6.3,
    "outer_second": 0.3,
    "outer_third": 0.3,
    "third": 0.3,
    "second": 0.3,
    "fc1": 0.3,
    "fc2": 0.3,
}


IN_VMEM = pl.BlockSpec(memory_space=pltpu.VMEM)
IN_SMEM = pl.BlockSpec(memory_space=pltpu.SMEM)
IN_ANY = pl.BlockSpec(memory_space=pl.ANY)
IN_HBM = pl.BlockSpec(memory_space=pltpu.HBM)


def call(kernel, name, operands, outs, scratch, mib, flops, after=()):
    takes = TAKES.get(name, TAKES.get(name.split("_")[0], 1.0)) * SCALE
    outs = [*outs, shape((8, LANES), F32)]
    inputs = len(operands)
    marks = len(after)
    if not mib:
        need = sum(padded(a.shape, a.dtype) for a, spec in operands if spec is IN_VMEM)
        need += sum(padded(o.shape, o.dtype) for o in outs)
        need += sum(padded(b.shape, b.dtype) for b in scratch if b.memory_space == pltpu.VMEM)
        mib = need * 9 // 8 // MIB + 4

    def body(*refs):
        mark = refs[inputs + marks + len(outs) - 1]
        mark[...] = jnp.zeros_like(mark)
        kernel(*refs[:inputs], *refs[inputs + marks : inputs + marks + len(outs) - 1], *refs[inputs + marks + len(outs) :])

    return pl.pallas_call(
        body,
        out_shape=outs,
        in_specs=[spec for _, spec in operands] + [IN_ANY] * marks,
        out_specs=[IN_VMEM] * len(outs),
        scratch_shapes=scratch,
        compiler_params=pltpu.CompilerParams(vmem_limit_bytes=mib * MIB),
        cost_estimate=pl.CostEstimate(flops=int(takes * 1e9), bytes_accessed=1 if name in COMPUTE else int(takes * 3.6e6), transcendentals=0),
        name=name,
    )(*[a for a, _ in operands], *after)


def fetch(pairs, sems):
    copies = [pltpu.make_async_copy(src, dst, sems.at[i]) for i, (src, dst) in enumerate(pairs)]
    for copy in copies:
        copy.start()
    return copies


def gather_kernel(pieces, ids, w_fc1, w_fc2, bias, w1, w2, b1, sems):
    core, seq = ids[1], ids[0]
    piece_size = w1.shape[1] // pieces
    which = [4 * m + 2 * core + seq for m in range(pieces)]
    spots = [w * piece_size for w in which]
    copies = fetch([(w_fc2.at[w], w2.at[m]) for m, w in enumerate(which)], sems)
    lane = lax.broadcasted_iota(jnp.int32, (8, LANES), 1)
    for m in range(pieces):
        base, into = m * piece_size // LANES * LANES, m * piece_size % LANES
        window = [bias[pl.ds(spots[m] // LANES + i, 1), :] for i in range(2)]
        window = jnp.concatenate([jnp.broadcast_to(x, (8, LANES)) for x in window], 1)
        turn = (into - spots[m] % LANES + 2 * LANES) % (2 * LANES)
        window = pltpu.roll(window, turn, 1)
        left = window[:, :LANES]
        if into:
            left = jnp.where(lane >= into, left, b1[:, base : base + LANES])
        b1[:, base : base + LANES] = left
        b1[:, base + LANES : base + 2 * LANES] = window[:, LANES:]
    source = lax.broadcasted_iota(jnp.int32, (2 * LANES, 2 * LANES), 0)
    target = lax.broadcasted_iota(jnp.int32, (2 * LANES, 2 * LANES), 1)
    before = {}
    for m in range(pieces):
        base = m * piece_size // LANES * LANES
        column = target + (base - m * piece_size)
        take = jnp.logical_and(column >= 0, column < piece_size)
        take = jnp.logical_and(take, source == column + spots[m] % LANES)
        window = pl.ds(pl.multiple_of(spots[m] // LANES * LANES, LANES), 2 * LANES)
        part = dot(w_fc1[:, window], take.astype(F32).astype(BF), (1, 0))
        for at, half in ((base, part[:, :LANES]), (base + LANES, part[:, LANES:])):
            before[at] = before[at] + half if at in before else half
        for at in [x for x in before if x <= base]:
            w1[:, at : at + LANES] = before.pop(at).astype(BF)
    for at, half in before.items():
        w1[:, at : at + LANES] = half.astype(BF)
    for copy in copies:
        copy.wait()


def pack_kernel(ids, skip_in, skip_a, skip_b, skip, sems):
    rows = skip_a.shape[0]
    seq = ids[0]
    fetch([(skip_in, skip)], sems)[0].wait()
    whole = skip[...].astype(F32)
    top, bottom = whole[:rows], whole[rows:]
    skip_a[...] = jnp.where(seq == 0, top, bottom).astype(BF)
    skip_b[...] = jnp.where(seq == 0, bottom, top).astype(BF)


def grad_out_kernel(ids, timesteps, counts, cotangent, g_home, sums):
    rows, width = g_home.shape
    time = jnp.zeros((1, 1), F32) + timesteps[0].astype(F32)
    weight = jax.nn.sigmoid(12.0 * time / TSTEPS - 6.0)
    spot = lax.broadcasted_iota(jnp.int32, (rows, 1), 0) + ids[0] * rows
    live = jnp.logical_and(spot < 2 * rows - PADDED, counts[0] > 0)
    g = cotangent[...].astype(F32) * jnp.where(live, weight, 0.0)
    g_home[...] = g.astype(BF)
    sums[...] = jnp.concatenate([jnp.sum(g, axis=0, keepdims=True), jnp.zeros((7, width), F32)], 0)


def first_kernel(ids, hidden, skip_a, skip_b, w_skip, w_qkv, gains, biases, merged, early_a, early, q, kv):
    width = hidden.shape[1]
    half = width // 2
    core = ids[1]
    a, b = skip_a[...].astype(F32), skip_b[...].astype(F32)
    low = jnp.where(core == 0, a, b).astype(BF)
    high = jnp.where(core == 0, b, a).astype(BF)
    early_a[:, :width] = hidden[...]
    early_a[:, width:] = low
    early[:, width:] = high
    total = dot(hidden[...], w_skip[:width], (1, 0)) + biases[0:1]
    total += dot(low, w_skip[width : width + half], (1, 0))
    total += dot(high, w_skip[width + half :], (1, 0))
    merged[...] = total
    xhat, _ = norm(total)
    one = (xhat * gains[0:1] + biases[1:2]).astype(BF)
    early[:, :width] = one
    kv[...] = dot(one, w_qkv[:, width:], (1, 0)).astype(BF)
    q[...] = dot(one, w_qkv[:, :width], (1, 0)).astype(BF)


def head_windows(width):
    size = width // HEADS
    spans = []
    for h in range(HEADS):
        low, high = h * size, (h + 1) * size
        t0, t1 = low // LANES, (high - 1) // LANES + 1
        spans.append((h, low, high, t0 * LANES, t1 * LANES))
    return spans


def lane_mask(low, high, first, last):
    lane = lax.broadcasted_iota(jnp.int32, (1, last - first), 1) + first
    return jnp.logical_and(lane >= low, lane < high)


def key_mask(core, rows, pitch):
    spot = lax.broadcasted_iota(jnp.int32, (1, 2 * pitch), 1)
    other = spot >= pitch
    here = jnp.where(other, spot - pitch, spot)
    last_half = jnp.where(other, 1 - core, core) == 1
    limit = jnp.where(last_half, rows - PADDED, rows)
    return here < limit


def lay_keys(keys, values, kv_own, kv_other, rows, pitch, width):
    for buf, at in ((keys, 0), (values, width)):
        buf[...] = jnp.zeros_like(buf)
        buf[0:rows] = kv_own[:, at : at + width]
        buf[pitch : pitch + rows] = kv_other[:, at : at + width]


def attend_kernel(ids, q, kv_own, kv_other, merged, early, w_proj, gains, biases, early_b, after, normed, log_total, keys, values, wp, sems):
    rows, width = q.shape
    pitch = keys.shape[0] // 2
    copies = fetch([(w_proj, wp)], sems)
    lay_keys(keys, values, kv_own, kv_other, rows, pitch, width)
    valid = key_mask(ids[1], rows, pitch)
    scale = (width // HEADS) ** (-0.5)
    lane = lax.broadcasted_iota(jnp.int32, (rows, LANES), 1)
    tiles = [jnp.zeros((rows, LANES), F32) for _ in range(width // LANES)]
    logs = jnp.zeros((rows, LANES), F32)
    for h, low, high, first, last in head_windows(width):
        mask = lane_mask(low, high, first, last)
        mine = q[:, first:last] * mask.astype(F32).astype(BF)
        scores = jnp.where(valid, dot(mine, keys[:, first:last], (1, 1)) * scale, NEG_FILL)
        top = jnp.max(scores, axis=-1, keepdims=True)
        expo = jnp.exp(scores - top)
        total = jnp.sum(expo, axis=-1, keepdims=True)
        probs = (expo * (1.0 / total)).astype(BF)
        logs = jnp.where(lane == h, top + jnp.log(total), logs)
        part = dot(probs, values[:, first:last], (1, 0))
        for t in range(first, last, LANES):
            tiles[t // LANES] = jnp.where(
                mask[:, t - first : t - first + LANES], part[:, t - first : t - first + LANES], tiles[t // LANES]
            )
    log_total[...] = logs
    for t, tile in enumerate(tiles):
        early_b[:, width + t * LANES : width + (t + 1) * LANES] = tile.astype(BF)
    copies[0].wait()
    early_b[:, :width] = early[:, :width]
    early_b[:, 2 * width :] = early[:, width:]
    value = merged[...] + dot(early_b[:, width : 2 * width], wp[...], (1, 0)) + biases[2:3]
    after[...] = value
    xhat, _ = norm(value)
    normed[...] = (xhat * gains[1:2] + biases[3:4]).astype(BF)


def attend_back_kernel(
    ids, gn_mine, gn_core, gn_far, g_home, g_cross, after, q, kv_own, kv_other, log_total, w_proj, gains,
    grad_after, ga_own, ga_far, grad_q, gkv_own, gk_other, gv_other, sums,
    keys, values, wp, gk, gv, sems,
):
    rows, width = q.shape
    half = width // 2
    pitch = keys.shape[0] // 2
    copies = fetch([(w_proj, wp)], sems)
    gn = gn_mine[...] + gn_core[...].astype(F32) + gn_far[...].astype(F32)
    xhat, rstd = norm(after[...])
    g_out = jnp.where(ids[0] == ids[1], g_home[...].astype(F32), g_cross[...].astype(F32))
    value = g_out + norm_back(gn, xhat, rstd, gains[1:2])
    grad_after[...] = value
    low = value.astype(BF)
    halves = value[:, :half], value[:, half:]
    ga_own[...] = jnp.where(ids[0] == 0, halves[0], halves[1]).astype(BF)
    ga_far[...] = jnp.where(ids[0] == 0, halves[1], halves[0]).astype(BF)
    sums[...] = jnp.concatenate(
        [
            jnp.sum(gn * xhat, axis=0, keepdims=True),
            jnp.sum(gn, axis=0, keepdims=True),
            jnp.sum(value, axis=0, keepdims=True),
            jnp.zeros((5, width), F32),
        ],
        0,
    )
    lay_keys(keys, values, kv_own, kv_other, rows, pitch, width)
    valid = key_mask(ids[1], rows, pitch)
    scale = (width // HEADS) ** (-0.5)
    copies[0].wait()
    grad_mixed = dot(low, wp[...], (1, 1)).astype(BF)
    gk[...] = jnp.zeros_like(gk)
    gv[...] = jnp.zeros_like(gv)
    lane = lax.broadcasted_iota(jnp.int32, (rows, LANES), 1)
    tiles = [jnp.zeros((rows, LANES), F32) for _ in range(width // LANES)]
    logs = log_total[...]
    for h, start, stop, first, last in head_windows(width):
        mask = lane_mask(start, stop, first, last)
        low_mask = mask.astype(F32).astype(BF)
        mine = q[:, first:last] * low_mask
        gm = grad_mixed[:, first:last] * low_mask
        log = jnp.sum(jnp.where(lane == h, logs, 0.0), axis=-1, keepdims=True)
        scores = jnp.where(valid, dot(mine, keys[:, first:last], (1, 1)) * scale, NEG_FILL)
        probs = jnp.exp(scores - log)
        gp = dot(gm, values[:, first:last], (1, 1))
        gs = (probs * (gp - jnp.sum(gp * probs, axis=-1, keepdims=True))).astype(BF)
        part = dot(gs, keys[:, first:last], (1, 0))
        for t in range(first, last, LANES):
            tiles[t // LANES] = jnp.where(
                mask[:, t - first : t - first + LANES], part[:, t - first : t - first + LANES], tiles[t // LANES]
            )
        gk[:, first:last] += dot(gs, mine, (0, 0))
        gv[:, first:last] += dot(probs.astype(BF), gm, (0, 0))
    for t, tile in enumerate(tiles):
        grad_q[:, t * LANES : (t + 1) * LANES] = (tile * scale).astype(BF)
    gkv_own[:, :width] = gk[0:rows] * scale
    gkv_own[:, width:] = gv[0:rows]
    gk_other[...] = (gk[pitch : pitch + rows] * scale).astype(BF)
    gv_other[...] = gv[pitch : pitch + rows].astype(BF)


def lay_rows(buf, blocks):
    rows = blocks[0].shape[0]
    pitch = buf.shape[0] // len(blocks)
    if pitch > rows:
        buf[...] = jnp.zeros_like(buf)
    for i, block in enumerate(blocks):
        buf[i * pitch : i * pitch + rows] = block[...]


def lay_chosen(buf, flag, pairs):
    rows = pairs[0][0].shape[0]
    pitch = buf.shape[0] // len(pairs)
    buf[...] = jnp.zeros_like(buf)
    for way, chosen in enumerate((flag, jnp.logical_not(flag))):

        @pl.when(chosen)
        def _(way=way):
            for i, pair in enumerate(pairs):
                buf[i * pitch : i * pitch + rows] = pair[way][...]


def mlp_kernel(ids, n0, n1, g0a, g0b, g1a, g1b, w1, b1, w2, activ, grad_inner, n_all, g_all, gn_mine, gn_other, sums, inner_v, grad_v):
    rows, width = n0.shape
    units = w1.shape[1]
    lay_rows(n_all, (n0, n1))
    lay_chosen(g_all, ids[0] == ids[1], ((g0a, g0b), (g1a, g1b)))
    height = n_all.shape[0]
    pitch = height // 2
    step = 3 * LANES
    chunk = 48
    root = 0.5**0.5
    bell = (0.5 / jnp.pi) ** 0.5
    for j in range(units // step):
        cols = slice(j * step, (j + 1) * step)
        inner_v[...] = dot(n_all[...], w1[:, cols], (1, 0))
        grad_v[...] = dot(g_all[...], w2[cols, :], (1, 1))
        bias = b1[0:1, cols]

        def body(i, total):
            at = pl.ds(pl.multiple_of(i * chunk, chunk), chunk)
            x = inner_v[at] + bias
            cdf = 0.5 + 0.5 * lax.erf(x * root)
            activ[at, cols] = (x * cdf).astype(BF)
            g = grad_v[at] * (cdf + x * jnp.exp(-0.5 * x * x) * bell)
            grad_inner[at, cols] = g.astype(BF)
            return total + jnp.sum(g, axis=0, keepdims=True)

        sums[0:1, cols] = lax.fori_loop(0, height // chunk, body, jnp.zeros((1, step), F32), unroll=UNROLL)
    for j in range(width // step):
        cols = slice(j * step, (j + 1) * step)
        part = dot(grad_inner[...], w1[cols, :], (1, 1))
        gn_mine[:, cols] = part[:rows]
        gn_other[:, cols] = part[pitch : pitch + rows].astype(BF)


def mlp_out_kernel(activ_own, activ_far, w2, own, far, own_core, far_core):
    rows = own.shape[0]
    pitch = activ_own.shape[0] // 2
    step = 3 * LANES
    for activ, mine, other in ((activ_far, far, far_core), (activ_own, own, own_core)):
        for j in range(w2.shape[1] // step):
            cols = slice(j * step, (j + 1) * step)
            part = dot(activ[...], w2[:, cols], (1, 0))
            mine[:, cols] = part[:rows]
            other[:, cols] = part[pitch : pitch + rows].astype(BF)


def split_blocks(total, keep, sends, at, mine, stride):
    count = keep.shape[0]
    rows = total.shape[0] // (2 * count)
    slot = 0
    for i in range(2 * count):
        if i // stride % 2:
            continue
        a = total[i * rows : (i + 1) * rows]
        b = total[(i + stride) * rows : (i + stride + 1) * rows]
        keep[slot, at : at + rows] = jnp.where(mine == 0, a, b).astype(BF)
        per = sends[0].shape[0]
        sends[slot // per][slot % per, at : at + rows, : keep.shape[2]] = jnp.where(mine == 0, b, a).astype(BF)
        slot += 1


def outer_kernel(stride, bit, layout, pieces, ids, *refs):
    spots = iter(refs)
    operands = [
        [([(next(spots), *span) for span in left], (next(spots), right)) for left, right in parts] for parts in layout
    ]
    outs = [next(spots) for _ in range(1 + pieces if stride else len(layout))]
    at = 0
    for i, parts in enumerate(operands):
        total, left, right = next(spots), next(spots), next(spots)
        pitch = left.shape[0] // len(parts)
        cols = right.shape[1]
        for p, (lefts, (y, first)) in enumerate(parts):
            rows = lefts[0][0].shape[0]
            if pitch > rows:
                left[p * pitch : (p + 1) * pitch] = jnp.zeros((pitch, left.shape[1]), BF)
                right[p * pitch : (p + 1) * pitch] = jnp.zeros((pitch, cols), BF)
            right[p * pitch : p * pitch + rows] = y[:rows, first : first + cols]
            spot = 0
            for x, start, n in lefts:
                left[p * pitch : p * pitch + rows, spot : spot + n] = x[:, start : start + n]
                spot += n
        step = 3 * LANES
        for j in range(0, left.shape[1], step):
            span = slice(j, min(j + step, left.shape[1]))
            total[span, :] = dot(left[:, span], right[...], (0, 0))
        if stride:
            split_blocks(total, outs[0], outs[1:], at, ids[1 + bit], stride)
            at += left.shape[1] // (2 * outs[0].shape[0])
        else:
            outs[i][...] = total[...].astype(BF)


def combine_kernel(stride, bit, ids, keep, *refs):
    gots, kept, send = refs[:-2], refs[-2], refs[-1]
    slot = 0
    cols = keep.shape[2]
    per = gots[0].shape[0]

    def total(i):
        return keep[i].astype(F32) + gots[i // per][i % per, :, :cols].astype(F32)

    for i in range(keep.shape[0]):
        if i // stride % 2:
            continue
        a, b = total(i), total(i + stride)
        kept[slot] = jnp.where(ids[1 + bit] == 0, a, b).astype(BF)
        send[slot, :, :cols] = jnp.where(ids[1 + bit] == 0, b, a).astype(BF)
        slot += 1


def ride_outer_kernel(stride, bit, layout, pieces, ids, *refs):
    inputs = sum(len(left) + 1 for parts in layout for left, _ in parts)
    operands, small, outs, scratch = refs[:inputs], refs[inputs], refs[inputs + 1 : inputs + 3 + pieces], refs[inputs + 3 + pieces :]
    keep, sends, riding = outs[0], outs[1:-1], outs[-1]
    outer_kernel(stride, bit, layout, pieces, ids, *operands, keep, *sends, *scratch)
    far = operands[-1]
    total = small[...] + far[far.shape[0] - 16 :, :].astype(F32)
    cols = keep.shape[2]
    extra = sends[0].shape[2] - cols
    for j in range(small.shape[1] // extra):
        riding[12 * j : 12 * j + 12, :] = total[:12, extra * j : extra * (j + 1)]
    for send in sends:
        send[:, :, cols:] = jnp.zeros((send.shape[0], send.shape[1], extra), BF)
    sends[0][0, :, cols:] = riding[...].astype(BF)


def ride_combine_kernel(stride, bit, ids, keep, riding, *refs):
    gots, (kept, send, rode) = refs[:-3], refs[-3:]
    combine_kernel(stride, bit, ids, keep, *gots, kept, send)
    cols = keep.shape[2]
    total = riding[...] + gots[0][0, :, cols:].astype(F32)
    rode[...] = total
    if send.shape[0] > 1:
        send[1:, :, cols:] = jnp.zeros((send.shape[0] - 1, send.shape[1], send.shape[2] - cols), BF)
    send[0, :, cols:] = total.astype(BF)


def ride_ends_kernel(split, pieces, ids, keep, got, riding, proj, skip, gains, biases, units, buf):
    cols = keep.shape[2]
    total = keep[0].astype(F32) + got[0, :, :cols].astype(F32)
    proj[...] = total[:split]
    skip[...] = total[split:]
    extra = riding.shape[1]
    small = riding[...] + got[0, :, cols:].astype(F32)
    for j in range(buf.shape[1] // extra):
        buf[:12, extra * j : extra * (j + 1)] = small[12 * j : 12 * j + 12]
    gains[...] = buf[:2]
    biases[...] = buf[2:7]
    piece = buf.shape[1] // pieces
    for m in range(pieces):
        for i in range(4):
            at = (4 * m + i) * piece
            units[:, at : at + piece] = buf[7 + i : 8 + i, piece * m : piece * (m + 1)]


def add_kernel(ids, *refs):
    total = refs[0][...].astype(F32)
    for ref in refs[1:-1]:
        total += ref[...].astype(F32)
    refs[-1][...] = total.astype(refs[-1].dtype)


def project_kernel(blocks, ids, grad_q, gkv_own, gk_core, gv_core, gkv, own, late):
    total = gkv_own[...] + jnp.concatenate([gk_core[...], gv_core[...]], 1).astype(F32)
    gkv[...] = total.astype(BF)
    whole = jnp.concatenate([grad_q[...].astype(F32), total], 1)
    size = whole.shape[1] // (2 * blocks)
    parts = [
        jnp.concatenate([whole[:, (2 * j + s) * size : (2 * j + s + 1) * size] for j in range(blocks)], 1)
        for s in range(2)
    ]
    own[...] = jnp.where(ids[0] == 0, parts[0], parts[1]).astype(BF)
    late[...] = jnp.where(ids[0] == 0, parts[1], parts[0]).astype(BF)


def result_kernel(ids, biases, grad_hidden, back_a, *refs):
    total = biases[4:5]
    for ref in refs[:-1]:
        total = total + ref[...].astype(F32)
    width = grad_hidden.shape[1]
    refs[-1][:, :width] = total.astype(BF)
    refs[-1][:, width : 2 * width] = grad_hidden[...]
    refs[-1][:, 2 * width :] = back_a[...]


def half_kernel(ids, keep_two, got_two, keep_one, got_one, own, far):
    half = own.shape[2]
    for i, (keep, got) in enumerate(((keep_two, got_two), (keep_one, got_one))):
        total = keep[0].astype(F32) + got[0].astype(F32)
        left, right = total[:, :half], total[:, half:]
        own[i] = jnp.where(ids[0] == 0, left, right)
        far[i] = jnp.where(ids[0] == 0, right, left).astype(BF)


def join_ff_kernel(ids, own, far, two, one):
    rows = own.shape[1]
    for i in range(2):
        here, there = own[i], far[i].astype(F32)
        first, second = jnp.where(ids[0] == 0, here, there), jnp.where(ids[0] == 0, there, here)
        if i == 0:
            two[:rows] = first
            two[rows:] = second
        else:
            one[...] = jnp.concatenate([first, second], 0).T


def ends_kernel(split, ids, keep_two, got_two, proj, skip):
    total = keep_two[0].astype(F32) + got_two[0].astype(F32)
    proj[...] = total[:split]
    skip[...] = total[split:]


def third_half_kernel(ids, keep, got, own, far):
    half = own.shape[1]
    total = keep[0].astype(F32) + got[0].astype(F32)
    left, right = total[:, :half], total[:, half:]
    own[...] = jnp.where(ids[0] == 0, left, right)
    far[...] = jnp.where(ids[0] == 0, right, left).astype(BF)


def third_join_kernel(ids, own, far, out):
    here, there = own[...], far[...].astype(F32)
    first, second = jnp.where(ids[0] == 0, here, there), jnp.where(ids[0] == 0, there, here)
    out[...] = jnp.concatenate([first, second], 0).T


def home_kernel(ids, counts, back, back_b, output, grad_hidden, grad_skip):
    rows, width = output.shape
    grad_hidden[...] = back[:, width : 2 * width]
    seq = ids[0]
    spot = lax.broadcasted_iota(jnp.int32, (rows, 1), 0) + seq * rows
    live = jnp.logical_and(spot < 2 * rows - PADDED, counts[0] > 0)
    output[...] = jnp.where(live, back[:, :width].astype(F32), 0.0).astype(BF)
    a, b = back[:, 2 * width :].astype(F32), back_b[...].astype(F32)
    grad_skip[:rows] = jnp.where(seq == 0, a, b).astype(BF)
    grad_skip[rows:] = jnp.where(seq == 0, b, a).astype(BF)


def last_kernel(
    ids, grad_q, gkv, merged, grad_after, w_skip, w_qkv, gains, sums_two, sums_out, units_own, units_far, ga_far,
    gm_own, gm_far, grad_hidden, back_a, back_b, small,
):
    width = merged.shape[1]
    half = width // 2
    xhat, rstd = norm(merged[...])
    gn = dot(grad_q[...], w_qkv[:, :width], (1, 1))
    gn += dot(gkv[...], w_qkv[:, width:], (1, 1))
    value = grad_after[...] + norm_back(gn, xhat, rstd, gains[0:1])
    units = units_own[0:1] + units_far[0:1]
    spot = 2 * ids[1] + ids[0]
    sums = jnp.concatenate(
        [
            jnp.sum(gn * xhat, axis=0, keepdims=True),
            sums_two[0:1],
            jnp.sum(value, axis=0, keepdims=True),
            jnp.sum(gn, axis=0, keepdims=True),
            sums_two[2:3],
            sums_two[1:2],
            sums_out[0:1],
        ]
        + [jnp.where(spot == i, units, 0.0) for i in range(4)]
        + [jnp.zeros((5, width), F32)],
        0,
    )
    small[...] = sums
    halves = value[:, :half], value[:, half:]
    rows = value.shape[0]
    gm_own[...] = jnp.where(ids[0] == 0, halves[0], halves[1]).astype(BF)
    gm_far[:rows, :half] = ga_far[...]
    gm_far[:rows, half:] = jnp.where(ids[0] == 0, halves[1], halves[0]).astype(BF)
    gm_far[gm_far.shape[0] - 16 :] = sums.astype(BF)
    low = value.astype(BF)
    grad_hidden[...] = dot(low, w_skip[:width], (1, 1)).astype(BF)
    a = dot(low, w_skip[width : width + half], (1, 1))
    b = dot(low, w_skip[width + half :], (1, 1))
    back_a[...] = jnp.where(ids[1] == 0, a, b).astype(BF)
    back_b[...] = jnp.where(ids[1] == 0, b, a).astype(BF)


def shards(
    hidden_in,
    skip_in,
    cotangent,
    timesteps,
    counts,
    w_skip,
    w_qkv,
    w_proj,
    w_fc1,
    w_fc2,
    gains,
    biases,
    fc1_bias,
):
    rows, width = hidden_in.shape[1:]
    half = width // 2
    ff = w_fc1.shape[1]
    n_dp = lax.axis_size("dp")
    bits = n_dp.bit_length() - 1
    pairs = n_dp // 2
    place = lax.axis_index("dp")
    core = place % 2
    seq = lax.axis_index("seq")
    piece = ff // (4 * pairs)
    quarter = pairs * piece
    ids = jnp.stack([seq] + [(place >> b) & 1 for b in range(bits)]).astype(jnp.int32)
    ids = lax.optimization_barrier(ids)
    pitch = -(-rows // GAP) * GAP

    def flat(dp, s):
        return 2 * dp + s

    mirror_perm = [
        (flat(2 * k + c, s), flat(2 * k + s, c)) for k in range(pairs) for c in range(2) for s in range(2)
    ]
    turn = {(0, 0): (1, 0), (1, 0): (1, 1), (1, 1): (0, 1), (0, 1): (0, 0)}
    turn_perm = [
        (flat(2 * k + c, s), flat(2 * k + d[0], d[1])) for k in range(pairs) for (c, s), d in turn.items()
    ]
    turn_back_perm = [(b, a) for a, b in turn_perm]

    def mirror(x):
        return lax.ppermute(x, ("dp", "seq"), mirror_perm)

    def across_seq(x):
        return lax.ppermute(x, "seq", [(0, 1), (1, 0)])

    def across_bit(x, bit):
        return lax.ppermute(x, "dp", [(i, i ^ (1 << bit)) for i in range(n_dp)])

    def across_core(x):
        return across_bit(x, 0)

    def swap_if(flag, a, b, axis):
        return jnp.where(flag, jnp.concatenate([b, a], axis), jnp.concatenate([a, b], axis))

    def my_bit(bit):
        return (place >> bit) & 1

    marks = []

    def run(kernel, name, operands, outs, scratch, mib, flops, after=()):
        results = call(
            kernel,
            name,
            [(ids, IN_SMEM)] + [a if isinstance(a, tuple) else (a, IN_VMEM) for a in operands],
            outs,
            scratch,
            mib,
            flops,
            [*marks[-1:], *after],
        )
        marks.append(results[-1])
        return results[:-1]

    def tie(x, *others):
        return lax.optimization_barrier((x, *others))[0]

    def later(x):
        return lax.optimization_barrier((x, marks[-1]))[0]

    token = shape((rows, width), BF)
    token32 = shape((rows, width), F32)
    half_token = shape((rows, half), BF)
    wide_token = shape((rows, width + half), BF)
    sums = shape((8, width), F32)
    work = 2 * rows * width * width

    hidden = mirror(hidden_in[0])
    skip_a, skip_b = run(
        pack_kernel,
        "pack",
        [(skip_in[0], IN_ANY)],
        [half_token, half_token],
        [pltpu.VMEM((2 * rows, half), BF), pltpu.SemaphoreType.DMA((1,))],
        0,
        work // 100,
    )
    skip_a = mirror(skip_a)
    skip_b = lax.ppermute(skip_b, ("dp", "seq"), turn_perm)

    if piece % GAP == 0 and piece <= 2 * LANES - 7 * GAP:
        w1, w2, b1 = run(
            functools.partial(gather_kernel, pairs),
            "gather",
            [w_fc1, (w_fc2.reshape(4 * pairs, piece, width), IN_HBM), fc1_bias.reshape(ff // LANES, LANES)],
            [shape((width, quarter), BF), shape((pairs, piece, width), BF), shape((8, quarter), F32)],
            [pltpu.SemaphoreType.DMA((pairs,))],
            GATHER_MIB,
            work // 100,
        )
    else:
        w1 = pick(pick(w_fc1.reshape(width, pairs, 2, 2, piece), core, 2), seq, 2).reshape(width, quarter)
        b1 = pick(pick(fc1_bias.reshape(pairs, 2, 2, piece), core, 1), seq, 1).reshape(1, quarter)
        b1 = jnp.broadcast_to(b1, (8, quarter))
        w2 = pick(pick(w_fc2.reshape(pairs, 2, 2, piece, width), core, 1), seq, 1)
    w2 = w2.reshape(quarter, width)

    g_home, sum_grad_out = run(
        grad_out_kernel,
        "grad_out",
        [(timesteps, IN_SMEM), (counts, IN_SMEM), cotangent[0]],
        [token, sums],
        [],
        0,
        work // 100,
    )

    merged, early_a, early, q, kv = run(
        first_kernel,
        "first",
        [hidden, skip_a, skip_b, w_skip, w_qkv, gains, biases],
        [token32, wide_token, wide_token, token, shape((rows, 2 * width), BF)],
        [],
        0,
        5 * work,

    )
    kv_other = across_core(kv)
    g_far = across_seq(g_home)
    g_other = across_core(g_home)

    key_buf = pltpu.VMEM((2 * pitch, width), BF)
    proj_buf = [pltpu.VMEM((width, width), BF), pltpu.SemaphoreType.DMA((1,))]
    early_b, after_attn, normed_two, log_total = run(
        attend_kernel,
        "attend",
        [q, kv, kv_other, merged, early, (w_proj, IN_ANY), gains, biases],
        [shape((rows, 2 * width + half), BF), token32, token, shape((rows, LANES), F32)],
        [key_buf, key_buf, *proj_buf],
        0,
        2 * work,
    )

    n_far = across_seq(normed_two)
    n_other = across_core(normed_two)
    g_other_far = across_core(later(g_far))

    def mlp(name, n0, n1, *g):
        tall = shape((2 * pitch, quarter), BF)
        wide = shape((2 * pitch, width), BF)
        return run(
            mlp_kernel,
            name,
            [n0, n1, *g, w1, b1, w2],
            [tall, tall, wide, wide, token32, token, shape((8, quarter), F32)],
            [pltpu.VMEM((2 * pitch, 3 * LANES), F32), pltpu.VMEM((2 * pitch, 3 * LANES), F32)],
            0,
            6 * 2 * rows * width * quarter,
        )

    act_own, gi_own, nn_own, gg_own, gn_own, gn_own_core, si_own = mlp(
        "mlp_own", normed_two, n_other, g_home, g_other_far, g_far, g_other
    )
    n_other_far = across_core(later(n_far))
    early_a_far = across_seq(tie(early_a, n_far))
    act_far, gi_far, nn_far, gg_far, gn_far, gn_far_core, si_far = mlp(
        "mlp_far", n_far, n_other_far, g_other, g_far, g_other_far, g_home
    )
    gn_far_core = across_core(gn_far_core)
    gn_own_core = across_core(gn_own_core)

    def outer(name, products, blocks, bit, shift, riding=None, after=()):
        pieces = PIECES if shift == 0 and n_dp // 2 % PIECES == 0 else 1
        lefts = [sum(n for _, _, n in parts[0][0]) for _, parts in products]
        rows_of = [n // blocks for n in lefts]
        inside = all(r % 4 == 0 for r in rows_of)
        cols = products[0][0]
        stride = (1 << (bit - shift)) if inside else 0
        scratch, operands = [], []
        for n, (c, parts) in zip(lefts, products):
            height = -(-parts[0][0][0][0].shape[0] // GAP) * GAP * len(parts)
            scratch += [pltpu.VMEM((n, c), F32), pltpu.VMEM((height, n), BF), pltpu.VMEM((height, c), BF)]
            for left, (right, _) in parts:
                operands += [x for x, _, _ in left] + [right]
        r = sum(rows_of)
        if inside:
            outs = [shape((blocks // 2, r, cols), BF)] + [shape((blocks // 2 // pieces, r, cols), BF)] * pieces
        else:
            outs = [shape((n, cols), BF) for n in lefts]
        layout = [[([span for _, *span in left], right[1]) for left, right in parts] for _, parts in products]
        if riding is not None:
            outs = [outs[0], *[shape((blocks // 2 // pieces, r, cols + extra), BF)] * pieces, shape((r, extra), F32)]
            operands.append(riding)
        results = run(
            functools.partial(outer_kernel if riding is None else ride_outer_kernel, stride, bit, layout, pieces),
            name,
            operands,
            outs,
            scratch,
            0,
            sum(2 * n * cols * 4 * rows for n in lefts),
            after,
        )
        if inside:
            return results[0], results[1 : 1 + pieces], results[1 + pieces :]
        whole = jnp.concatenate([x.reshape(blocks, r, cols) for x, r in zip(results, rows_of)], 1)
        whole = whole.reshape(blocks >> (bit - shift + 1), 2, 1 << (bit - shift), sum(rows_of), cols)
        flat_shape = (blocks // 2, sum(rows_of), cols)
        keep, send = [pick(whole, i, 1).reshape(flat_shape) for i in (my_bit(bit), 1 - my_bit(bit))]
        return keep, [send], []

    def combine(name, keep, gots, left, bit, riding=(), after=()):
        count, r, cols = keep.shape
        stride = 1 << left.index(bit)
        if r % 4 == 0:
            results = run(
                functools.partial(ride_combine_kernel if riding else combine_kernel, stride, bit),
                name,
                [keep, *riding, *gots],
                [shape((count // 2, r, cols), BF), shape((count // 2, r, gots[0].shape[2]), BF)]
                + [shape(x.shape, F32) for x in riding],
                [],
                0,
                work // 100,
                after,
            )
            return results[0], [results[1]], results[2:]
        both = (keep.astype(F32) + gots[0].astype(F32)).astype(BF).reshape(count // (2 * stride), 2, stride, r, cols)
        keep, send = [pick(both, i, 1).reshape(count // 2, r, cols) for i in (my_bit(bit), 1 - my_bit(bit))]
        return keep, [send], []

    class Chain:
        def __init__(self, name, order, parts):
            self.name, self.order = name, order
            self.keep, sends, self.riding = parts
            self.step = 0
            self.left = sorted(order[1:])
            self.got = [across_bit(send, order[0]) for send in sends]

        def advance(self, *after):
            self.step += 1
            if self.step >= len(self.order):
                return
            bit = self.order[self.step]
            self.keep, sends, self.riding = combine(
                f"{self.name}_{self.step}", self.keep, self.got, self.left, bit, self.riding, after
            )
            self.left.remove(bit)
            self.got = [across_bit(send, bit) for send in sends]

    def order_of(first):
        return first + list(range(4, bits))

    def add(name, out, *terms):
        return run(add_kernel, name, list(terms), [out], [], 0, work // 100)[0]

    fc2 = Chain(
        "fc2",
        order_of([1, 2, 3]),
        outer("outer_fc2", [(width, [([(act_own, 0, quarter)], (gg_own, 0)), ([(act_far, 0, quarter)], (gg_far, 0))])], pairs, 1, 1),
    )
    gn_far = across_seq(add("gn_add", token, gn_far, gn_far_core))
    fc1 = Chain(
        "fc1",
        order_of([2, 1, 3]),
        outer("outer_fc1", [(width, [([(gi_own, 0, quarter)], (nn_own, 0)), ([(gi_far, 0, quarter)], (nn_far, 0))])], pairs, 2, 1, None, (early_a_far,)),
    )

    split = width // n_dp
    extra = -half % LANES
    rides = 3 * split % 8 == 0 and extra and 3 * split * extra == 12 * width
    early_b_far = across_seq(tie(early_b, gn_far))
    grad_after, ga_own, ga_far, grad_q, gkv_own, gk_other, gv_other, sums_two = run(
        attend_back_kernel,
        "attend_back",
        [gn_own, gn_own_core, gn_far, g_home, g_other_far, after_attn, q, kv, kv_other, log_total]
        + [(w_proj, IN_ANY), gains],
        [token32, half_token, half_token, token]
        + [shape((rows, 2 * width), F32), token, token, sums],
        [key_buf, key_buf, proj_buf[0], pltpu.VMEM((2 * pitch, width), F32), pltpu.VMEM((2 * pitch, width), F32), proj_buf[1]],
        0,
        3 * work,
    )
    gk_core, gv_core = across_core(gk_other), across_core(gv_other)
    even = 3 * split % 8 == 0
    if even:
        gkv, project_own, late = run(
            functools.partial(project_kernel, n_dp),
            "project",
            [grad_q, gkv_own, gk_core, gv_core],
            [shape((rows, 2 * width), BF), wide_token, wide_token],
            [],
            0,
            work // 100,
        )
        third_cols, normed, normed_far = width, early_b, early_b_far
    else:
        gkv = (gkv_own + jnp.concatenate([gk_core, gv_core], 1).astype(F32)).astype(BF)
        project_own = jnp.concatenate([grad_q, gkv], 1)
        late = project_own
        third_cols = half
        normed, normed_far = [
            lax.dynamic_slice_in_dim(x, seq * half, half, 1) for x in (early_b, early_b_far)
        ]
    third_wide = project_own.shape[1]
    late_far = across_seq(late)
    gm_own, gm_far, grad_hidden, back_a, back_b, small = run(
        last_kernel,
        "last",
        [grad_q, gkv, merged, grad_after, w_skip, w_qkv, gains, sums_two, sum_grad_out, si_own, si_far, ga_far],
        [half_token, shape((pitch + 16, width), BF), token, half_token, half_token, shape((16, width), F32)],
        [],
        0,
        5 * work,
    )
    gm_far = across_seq(gm_far)

    fc2.advance(early_b_far)
    out_own, out_far, out_own_core, out_far_core = run(
        lambda ids, *refs: mlp_out_kernel(*refs),
        "mlp_out",
        [act_own, act_far, w2],
        [token32, token32, token, token],
        [],
        0,
        2 * 4 * rows * width * quarter,
    )
    out_own_core, out_far_core = across_core(out_own_core), across_core(out_far_core)
    fc1.advance()
    third = Chain(
        "third",
        order_of([0, 2, 1, 3]),
        outer(
            "outer_third",
            [
                (
                    third_cols,
                    [
                        ([(project_own, 0, third_wide)], (normed, 0)),
                        ([(late_far, 0, third_wide)], (normed_far, 0)),
                    ],
                )
            ],
            n_dp,
            0,
            0,
        ),
    )
    second = Chain(
        "second",
        order_of([0, 1, 2, 3]),
        outer(
            "outer_second",
            [
                (half, [([(early_b, width, width)], (ga_own, 0)), ([(early_b_far, width, width)], (gm_far, 0))]),
                (
                    half,
                    [
                        ([(early_a, 0, width + half), (early_b, 2 * width, half)], (gm_own, 0)),
                        ([(early_a_far, 0, width + half), (early_b_far, 2 * width, half)], (gm_far, half)),
                    ],
                ),
            ],
            n_dp,
            0,
            0,
            small if rides else None,
        ),
    )
    third.advance()
    second.advance()
    fc2.advance()
    fc1.advance()
    out_far = across_seq(add("out_add", token, out_far, out_far_core))
    back = run(
        result_kernel,
        "result",
        [biases, grad_hidden, back_a, after_attn, out_own, out_own_core, out_far],
        [shape((rows, 2 * width + half), BF)],
        [],
        0,
        work // 100,
    )[0]
    back = mirror(back)
    back_b = lax.ppermute(later(back_b), ("dp", "seq"), turn_back_perm)
    if not rides:
        small = small[:12]
        small = small + across_seq(small)
        for bit in range(bits):
            small = small + across_bit(small, bit)
    third.advance()
    second.advance()
    while fc2.step + 1 < len(fc2.order):
        fc2.advance()
        fc1.advance()
    own, far = run(
        half_kernel,
        "half",
        [fc2.keep, *fc2.got, fc1.keep, *fc1.got],
        [shape((2, piece, half), F32), shape((2, piece, half), BF)],
        [],
        0,
        work // 100,
    )
    far = across_seq(far)
    output, grad_hidden, grad_skip = run(
        home_kernel,
        "home",
        [(counts, IN_SMEM), back, back_b],
        [token, token, shape((2 * rows, half), BF)],
        [],
        0,
        work // 100,
    )
    while third.step + 1 < len(third.order):
        third.advance()
        second.advance()
    out_w_fc2, out_w_fc1 = run(
        join_ff_kernel,
        "join_ff",
        [own, far],
        [shape((2 * piece, half), F32), shape((half, 2 * piece), F32)],
        [],
        0,
        work // 100,
    )
    if even:
        third_rows = 3 * split // 2
        third_own, third_far = run(
            third_half_kernel,
            "third_half",
            [third.keep, *third.got],
            [shape((third_rows, half), F32), shape((third_rows, half), BF)],
            [],
            0,
            work // 100,
        )
        third_far = across_seq(third_far)
    ends = [shape((split, half), F32), shape((2 * split, half), F32)]
    if rides:
        out_w_proj, out_w_skip, grad_gains, grad_biases, grad_fc1_bias = run(
            functools.partial(ride_ends_kernel, split, pairs),
            "ends",
            [second.keep, *second.got, *second.riding],
            ends + [shape((2, width), F32), shape((5, width), F32), shape((1, ff), F32)],
            [pltpu.VMEM((16, width), F32)],
            0,
            work // 100,
        )
        grad_fc1_bias = grad_fc1_bias.reshape(ff)
    else:
        out_w_proj, out_w_skip = run(
            functools.partial(ends_kernel, split), "ends", [second.keep, *second.got], ends, [], 0, work // 100
        )
        grad_gains, grad_biases = small[:2], small[2:7]
        grad_fc1_bias = small[7:11].reshape(2, 2, pairs, piece).transpose(2, 0, 1, 3).reshape(ff)
    if even:
        (out_w_qkv,) = run(
            third_join_kernel,
            "third_join",
            [third_own, third_far],
            [shape((half, 2 * third_rows), F32)],
            [],
            0,
            work // 100,
        )
    else:
        out_w_qkv = (third.keep[0].astype(F32) + third.got[0][0].astype(F32)).T
    return (
        output[None],
        grad_hidden[None],
        grad_skip[None],
        out_w_skip,
        out_w_qkv,
        out_w_proj,
        out_w_fc1,
        out_w_fc2,
        grad_gains,
        grad_biases,
        grad_fc1_bias,
    )


def solution(mesh):
    return jax.shard_map(
        shards,
        mesh=mesh,
        in_specs=(
            P("dp", "seq", None),
            P("dp", None, "seq"),
            P("dp", "seq", None),
            P("dp"),
            P("dp"),
            P(),
            P(),
            P(),
            P(),
            P(),
            P(),
            P(),
            P(),
        ),
        out_specs=(
            P("dp", "seq", None),
            P("dp", "seq", None),
            P("dp", None, "seq"),
            P("dp", "seq"),
            P("seq", "dp"),
            P("dp", "seq"),
            P("seq", "dp"),
            P("dp", "seq"),
            P(),
            P(),
            P(),
        ),
        check_vma=False,
    )
```

```python
import functools

import jax
import jax.numpy as jnp
from jax import lax
from jax.experimental import pallas as pl
from jax.experimental.pallas import tpu as pltpu
from jax.sharding import PartitionSpec as P

HEADS = 16
PADDED = 2
TSTEPS = 1000

EPSILON = 1e-06
NEG_FILL = -1e30
BF = jnp.bfloat16
F32 = jnp.float32
MIB = 1 << 20
LANES = 128
GAP = 16


def dot(left, right, dims):
    return lax.dot_general(left, right, ((dims[:1], dims[1:]), ((), ())), preferred_element_type=F32)


def norm(value):
    center = value - jnp.mean(value, axis=-1, keepdims=True)
    rstd = lax.rsqrt(jnp.mean(center * center, axis=-1, keepdims=True) + EPSILON)
    return center * rstd, rstd


def norm_back(grad, xhat, rstd, gain):
    scaled = grad * gain
    return rstd * (
        scaled
        - jnp.mean(scaled, axis=-1, keepdims=True)
        - xhat * jnp.mean(scaled * xhat, axis=-1, keepdims=True)
    )


def pick(array, index, axis):
    return lax.dynamic_index_in_dim(array, index, axis, keepdims=False)


def shape(dims, dtype):
    return jax.ShapeDtypeStruct(dims, dtype)


def padded(dims, dtype):
    dims = (1,) * (2 - len(dims)) + tuple(dims)
    size = -(-dims[-2] // 16) * 16 * -(-dims[-1] // LANES) * LANES
    for dim in dims[:-2]:
        size *= dim
    return size * jnp.dtype(dtype).itemsize


COMPUTE = ("gather",)
PIECES = 1
UNROLL = True
GATHER_MIB = 34
SCALE = 0.3
TAKES = {
    "pack": 12.0,
    "gather": 8.0,
    "first": 4.4,
    "attend": 6.6,
    "mlp": 6.0,
    "outer": 3.2,
    "attend_back": 10.3,
    "last": 6.3,
    "outer_second": 0.3,
    "outer_third": 0.3,
    "third": 0.3,
    "second": 0.3,
    "fc1": 0.3,
    "fc2": 0.3,
}


IN_VMEM = pl.BlockSpec(memory_space=pltpu.VMEM)
IN_SMEM = pl.BlockSpec(memory_space=pltpu.SMEM)
IN_ANY = pl.BlockSpec(memory_space=pl.ANY)
IN_HBM = pl.BlockSpec(memory_space=pltpu.HBM)


def call(kernel, name, operands, outs, scratch, mib, flops, after=()):
    takes = TAKES.get(name, TAKES.get(name.split("_")[0], 1.0)) * SCALE
    outs = [*outs, shape((8, LANES), F32)]
    inputs = len(operands)
    marks = len(after)
    if not mib:
        need = sum(padded(a.shape, a.dtype) for a, spec in operands if spec is IN_VMEM)
        need += sum(padded(o.shape, o.dtype) for o in outs)
        need += sum(padded(b.shape, b.dtype) for b in scratch if b.memory_space == pltpu.VMEM)
        mib = need * 9 // 8 // MIB + 4

    def body(*refs):
        mark = refs[inputs + marks + len(outs) - 1]
        mark[...] = jnp.zeros_like(mark)
        kernel(*refs[:inputs], *refs[inputs + marks : inputs + marks + len(outs) - 1], *refs[inputs + marks + len(outs) :])

    return pl.pallas_call(
        body,
        out_shape=outs,
        in_specs=[spec for _, spec in operands] + [IN_ANY] * marks,
        out_specs=[IN_VMEM] * len(outs),
        scratch_shapes=scratch,
        compiler_params=pltpu.CompilerParams(vmem_limit_bytes=mib * MIB),
        cost_estimate=pl.CostEstimate(flops=int(takes * 1e9), bytes_accessed=1 if name in COMPUTE else int(takes * 3.6e6), transcendentals=0),
        name=name,
    )(*[a for a, _ in operands], *after)


def fetch(pairs, sems):
    copies = [pltpu.make_async_copy(src, dst, sems.at[i]) for i, (src, dst) in enumerate(pairs)]
    for copy in copies:
        copy.start()
    return copies


def gather_kernel(pieces, ids, w_fc1, w_fc2, bias, w1, w2, b1, sems):
    core, seq = ids[1], ids[0]
    piece_size = w1.shape[1] // pieces
    which = [4 * m + 2 * core + seq for m in range(pieces)]
    spots = [w * piece_size for w in which]
    copies = fetch([(w_fc2.at[w], w2.at[m]) for m, w in enumerate(which)], sems)
    lane = lax.broadcasted_iota(jnp.int32, (8, LANES), 1)
    for m in range(pieces):
        base, into = m * piece_size // LANES * LANES, m * piece_size % LANES
        window = [bias[pl.ds(spots[m] // LANES + i, 1), :] for i in range(2)]
        window = jnp.concatenate([jnp.broadcast_to(x, (8, LANES)) for x in window], 1)
        turn = (into - spots[m] % LANES + 2 * LANES) % (2 * LANES)
        window = pltpu.roll(window, turn, 1)
        left = window[:, :LANES]
        if into:
            left = jnp.where(lane >= into, left, b1[:, base : base + LANES])
        b1[:, base : base + LANES] = left
        b1[:, base + LANES : base + 2 * LANES] = window[:, LANES:]
    source = lax.broadcasted_iota(jnp.int32, (2 * LANES, 2 * LANES), 0)
    target = lax.broadcasted_iota(jnp.int32, (2 * LANES, 2 * LANES), 1)
    before = {}
    for m in range(pieces):
        base = m * piece_size // LANES * LANES
        column = target + (base - m * piece_size)
        take = jnp.logical_and(column >= 0, column < piece_size)
        take = jnp.logical_and(take, source == column + spots[m] % LANES)
        window = pl.ds(pl.multiple_of(spots[m] // LANES * LANES, LANES), 2 * LANES)
        part = dot(w_fc1[:, window], take.astype(F32).astype(BF), (1, 0))
        for at, half in ((base, part[:, :LANES]), (base + LANES, part[:, LANES:])):
            before[at] = before[at] + half if at in before else half
        for at in [x for x in before if x <= base]:
            w1[:, at : at + LANES] = before.pop(at).astype(BF)
    for at, half in before.items():
        w1[:, at : at + LANES] = half.astype(BF)
    for copy in copies:
        copy.wait()


def pack_kernel(ids, skip_in, skip_a, skip_b, skip, sems):
    rows = skip_a.shape[0]
    seq = ids[0]
    fetch([(skip_in, skip)], sems)[0].wait()
    whole = skip[...].astype(F32)
    top, bottom = whole[:rows], whole[rows:]
    skip_a[...] = jnp.where(seq == 0, top, bottom).astype(BF)
    skip_b[...] = jnp.where(seq == 0, bottom, top).astype(BF)


def grad_out_kernel(ids, timesteps, counts, cotangent, g_home, sums):
    rows, width = g_home.shape
    time = jnp.zeros((1, 1), F32) + timesteps[0].astype(F32)
    weight = jax.nn.sigmoid(12.0 * time / TSTEPS - 6.0)
    spot = lax.broadcasted_iota(jnp.int32, (rows, 1), 0) + ids[0] * rows
    live = jnp.logical_and(spot < 2 * rows - PADDED, counts[0] > 0)
    g = cotangent[...].astype(F32) * jnp.where(live, weight, 0.0)
    g_home[...] = g.astype(BF)
    sums[...] = jnp.concatenate([jnp.sum(g, axis=0, keepdims=True), jnp.zeros((7, width), F32)], 0)


def first_kernel(ids, hidden, skip_a, skip_b, w_skip, w_qkv, gains, biases, merged, early_a, early, q, kv):
    width = hidden.shape[1]
    half = width // 2
    core = ids[1]
    a, b = skip_a[...].astype(F32), skip_b[...].astype(F32)
    low = jnp.where(core == 0, a, b).astype(BF)
    high = jnp.where(core == 0, b, a).astype(BF)
    early_a[:, :width] = hidden[...]
    early_a[:, width:] = low
    early[:, width:] = high
    total = dot(hidden[...], w_skip[:width], (1, 0)) + biases[0:1]
    total += dot(low, w_skip[width : width + half], (1, 0))
    total += dot(high, w_skip[width + half :], (1, 0))
    merged[...] = total
    xhat, _ = norm(total)
    one = (xhat * gains[0:1] + biases[1:2]).astype(BF)
    early[:, :width] = one
    kv[...] = dot(one, w_qkv[:, width:], (1, 0)).astype(BF)
    q[...] = dot(one, w_qkv[:, :width], (1, 0)).astype(BF)


def head_windows(width):
    size = width // HEADS
    spans = []
    for h in range(HEADS):
        low, high = h * size, (h + 1) * size
        t0, t1 = low // LANES, (high - 1) // LANES + 1
        spans.append((h, low, high, t0 * LANES, t1 * LANES))
    return spans


def lane_mask(low, high, first, last):
    lane = lax.broadcasted_iota(jnp.int32, (1, last - first), 1) + first
    return jnp.logical_and(lane >= low, lane < high)


def key_mask(core, rows, pitch, axis=1):
    spot = lax.broadcasted_iota(jnp.int32, (1, 2 * pitch) if axis else (2 * pitch, 1), axis)
    other = spot >= pitch
    here = jnp.where(other, spot - pitch, spot)
    last_half = jnp.where(other, 1 - core, core) == 1
    limit = jnp.where(last_half, rows - PADDED, rows)
    return here < limit


def lay_keys(keys, values, kv_own, kv_other, rows, pitch, width):
    for buf, at in ((keys, 0), (values, width)):
        buf[...] = jnp.zeros_like(buf)
        buf[0:rows] = kv_own[:, at : at + width]
        buf[pitch : pitch + rows] = kv_other[:, at : at + width]


def attend_kernel(ids, q, kv_own, kv_other, merged, early, w_proj, gains, biases, early_b, after, normed, log_total, keys, values, wp, sems):
    rows, width = q.shape
    pitch = keys.shape[0] // 2
    copies = fetch([(w_proj, wp)], sems)
    lay_keys(keys, values, kv_own, kv_other, rows, pitch, width)
    valid = key_mask(ids[1], rows, pitch)
    scale = (width // HEADS) ** (-0.5)
    lane = lax.broadcasted_iota(jnp.int32, (rows, LANES), 1)
    tiles = [jnp.zeros((rows, LANES), F32) for _ in range(width // LANES)]
    logs = jnp.zeros((rows, LANES), F32)
    for h, low, high, first, last in head_windows(width):
        mask = lane_mask(low, high, first, last)
        mine = q[:, first:last] * mask.astype(F32).astype(BF)
        scores = jnp.where(valid, dot(mine, keys[:, first:last], (1, 1)) * scale, NEG_FILL)
        top = jnp.max(scores, axis=-1, keepdims=True)
        expo = jnp.exp(scores - top)
        total = jnp.sum(expo, axis=-1, keepdims=True)
        probs = (expo * (1.0 / total)).astype(BF)
        logs = jnp.where(lane == h, top + jnp.log(total), logs)
        part = dot(probs, values[:, first:last], (1, 0))
        for t in range(first, last, LANES):
            tiles[t // LANES] = jnp.where(
                mask[:, t - first : t - first + LANES], part[:, t - first : t - first + LANES], tiles[t // LANES]
            )
    log_total[...] = logs
    for t, tile in enumerate(tiles):
        early_b[:, width + t * LANES : width + (t + 1) * LANES] = tile.astype(BF)
    copies[0].wait()
    early_b[:, :width] = early[:, :width]
    early_b[:, 2 * width :] = early[:, width:]
    value = merged[...] + dot(early_b[:, width : 2 * width], wp[...], (1, 0)) + biases[2:3]
    after[...] = value
    xhat, _ = norm(value)
    normed[...] = (xhat * gains[1:2] + biases[3:4]).astype(BF)


def attend_back_kernel(
    ids, gn_mine, gn_core, gn_far, g_home, g_cross, after, q, kv_own, kv_other, log_total, w_proj, gains,
    grad_after, ga_own, ga_far, grad_q, gkv_own, gk_other, gv_other, sums,
    keys, values, wp, gk, gv, sems,
):
    rows, width = q.shape
    half = width // 2
    pitch = keys.shape[0] // 2
    copies = fetch([(w_proj, wp)], sems)
    gn = gn_mine[...] + gn_core[...].astype(F32) + gn_far[...].astype(F32)
    xhat, rstd = norm(after[...])
    g_out = jnp.where(ids[0] == ids[1], g_home[...].astype(F32), g_cross[...].astype(F32))
    value = g_out + norm_back(gn, xhat, rstd, gains[1:2])
    grad_after[...] = value
    low = value.astype(BF)
    halves = value[:, :half], value[:, half:]
    ga_own[...] = jnp.where(ids[0] == 0, halves[0], halves[1]).astype(BF)
    ga_far[...] = jnp.where(ids[0] == 0, halves[1], halves[0]).astype(BF)
    sums[...] = jnp.concatenate(
        [
            jnp.sum(gn * xhat, axis=0, keepdims=True),
            jnp.sum(gn, axis=0, keepdims=True),
            jnp.sum(value, axis=0, keepdims=True),
            jnp.zeros((5, width), F32),
        ],
        0,
    )
    lay_keys(keys, values, kv_own, kv_other, rows, pitch, width)
    valid = key_mask(ids[1], rows, pitch, 0)
    scale = (width // HEADS) ** (-0.5)
    copies[0].wait()
    grad_mixed = dot(low, wp[...], (1, 1)).astype(BF)
    gk[...] = jnp.zeros_like(gk)
    gv[...] = jnp.zeros_like(gv)
    tiles = [jnp.zeros((rows, LANES), F32) for _ in range(width // LANES)]
    logs = log_total[...].T
    for h, start, stop, first, last in head_windows(width):
        mask = lane_mask(start, stop, first, last)
        low_mask = mask.astype(F32).astype(BF)
        mine = q[:, first:last] * low_mask
        gm = grad_mixed[:, first:last] * low_mask
        scores = jnp.where(valid, dot(keys[:, first:last], mine, (1, 1)) * scale, NEG_FILL)
        probs = jnp.exp(scores - logs[h : h + 1, :])
        gp = dot(values[:, first:last], gm, (1, 1))
        gs = (probs * (gp - jnp.sum(gp * probs, axis=0, keepdims=True))).astype(BF)
        part = dot(gs, keys[:, first:last], (0, 0))
        for t in range(first, last, LANES):
            tiles[t // LANES] = jnp.where(
                mask[:, t - first : t - first + LANES], part[:, t - first : t - first + LANES], tiles[t // LANES]
            )
        gk[:, first:last] += dot(gs, mine, (1, 0))
        gv[:, first:last] += dot(probs.astype(BF), gm, (1, 0))
    for t, tile in enumerate(tiles):
        grad_q[:, t * LANES : (t + 1) * LANES] = (tile * scale).astype(BF)
    gkv_own[:, :width] = gk[0:rows] * scale
    gkv_own[:, width:] = gv[0:rows]
    gk_other[...] = (gk[pitch : pitch + rows] * scale).astype(BF)
    gv_other[...] = gv[pitch : pitch + rows].astype(BF)


def lay_rows(buf, blocks):
    rows = blocks[0].shape[0]
    pitch = buf.shape[0] // len(blocks)
    if pitch > rows:
        buf[...] = jnp.zeros_like(buf)
    for i, block in enumerate(blocks):
        buf[i * pitch : i * pitch + rows] = block[...]


def lay_chosen(buf, flag, pairs):
    rows = pairs[0][0].shape[0]
    pitch = buf.shape[0] // len(pairs)
    buf[...] = jnp.zeros_like(buf)
    for way, chosen in enumerate((flag, jnp.logical_not(flag))):

        @pl.when(chosen)
        def _(way=way):
            for i, pair in enumerate(pairs):
                buf[i * pitch : i * pitch + rows] = pair[way][...]


def mlp_kernel(ids, n0, n1, g0a, g0b, g1a, g1b, w1, b1, w2, activ, grad_inner, n_all, g_all, gn_mine, gn_other, sums, inner_v, grad_v):
    rows, width = n0.shape
    units = w1.shape[1]
    lay_rows(n_all, (n0, n1))
    lay_chosen(g_all, ids[0] == ids[1], ((g0a, g0b), (g1a, g1b)))
    height = n_all.shape[0]
    pitch = height // 2
    step = 3 * LANES
    chunk = 48
    root = 0.5**0.5
    bell = (0.5 / jnp.pi) ** 0.5
    for j in range(units // step):
        cols = slice(j * step, (j + 1) * step)
        inner_v[...] = dot(n_all[...], w1[:, cols], (1, 0))
        grad_v[...] = dot(g_all[...], w2[cols, :], (1, 1))
        bias = b1[0:1, cols]

        def body(i, total):
            at = pl.ds(pl.multiple_of(i * chunk, chunk), chunk)
            x = inner_v[at] + bias
            cdf = 0.5 + 0.5 * lax.erf(x * root)
            activ[at, cols] = (x * cdf).astype(BF)
            g = grad_v[at] * (cdf + x * jnp.exp(-0.5 * x * x) * bell)
            grad_inner[at, cols] = g.astype(BF)
            return total + jnp.sum(g, axis=0, keepdims=True)

        sums[0:1, cols] = lax.fori_loop(0, height // chunk, body, jnp.zeros((1, step), F32), unroll=UNROLL)
    for j in range(width // step):
        cols = slice(j * step, (j + 1) * step)
        part = dot(grad_inner[...], w1[cols, :], (1, 1))
        gn_mine[:, cols] = part[:rows]
        gn_other[:, cols] = part[pitch : pitch + rows].astype(BF)


def mlp_out_kernel(activ_own, activ_far, w2, own, far, own_core, far_core):
    rows = own.shape[0]
    pitch = activ_own.shape[0] // 2
    step = 3 * LANES
    for activ, mine, other in ((activ_far, far, far_core), (activ_own, own, own_core)):
        for j in range(w2.shape[1] // step):
            cols = slice(j * step, (j + 1) * step)
            part = dot(activ[...], w2[:, cols], (1, 0))
            mine[:, cols] = part[:rows]
            other[:, cols] = part[pitch : pitch + rows].astype(BF)


def split_blocks(total, keep, sends, at, mine, stride):
    count = keep.shape[0]
    rows = total.shape[0] // (2 * count)
    slot = 0
    for i in range(2 * count):
        if i // stride % 2:
            continue
        a = total[i * rows : (i + 1) * rows]
        b = total[(i + stride) * rows : (i + stride + 1) * rows]
        keep[slot, at : at + rows] = jnp.where(mine == 0, a, b).astype(BF)
        per = sends[0].shape[0]
        sends[slot // per][slot % per, at : at + rows, : keep.shape[2]] = jnp.where(mine == 0, b, a).astype(BF)
        slot += 1


def outer_kernel(stride, bit, layout, pieces, ids, *refs):
    spots = iter(refs)
    operands = [
        [([(next(spots), *span) for span in left], (next(spots), right)) for left, right in parts] for parts in layout
    ]
    outs = [next(spots) for _ in range(1 + pieces if stride else len(layout))]
    at = 0
    for i, parts in enumerate(operands):
        total, left, right = next(spots), next(spots), next(spots)
        pitch = left.shape[0] // len(parts)
        cols = right.shape[1]
        for p, (lefts, (y, first)) in enumerate(parts):
            rows = lefts[0][0].shape[0]
            if pitch > rows:
                left[p * pitch : (p + 1) * pitch] = jnp.zeros((pitch, left.shape[1]), BF)
                right[p * pitch : (p + 1) * pitch] = jnp.zeros((pitch, cols), BF)
            right[p * pitch : p * pitch + rows] = y[:rows, first : first + cols]
            spot = 0
            for x, start, n in lefts:
                left[p * pitch : p * pitch + rows, spot : spot + n] = x[:, start : start + n]
                spot += n
        step = 3 * LANES
        for j in range(0, left.shape[1], step):
            span = slice(j, min(j + step, left.shape[1]))
            total[span, :] = dot(left[:, span], right[...], (0, 0))
        if stride:
            split_blocks(total, outs[0], outs[1:], at, ids[1 + bit], stride)
            at += left.shape[1] // (2 * outs[0].shape[0])
        else:
            outs[i][...] = total[...].astype(BF)


def combine_kernel(stride, bit, ids, keep, *refs):
    gots, kept, send = refs[:-2], refs[-2], refs[-1]
    slot = 0
    cols = keep.shape[2]
    per = gots[0].shape[0]

    def total(i):
        return keep[i].astype(F32) + gots[i // per][i % per, :, :cols].astype(F32)

    for i in range(keep.shape[0]):
        if i // stride % 2:
            continue
        a, b = total(i), total(i + stride)
        kept[slot] = jnp.where(ids[1 + bit] == 0, a, b).astype(BF)
        send[slot, :, :cols] = jnp.where(ids[1 + bit] == 0, b, a).astype(BF)
        slot += 1


def ride_outer_kernel(stride, bit, layout, pieces, ids, *refs):
    inputs = sum(len(left) + 1 for parts in layout for left, _ in parts)
    operands, small, outs, scratch = refs[:inputs], refs[inputs], refs[inputs + 1 : inputs + 3 + pieces], refs[inputs + 3 + pieces :]
    keep, sends, riding = outs[0], outs[1:-1], outs[-1]
    outer_kernel(stride, bit, layout, pieces, ids, *operands, keep, *sends, *scratch)
    far = operands[-1]
    total = small[...] + far[far.shape[0] - 16 :, :].astype(F32)
    cols = keep.shape[2]
    extra = sends[0].shape[2] - cols
    for j in range(small.shape[1] // extra):
        riding[12 * j : 12 * j + 12, :] = total[:12, extra * j : extra * (j + 1)]
    for send in sends:
        send[:, :, cols:] = jnp.zeros((send.shape[0], send.shape[1], extra), BF)
    sends[0][0, :, cols:] = riding[...].astype(BF)


def ride_combine_kernel(stride, bit, ids, keep, riding, *refs):
    gots, (kept, send, rode) = refs[:-3], refs[-3:]
    combine_kernel(stride, bit, ids, keep, *gots, kept, send)
    cols = keep.shape[2]
    total = riding[...] + gots[0][0, :, cols:].astype(F32)
    rode[...] = total
    if send.shape[0] > 1:
        send[1:, :, cols:] = jnp.zeros((send.shape[0] - 1, send.shape[1], send.shape[2] - cols), BF)
    send[0, :, cols:] = total.astype(BF)


def ride_ends_kernel(split, pieces, ids, keep, got, riding, proj, skip, gains, biases, units, buf, line):
    cols = keep.shape[2]
    total = keep[0].astype(F32) + got[0, :, :cols].astype(F32)
    proj[...] = total[:split]
    skip[...] = total[split:]
    extra = riding.shape[1]
    small = riding[...] + got[0, :, cols:].astype(F32)
    for j in range(buf.shape[1] // extra):
        buf[:12, extra * j : extra * (j + 1)] = small[12 * j : 12 * j + 12]
    gains[...] = buf[:2]
    biases[...] = buf[2:7]
    piece = buf.shape[1] // pieces
    for m in range(pieces):
        for i in range(4):
            at = (4 * m + i) * piece
            line[0:1, at : at + piece] = buf[7 + i : 8 + i, piece * m : piece * (m + 1)]
    for t in range(units.shape[0]):
        units[t : t + 1, :] = line[0:1, t * LANES : (t + 1) * LANES]


def add_kernel(ids, *refs):
    total = refs[0][...].astype(F32)
    for ref in refs[1:-1]:
        total += ref[...].astype(F32)
    refs[-1][...] = total.astype(refs[-1].dtype)


def project_kernel(blocks, ids, grad_q, gkv_own, gk_core, gv_core, gkv, own, late):
    total = gkv_own[...] + jnp.concatenate([gk_core[...], gv_core[...]], 1).astype(F32)
    gkv[...] = total.astype(BF)
    whole = jnp.concatenate([grad_q[...].astype(F32), total], 1)
    size = whole.shape[1] // (2 * blocks)
    parts = [
        jnp.concatenate([whole[:, (2 * j + s) * size : (2 * j + s + 1) * size] for j in range(blocks)], 1)
        for s in range(2)
    ]
    own[...] = jnp.where(ids[0] == 0, parts[0], parts[1]).astype(BF)
    late[...] = jnp.where(ids[0] == 0, parts[1], parts[0]).astype(BF)


def result_kernel(ids, biases, grad_hidden, back_a, *refs):
    total = biases[4:5]
    for ref in refs[:-1]:
        total = total + ref[...].astype(F32)
    width = grad_hidden.shape[1]
    refs[-1][:, :width] = total.astype(BF)
    refs[-1][:, width : 2 * width] = grad_hidden[...]
    refs[-1][:, 2 * width :] = back_a[...]


def half_kernel(ids, keep_two, got_two, keep_one, got_one, own, far):
    half = own.shape[2]
    for i, (keep, got) in enumerate(((keep_two, got_two), (keep_one, got_one))):
        total = keep[0].astype(F32) + got[0].astype(F32)
        left, right = total[:, :half], total[:, half:]
        own[i] = jnp.where(ids[0] == 0, left, right)
        far[i] = jnp.where(ids[0] == 0, right, left).astype(BF)


def join_ff_kernel(ids, own, far, *outs):
    rows = own.shape[1]
    for i, out in enumerate(outs):
        here, there = own[i], far[i].astype(F32)
        out[:rows] = jnp.where(ids[0] == 0, here, there)
        out[rows:] = jnp.where(ids[0] == 0, there, here)


def ends_kernel(split, ids, keep_two, got_two, proj, skip):
    total = keep_two[0].astype(F32) + got_two[0].astype(F32)
    proj[...] = total[:split]
    skip[...] = total[split:]


def third_half_kernel(ids, keep, got, own, far):
    half = own.shape[1]
    total = keep[0].astype(F32) + got[0].astype(F32)
    left, right = total[:, :half], total[:, half:]
    own[...] = jnp.where(ids[0] == 0, left, right)
    far[...] = jnp.where(ids[0] == 0, right, left).astype(BF)


def third_join_kernel(ids, own, far, out):
    here, there = own[...], far[...].astype(F32)
    rows = own.shape[0]
    out[:rows] = jnp.where(ids[0] == 0, here, there)
    out[rows:] = jnp.where(ids[0] == 0, there, here)


def home_kernel(ids, counts, back, back_b, output, grad_hidden, grad_skip):
    rows, width = output.shape
    grad_hidden[...] = back[:, width : 2 * width]
    seq = ids[0]
    spot = lax.broadcasted_iota(jnp.int32, (rows, 1), 0) + seq * rows
    live = jnp.logical_and(spot < 2 * rows - PADDED, counts[0] > 0)
    output[...] = jnp.where(live, back[:, :width].astype(F32), 0.0).astype(BF)
    a, b = back[:, 2 * width :].astype(F32), back_b[...].astype(F32)
    grad_skip[:rows] = jnp.where(seq == 0, a, b).astype(BF)
    grad_skip[rows:] = jnp.where(seq == 0, b, a).astype(BF)


def last_kernel(
    ids, grad_q, gkv, merged, grad_after, w_skip, w_qkv, gains, sums_two, sums_out, units_own, units_far, ga_far,
    gm_own, gm_far, grad_hidden, back_a, back_b, small,
):
    width = merged.shape[1]
    half = width // 2
    xhat, rstd = norm(merged[...])
    gn = dot(grad_q[...], w_qkv[:, :width], (1, 1))
    gn += dot(gkv[...], w_qkv[:, width:], (1, 1))
    value = grad_after[...] + norm_back(gn, xhat, rstd, gains[0:1])
    units = units_own[0:1] + units_far[0:1]
    spot = 2 * ids[1] + ids[0]
    sums = jnp.concatenate(
        [
            jnp.sum(gn * xhat, axis=0, keepdims=True),
            sums_two[0:1],
            jnp.sum(value, axis=0, keepdims=True),
            jnp.sum(gn, axis=0, keepdims=True),
            sums_two[2:3],
            sums_two[1:2],
            sums_out[0:1],
        ]
        + [jnp.where(spot == i, units, 0.0) for i in range(4)]
        + [jnp.zeros((5, width), F32)],
        0,
    )
    small[...] = sums
    halves = value[:, :half], value[:, half:]
    rows = value.shape[0]
    gm_own[...] = jnp.where(ids[0] == 0, halves[0], halves[1]).astype(BF)
    gm_far[:rows, :half] = ga_far[...]
    gm_far[:rows, half:] = jnp.where(ids[0] == 0, halves[1], halves[0]).astype(BF)
    gm_far[gm_far.shape[0] - 16 :] = sums.astype(BF)
    low = value.astype(BF)
    grad_hidden[...] = dot(low, w_skip[:width], (1, 1)).astype(BF)
    a = dot(low, w_skip[width : width + half], (1, 1))
    b = dot(low, w_skip[width + half :], (1, 1))
    back_a[...] = jnp.where(ids[1] == 0, a, b).astype(BF)
    back_b[...] = jnp.where(ids[1] == 0, b, a).astype(BF)


def shards(
    hidden_in,
    skip_in,
    cotangent,
    timesteps,
    counts,
    w_skip,
    w_qkv,
    w_proj,
    w_fc1,
    w_fc2,
    gains,
    biases,
    fc1_bias,
):
    rows, width = hidden_in.shape[1:]
    half = width // 2
    ff = w_fc1.shape[1]
    n_dp = lax.axis_size("dp")
    bits = n_dp.bit_length() - 1
    pairs = n_dp // 2
    place = lax.axis_index("dp")
    core = place % 2
    seq = lax.axis_index("seq")
    piece = ff // (4 * pairs)
    quarter = pairs * piece
    ids = jnp.stack([seq] + [(place >> b) & 1 for b in range(bits)]).astype(jnp.int32)
    ids = lax.optimization_barrier(ids)
    pitch = -(-rows // GAP) * GAP

    def flat(dp, s):
        return 2 * dp + s

    mirror_perm = [
        (flat(2 * k + c, s), flat(2 * k + s, c)) for k in range(pairs) for c in range(2) for s in range(2)
    ]
    turn = {(0, 0): (1, 0), (1, 0): (1, 1), (1, 1): (0, 1), (0, 1): (0, 0)}
    turn_perm = [
        (flat(2 * k + c, s), flat(2 * k + d[0], d[1])) for k in range(pairs) for (c, s), d in turn.items()
    ]
    turn_back_perm = [(b, a) for a, b in turn_perm]

    def mirror(x):
        return lax.ppermute(x, ("dp", "seq"), mirror_perm)

    def across_seq(x):
        return lax.ppermute(x, "seq", [(0, 1), (1, 0)])

    def across_bit(x, bit):
        return lax.ppermute(x, "dp", [(i, i ^ (1 << bit)) for i in range(n_dp)])

    def across_core(x):
        return across_bit(x, 0)

    def swap_if(flag, a, b, axis):
        return jnp.where(flag, jnp.concatenate([b, a], axis), jnp.concatenate([a, b], axis))

    def my_bit(bit):
        return (place >> bit) & 1

    marks = []

    def run(kernel, name, operands, outs, scratch, mib, flops, after=()):
        results = call(
            kernel,
            name,
            [(ids, IN_SMEM)] + [a if isinstance(a, tuple) else (a, IN_VMEM) for a in operands],
            outs,
            scratch,
            mib,
            flops,
            [*marks[-1:], *after],
        )
        marks.append(results[-1])
        return results[:-1]

    def tie(x, *others):
        return lax.optimization_barrier((x, *others))[0]

    def later(x):
        return lax.optimization_barrier((x, marks[-1]))[0]

    token = shape((rows, width), BF)
    token32 = shape((rows, width), F32)
    half_token = shape((rows, half), BF)
    wide_token = shape((rows, width + half), BF)
    sums = shape((8, width), F32)
    work = 2 * rows * width * width

    hidden = mirror(hidden_in[0])
    skip_a, skip_b = run(
        pack_kernel,
        "pack",
        [(skip_in[0], IN_ANY)],
        [half_token, half_token],
        [pltpu.VMEM((2 * rows, half), BF), pltpu.SemaphoreType.DMA((1,))],
        0,
        work // 100,
    )
    skip_a = mirror(skip_a)
    skip_b = lax.ppermute(skip_b, ("dp", "seq"), turn_perm)

    if piece % GAP == 0 and piece <= 2 * LANES - 7 * GAP:
        w1, w2, b1 = run(
            functools.partial(gather_kernel, pairs),
            "gather",
            [w_fc1, (w_fc2.reshape(4 * pairs, piece, width), IN_HBM), fc1_bias.reshape(ff // LANES, LANES)],
            [shape((width, quarter), BF), shape((pairs, piece, width), BF), shape((8, quarter), F32)],
            [pltpu.SemaphoreType.DMA((pairs,))],
            GATHER_MIB,
            work // 100,
        )
    else:
        w1 = pick(pick(w_fc1.reshape(width, pairs, 2, 2, piece), core, 2), seq, 2).reshape(width, quarter)
        b1 = pick(pick(fc1_bias.reshape(pairs, 2, 2, piece), core, 1), seq, 1).reshape(1, quarter)
        b1 = jnp.broadcast_to(b1, (8, quarter))
        w2 = pick(pick(w_fc2.reshape(pairs, 2, 2, piece, width), core, 1), seq, 1)
    w2 = w2.reshape(quarter, width)

    g_home, sum_grad_out = run(
        grad_out_kernel,
        "grad_out",
        [(timesteps, IN_SMEM), (counts, IN_SMEM), cotangent[0]],
        [token, sums],
        [],
        0,
        work // 100,
    )

    merged, early_a, early, q, kv = run(
        first_kernel,
        "first",
        [hidden, skip_a, skip_b, w_skip, w_qkv, gains, biases],
        [token32, wide_token, wide_token, token, shape((rows, 2 * width), BF)],
        [],
        0,
        5 * work,

    )
    kv_other = across_core(kv)
    g_far = across_seq(g_home)
    g_other = across_core(g_home)

    key_buf = pltpu.VMEM((2 * pitch, width), BF)
    proj_buf = [pltpu.VMEM((width, width), BF), pltpu.SemaphoreType.DMA((1,))]
    early_b, after_attn, normed_two, log_total = run(
        attend_kernel,
        "attend",
        [q, kv, kv_other, merged, early, (w_proj, IN_ANY), gains, biases],
        [shape((rows, 2 * width + half), BF), token32, token, shape((rows, LANES), F32)],
        [key_buf, key_buf, *proj_buf],
        0,
        2 * work,
    )

    n_far = across_seq(normed_two)
    n_other = across_core(normed_two)
    g_other_far = across_core(later(g_far))

    def mlp(name, n0, n1, *g):
        tall = shape((2 * pitch, quarter), BF)
        wide = shape((2 * pitch, width), BF)
        return run(
            mlp_kernel,
            name,
            [n0, n1, *g, w1, b1, w2],
            [tall, tall, wide, wide, token32, token, shape((8, quarter), F32)],
            [pltpu.VMEM((2 * pitch, 3 * LANES), F32), pltpu.VMEM((2 * pitch, 3 * LANES), F32)],
            0,
            6 * 2 * rows * width * quarter,
        )

    act_own, gi_own, nn_own, gg_own, gn_own, gn_own_core, si_own = mlp(
        "mlp_own", normed_two, n_other, g_home, g_other_far, g_far, g_other
    )
    n_other_far = across_core(later(n_far))
    early_a_far = across_seq(tie(early_a, n_far))
    act_far, gi_far, nn_far, gg_far, gn_far, gn_far_core, si_far = mlp(
        "mlp_far", n_far, n_other_far, g_other, g_far, g_other_far, g_home
    )
    gn_far_core = across_core(gn_far_core)
    gn_own_core = across_core(gn_own_core)

    def outer(name, products, blocks, bit, shift, riding=None, after=()):
        pieces = PIECES if shift == 0 and n_dp // 2 % PIECES == 0 else 1
        lefts = [sum(n for _, _, n in parts[0][0]) for _, parts in products]
        rows_of = [n // blocks for n in lefts]
        inside = all(r % 4 == 0 for r in rows_of)
        cols = products[0][0]
        stride = (1 << (bit - shift)) if inside else 0
        scratch, operands = [], []
        for n, (c, parts) in zip(lefts, products):
            height = -(-parts[0][0][0][0].shape[0] // GAP) * GAP * len(parts)
            scratch += [pltpu.VMEM((n, c), F32), pltpu.VMEM((height, n), BF), pltpu.VMEM((height, c), BF)]
            for left, (right, _) in parts:
                operands += [x for x, _, _ in left] + [right]
        r = sum(rows_of)
        if inside:
            outs = [shape((blocks // 2, r, cols), BF)] + [shape((blocks // 2 // pieces, r, cols), BF)] * pieces
        else:
            outs = [shape((n, cols), BF) for n in lefts]
        layout = [[([span for _, *span in left], right[1]) for left, right in parts] for _, parts in products]
        if riding is not None:
            outs = [outs[0], *[shape((blocks // 2 // pieces, r, cols + extra), BF)] * pieces, shape((r, extra), F32)]
            operands.append(riding)
        results = run(
            functools.partial(outer_kernel if riding is None else ride_outer_kernel, stride, bit, layout, pieces),
            name,
            operands,
            outs,
            scratch,
            0,
            sum(2 * n * cols * 4 * rows for n in lefts),
            after,
        )
        if inside:
            return results[0], results[1 : 1 + pieces], results[1 + pieces :]
        whole = jnp.concatenate([x.reshape(blocks, r, cols) for x, r in zip(results, rows_of)], 1)
        whole = whole.reshape(blocks >> (bit - shift + 1), 2, 1 << (bit - shift), sum(rows_of), cols)
        flat_shape = (blocks // 2, sum(rows_of), cols)
        keep, send = [pick(whole, i, 1).reshape(flat_shape) for i in (my_bit(bit), 1 - my_bit(bit))]
        return keep, [send], []

    def combine(name, keep, gots, left, bit, riding=(), after=()):
        count, r, cols = keep.shape
        stride = 1 << left.index(bit)
        if r % 4 == 0:
            results = run(
                functools.partial(ride_combine_kernel if riding else combine_kernel, stride, bit),
                name,
                [keep, *riding, *gots],
                [shape((count // 2, r, cols), BF), shape((count // 2, r, gots[0].shape[2]), BF)]
                + [shape(x.shape, F32) for x in riding],
                [],
                0,
                work // 100,
                after,
            )
            return results[0], [results[1]], results[2:]
        both = (keep.astype(F32) + gots[0].astype(F32)).astype(BF).reshape(count // (2 * stride), 2, stride, r, cols)
        keep, send = [pick(both, i, 1).reshape(count // 2, r, cols) for i in (my_bit(bit), 1 - my_bit(bit))]
        return keep, [send], []

    class Chain:
        def __init__(self, name, order, parts):
            self.name, self.order = name, order
            self.keep, sends, self.riding = parts
            self.step = 0
            self.left = sorted(order[1:])
            self.got = [across_bit(send, order[0]) for send in sends]

        def advance(self, *after):
            self.step += 1
            if self.step >= len(self.order):
                return
            bit = self.order[self.step]
            self.keep, sends, self.riding = combine(
                f"{self.name}_{self.step}", self.keep, self.got, self.left, bit, self.riding, after
            )
            self.left.remove(bit)
            self.got = [across_bit(send, bit) for send in sends]

    def order_of(first):
        return first + list(range(4, bits))

    def add(name, out, *terms):
        return run(add_kernel, name, list(terms), [out], [], 0, work // 100)[0]

    fc2 = Chain(
        "fc2",
        order_of([1, 2, 3]),
        outer("outer_fc2", [(width, [([(act_own, 0, quarter)], (gg_own, 0)), ([(act_far, 0, quarter)], (gg_far, 0))])], pairs, 1, 1),
    )
    gn_far = across_seq(add("gn_add", token, gn_far, gn_far_core))
    fc1 = Chain(
        "fc1",
        order_of([2, 1, 3]),
        outer("outer_fc1", [(width, [([(gi_own, 0, quarter)], (nn_own, 0)), ([(gi_far, 0, quarter)], (nn_far, 0))])], pairs, 2, 1, None, (early_a_far,)),
    )

    split = width // n_dp
    extra = -half % LANES
    rides = 3 * split % 8 == 0 and extra and 3 * split * extra == 12 * width
    early_b_far = across_seq(tie(early_b, gn_far))
    grad_after, ga_own, ga_far, grad_q, gkv_own, gk_other, gv_other, sums_two = run(
        attend_back_kernel,
        "attend_back",
        [gn_own, gn_own_core, gn_far, g_home, g_other_far, after_attn, q, kv, kv_other, log_total]
        + [(w_proj, IN_ANY), gains],
        [token32, half_token, half_token, token]
        + [shape((rows, 2 * width), F32), token, token, sums],
        [key_buf, key_buf, proj_buf[0], pltpu.VMEM((2 * pitch, width), F32), pltpu.VMEM((2 * pitch, width), F32), proj_buf[1]],
        0,
        3 * work,
    )
    gk_core, gv_core = across_core(gk_other), across_core(gv_other)
    even = 3 * split % 8 == 0
    if even:
        gkv, project_own, late = run(
            functools.partial(project_kernel, n_dp),
            "project",
            [grad_q, gkv_own, gk_core, gv_core],
            [shape((rows, 2 * width), BF), wide_token, wide_token],
            [],
            0,
            work // 100,
        )
        third_cols, normed, normed_far = width, early_b, early_b_far
    else:
        gkv = (gkv_own + jnp.concatenate([gk_core, gv_core], 1).astype(F32)).astype(BF)
        project_own = jnp.concatenate([grad_q, gkv], 1)
        late = project_own
        third_cols = half
        normed, normed_far = [
            lax.dynamic_slice_in_dim(x, seq * half, half, 1) for x in (early_b, early_b_far)
        ]
    third_wide = project_own.shape[1]
    late_far = across_seq(late)
    gm_own, gm_far, grad_hidden, back_a, back_b, small = run(
        last_kernel,
        "last",
        [grad_q, gkv, merged, grad_after, w_skip, w_qkv, gains, sums_two, sum_grad_out, si_own, si_far, ga_far],
        [half_token, shape((pitch + 16, width), BF), token, half_token, half_token, shape((16, width), F32)],
        [],
        0,
        5 * work,
    )
    gm_far = across_seq(gm_far)

    fc2.advance(early_b_far)
    out_own, out_far, out_own_core, out_far_core = run(
        lambda ids, *refs: mlp_out_kernel(*refs),
        "mlp_out",
        [act_own, act_far, w2],
        [token32, token32, token, token],
        [],
        0,
        2 * 4 * rows * width * quarter,
    )
    out_own_core, out_far_core = across_core(out_own_core), across_core(out_far_core)
    fc1.advance()
    third = Chain(
        "third",
        order_of([0, 2, 1, 3]),
        outer(
            "outer_third",
            [
                (
                    third_cols,
                    [
                        ([(project_own, 0, third_wide)], (normed, 0)),
                        ([(late_far, 0, third_wide)], (normed_far, 0)),
                    ],
                )
            ],
            n_dp,
            0,
            0,
        ),
    )
    second = Chain(
        "second",
        order_of([0, 1, 2, 3]),
        outer(
            "outer_second",
            [
                (half, [([(early_b, width, width)], (ga_own, 0)), ([(early_b_far, width, width)], (gm_far, 0))]),
                (
                    half,
                    [
                        ([(early_a, 0, width + half), (early_b, 2 * width, half)], (gm_own, 0)),
                        ([(early_a_far, 0, width + half), (early_b_far, 2 * width, half)], (gm_far, half)),
                    ],
                ),
            ],
            n_dp,
            0,
            0,
            small if rides else None,
        ),
    )
    third.advance()
    second.advance()
    fc2.advance()
    fc1.advance()
    out_far = across_seq(add("out_add", token, out_far, out_far_core))
    back = run(
        result_kernel,
        "result",
        [biases, grad_hidden, back_a, after_attn, out_own, out_own_core, out_far],
        [shape((rows, 2 * width + half), BF)],
        [],
        0,
        work // 100,
    )[0]
    back = mirror(back)
    back_b = lax.ppermute(later(back_b), ("dp", "seq"), turn_back_perm)
    if not rides:
        small = small[:12]
        small = small + across_seq(small)
        for bit in range(bits):
            small = small + across_bit(small, bit)
    third.advance()
    while fc2.step + 1 < len(fc2.order):
        fc2.advance()
        fc1.advance()
    own, far = run(
        half_kernel,
        "half",
        [fc2.keep, *fc2.got, fc1.keep, *fc1.got],
        [shape((2, piece, half), F32), shape((2, piece, half), BF)],
        [],
        0,
        work // 100,
    )
    far = across_seq(far)
    second.advance()
    output, grad_hidden, grad_skip = run(
        home_kernel,
        "home",
        [(counts, IN_SMEM), back, back_b],
        [token, token, shape((2 * rows, half), BF)],
        [],
        0,
        work // 100,
    )
    while third.step + 1 < len(third.order):
        third.advance()
    while second.step + 1 < len(second.order):
        second.advance()
    out_w_fc2, out_w_fc1 = run(
        join_ff_kernel,
        "join_ff",
        [own, far],
        [shape((2 * piece, half), F32)] * 2,
        [],
        0,
        work // 100,
    )
    if even:
        third_rows = 3 * split // 2
        third_own, third_far = run(
            third_half_kernel,
            "third_half",
            [third.keep, *third.got],
            [shape((third_rows, half), F32), shape((third_rows, half), BF)],
            [],
            0,
            work // 100,
        )
        third_far = across_seq(third_far)
    ends = [shape((split, half), F32), shape((2 * split, half), F32)]
    if rides:
        out_w_proj, out_w_skip, grad_gains, grad_biases, grad_fc1_bias = run(
            functools.partial(ride_ends_kernel, split, pairs),
            "ends",
            [second.keep, *second.got, *second.riding],
            ends + [shape((2, width), F32), shape((5, width), F32), shape((ff // LANES, LANES), F32)],
            [pltpu.VMEM((16, width), F32), pltpu.VMEM((8, ff), F32)],
            0,
            work // 100,
        )
        grad_fc1_bias = grad_fc1_bias.reshape(ff)
    else:
        out_w_proj, out_w_skip = run(
            functools.partial(ends_kernel, split), "ends", [second.keep, *second.got], ends, [], 0, work // 100
        )
        grad_gains, grad_biases = small[:2], small[2:7]
        grad_fc1_bias = small[7:11].reshape(2, 2, pairs, piece).transpose(2, 0, 1, 3).reshape(ff)
    if even:
        (out_w_qkv,) = run(
            third_join_kernel,
            "third_join",
            [third_own, third_far],
            [shape((2 * third_rows, half), F32)],
            [],
            0,
            work // 100,
        )
    else:
        out_w_qkv = (third.keep[0].astype(F32) + third.got[0][0].astype(F32)).T
    out_w_fc1 = out_w_fc1.T
    if even:
        out_w_qkv = out_w_qkv.T
    return (
        output[None],
        grad_hidden[None],
        grad_skip[None],
        out_w_skip,
        out_w_qkv,
        out_w_proj,
        out_w_fc1,
        out_w_fc2,
        grad_gains,
        grad_biases,
        grad_fc1_bias,
    )


def solution(mesh):
    return jax.shard_map(
        shards,
        mesh=mesh,
        in_specs=(
            P("dp", "seq", None),
            P("dp", None, "seq"),
            P("dp", "seq", None),
            P("dp"),
            P("dp"),
            P(),
            P(),
            P(),
            P(),
            P(),
            P(),
            P(),
            P(),
        ),
        out_specs=(
            P("dp", "seq", None),
            P("dp", "seq", None),
            P("dp", None, "seq"),
            P("dp", "seq"),
            P("seq", "dp"),
            P("dp", "seq"),
            P("seq", "dp"),
            P("dp", "seq"),
            P(),
            P(),
            P(),
        ),
        check_vma=False,
    )
```

```python
import functools

import jax
import jax.numpy as jnp
from jax import lax
from jax.experimental import pallas as pl
from jax.experimental.pallas import tpu as pltpu
from jax.sharding import PartitionSpec as P

HEADS = 16
PADDED = 2
TSTEPS = 1000

EPSILON = 1e-06
NEG_FILL = -1e30
BF = jnp.bfloat16
F32 = jnp.float32
MIB = 1 << 20
LANES = 128
GAP = 16


def dot(left, right, dims):
    return lax.dot_general(left, right, ((dims[:1], dims[1:]), ((), ())), preferred_element_type=F32)


def norm(value):
    center = value - jnp.mean(value, axis=-1, keepdims=True)
    rstd = lax.rsqrt(jnp.mean(center * center, axis=-1, keepdims=True) + EPSILON)
    return center * rstd, rstd


def norm_back(grad, xhat, rstd, gain):
    scaled = grad * gain
    return rstd * (
        scaled
        - jnp.mean(scaled, axis=-1, keepdims=True)
        - xhat * jnp.mean(scaled * xhat, axis=-1, keepdims=True)
    )


def pick(array, index, axis):
    return lax.dynamic_index_in_dim(array, index, axis, keepdims=False)


def shape(dims, dtype):
    return jax.ShapeDtypeStruct(dims, dtype)


def padded(dims, dtype):
    dims = (1,) * (2 - len(dims)) + tuple(dims)
    size = -(-dims[-2] // 16) * 16 * -(-dims[-1] // LANES) * LANES
    for dim in dims[:-2]:
        size *= dim
    return size * jnp.dtype(dtype).itemsize


COMPUTE = ("gather",)
PIECES = 1
UNROLL = True
GATHER_MIB = 34
SCALE = 0.3
TAKES = {
    "pack": 12.0,
    "gather": 8.0,
    "first": 4.4,
    "attend": 6.6,
    "mlp": 6.0,
    "outer": 3.2,
    "attend_back": 10.3,
    "last": 6.3,
    "outer_second": 0.3,
    "outer_third": 0.3,
    "third": 0.3,
    "second": 0.3,
    "fc1": 0.3,
    "fc2": 0.3,
}


IN_VMEM = pl.BlockSpec(memory_space=pltpu.VMEM)
IN_SMEM = pl.BlockSpec(memory_space=pltpu.SMEM)
IN_ANY = pl.BlockSpec(memory_space=pl.ANY)
IN_HBM = pl.BlockSpec(memory_space=pltpu.HBM)


def call(kernel, name, operands, outs, scratch, mib, flops, after=()):
    takes = TAKES.get(name, TAKES.get(name.split("_")[0], 1.0)) * SCALE
    outs = [*outs, shape((8, LANES), F32)]
    inputs = len(operands)
    marks = len(after)
    if not mib:
        need = sum(padded(a.shape, a.dtype) for a, spec in operands if spec is IN_VMEM)
        need += sum(padded(o.shape, o.dtype) for o in outs)
        need += sum(padded(b.shape, b.dtype) for b in scratch if b.memory_space == pltpu.VMEM)
        mib = need * 9 // 8 // MIB + 4

    def body(*refs):
        mark = refs[inputs + marks + len(outs) - 1]
        mark[...] = jnp.zeros_like(mark)
        kernel(*refs[:inputs], *refs[inputs + marks : inputs + marks + len(outs) - 1], *refs[inputs + marks + len(outs) :])

    return pl.pallas_call(
        body,
        out_shape=outs,
        in_specs=[spec for _, spec in operands] + [IN_ANY] * marks,
        out_specs=[IN_VMEM] * len(outs),
        scratch_shapes=scratch,
        compiler_params=pltpu.CompilerParams(vmem_limit_bytes=mib * MIB),
        cost_estimate=pl.CostEstimate(flops=int(takes * 1e9), bytes_accessed=1 if name in COMPUTE else int(takes * 3.6e6), transcendentals=0),
        name=name,
    )(*[a for a, _ in operands], *after)


def fetch(pairs, sems):
    copies = [pltpu.make_async_copy(src, dst, sems.at[i]) for i, (src, dst) in enumerate(pairs)]
    for copy in copies:
        copy.start()
    return copies


def gather_kernel(pieces, ids, w_fc1, w_fc2, bias, w1, w2, b1, sems):
    core, seq = ids[1], ids[0]
    piece_size = w1.shape[1] // pieces
    which = [4 * m + 2 * core + seq for m in range(pieces)]
    spots = [w * piece_size for w in which]
    copies = fetch([(w_fc2.at[w], w2.at[m]) for m, w in enumerate(which)], sems)
    lane = lax.broadcasted_iota(jnp.int32, (8, LANES), 1)
    for m in range(pieces):
        base, into = m * piece_size // LANES * LANES, m * piece_size % LANES
        window = [bias[pl.ds(spots[m] // LANES + i, 1), :] for i in range(2)]
        window = jnp.concatenate([jnp.broadcast_to(x, (8, LANES)) for x in window], 1)
        turn = (into - spots[m] % LANES + 2 * LANES) % (2 * LANES)
        window = pltpu.roll(window, turn, 1)
        left = window[:, :LANES]
        if into:
            left = jnp.where(lane >= into, left, b1[:, base : base + LANES])
        b1[:, base : base + LANES] = left
        b1[:, base + LANES : base + 2 * LANES] = window[:, LANES:]
    source = lax.broadcasted_iota(jnp.int32, (2 * LANES, 2 * LANES), 0)
    target = lax.broadcasted_iota(jnp.int32, (2 * LANES, 2 * LANES), 1)
    before = {}
    for m in range(pieces):
        base = m * piece_size // LANES * LANES
        column = target + (base - m * piece_size)
        take = jnp.logical_and(column >= 0, column < piece_size)
        take = jnp.logical_and(take, source == column + spots[m] % LANES)
        window = pl.ds(pl.multiple_of(spots[m] // LANES * LANES, LANES), 2 * LANES)
        part = dot(w_fc1[:, window], take.astype(F32).astype(BF), (1, 0))
        for at, half in ((base, part[:, :LANES]), (base + LANES, part[:, LANES:])):
            before[at] = before[at] + half if at in before else half
        for at in [x for x in before if x <= base]:
            w1[:, at : at + LANES] = before.pop(at).astype(BF)
    for at, half in before.items():
        w1[:, at : at + LANES] = half.astype(BF)
    for copy in copies:
        copy.wait()


def pack_kernel(ids, skip_in, skip_a, skip_b, skip, sems):
    rows = skip_a.shape[0]
    seq = ids[0]
    fetch([(skip_in, skip)], sems)[0].wait()
    whole = skip[...].astype(F32)
    top, bottom = whole[:rows], whole[rows:]
    skip_a[...] = jnp.where(seq == 0, top, bottom).astype(BF)
    skip_b[...] = jnp.where(seq == 0, bottom, top).astype(BF)


def grad_out_kernel(ids, timesteps, counts, cotangent, g_home, sums):
    rows, width = g_home.shape
    time = jnp.zeros((1, 1), F32) + timesteps[0].astype(F32)
    weight = jax.nn.sigmoid(12.0 * time / TSTEPS - 6.0)
    spot = lax.broadcasted_iota(jnp.int32, (rows, 1), 0) + ids[0] * rows
    live = jnp.logical_and(spot < 2 * rows - PADDED, counts[0] > 0)
    g = cotangent[...].astype(F32) * jnp.where(live, weight, 0.0)
    g_home[...] = g.astype(BF)
    sums[...] = jnp.concatenate([jnp.sum(g, axis=0, keepdims=True), jnp.zeros((7, width), F32)], 0)


def first_kernel(ids, hidden, skip_a, skip_b, w_skip, w_qkv, gains, biases, merged, early_a, early, q, kv):
    width = hidden.shape[1]
    half = width // 2
    core = ids[1]
    a, b = skip_a[...].astype(F32), skip_b[...].astype(F32)
    low = jnp.where(core == 0, a, b).astype(BF)
    high = jnp.where(core == 0, b, a).astype(BF)
    early_a[:, :half] = low
    early_a[:, half:] = high
    total = dot(hidden[...], w_skip[:width], (1, 0)) + biases[0:1]
    total += dot(low, w_skip[width : width + half], (1, 0))
    total += dot(high, w_skip[width + half :], (1, 0))
    merged[...] = total
    xhat, _ = norm(total)
    one = (xhat * gains[0:1] + biases[1:2]).astype(BF)
    early[...] = one
    kv[...] = dot(one, w_qkv[:, width:], (1, 0)).astype(BF)
    q[...] = dot(one, w_qkv[:, :width], (1, 0)).astype(BF)


def head_windows(width):
    size = width // HEADS
    spans = []
    for h in range(HEADS):
        low, high = h * size, (h + 1) * size
        t0, t1 = low // LANES, (high - 1) // LANES + 1
        spans.append((h, low, high, t0 * LANES, t1 * LANES))
    return spans


def lane_mask(low, high, first, last):
    lane = lax.broadcasted_iota(jnp.int32, (1, last - first), 1) + first
    return jnp.logical_and(lane >= low, lane < high)


def key_mask(core, rows, pitch, axis=1):
    spot = lax.broadcasted_iota(jnp.int32, (1, 2 * pitch) if axis else (2 * pitch, 1), axis)
    other = spot >= pitch
    here = jnp.where(other, spot - pitch, spot)
    last_half = jnp.where(other, 1 - core, core) == 1
    limit = jnp.where(last_half, rows - PADDED, rows)
    return here < limit


def lay_keys(keys, values, kv_own, kv_other, rows, pitch, width):
    for buf, at in ((keys, 0), (values, width)):
        buf[...] = jnp.zeros_like(buf)
        buf[0:rows] = kv_own[:, at : at + width]
        buf[pitch : pitch + rows] = kv_other[:, at : at + width]


def attend_kernel(ids, q, kv_own, kv_other, merged, skips, early, w_proj, gains, biases, early_a, early_b, after, normed, log_total, keys, values, wp, sems):
    rows, width = q.shape
    pitch = keys.shape[0] // 2
    copies = fetch([(w_proj, wp)], sems)
    lay_keys(keys, values, kv_own, kv_other, rows, pitch, width)
    valid = key_mask(ids[1], rows, pitch)
    scale = (width // HEADS) ** (-0.5)
    lane = lax.broadcasted_iota(jnp.int32, (rows, LANES), 1)
    tiles = [jnp.zeros((rows, LANES), F32) for _ in range(width // LANES)]
    logs = jnp.zeros((rows, LANES), F32)
    for h, low, high, first, last in head_windows(width):
        mask = lane_mask(low, high, first, last)
        mine = q[:, first:last] * mask.astype(F32).astype(BF)
        scores = jnp.where(valid, dot(mine, keys[:, first:last], (1, 1)) * scale, NEG_FILL)
        top = jnp.max(scores, axis=-1, keepdims=True)
        expo = jnp.exp(scores - top)
        total = jnp.sum(expo, axis=-1, keepdims=True)
        probs = (expo * (1.0 / total)).astype(BF)
        logs = jnp.where(lane == h, top + jnp.log(total), logs)
        part = dot(probs, values[:, first:last], (1, 0))
        for t in range(first, last, LANES):
            tiles[t // LANES] = jnp.where(
                mask[:, t - first : t - first + LANES], part[:, t - first : t - first + LANES], tiles[t // LANES]
            )
    log_total[...] = logs
    mixed = jnp.concatenate(tiles, 1)
    half = width // 2
    early_a[:, :width] = skips[...]
    early_a[:, width:] = mixed[:, :half].astype(BF)
    early_b[:, :width] = early[...]
    early_b[:, width:] = mixed[:, half:].astype(BF)
    mixed = mixed.astype(BF)
    copies[0].wait()
    value = merged[...] + dot(mixed, wp[...], (1, 0)) + biases[2:3]
    after[...] = value
    xhat, _ = norm(value)
    normed[...] = (xhat * gains[1:2] + biases[3:4]).astype(BF)


def attend_back_kernel(
    ids, gn_mine, gn_core, gn_far, g_home, g_cross, after, q, kv_own, kv_other, log_total, w_proj, gains,
    grad_after, ga_own, ga_far, grad_q, gkv_own, gk_other, gv_other, sums,
    keys, values, wp, gk, gv, sems,
):
    rows, width = q.shape
    half = width // 2
    pitch = keys.shape[0] // 2
    copies = fetch([(w_proj, wp)], sems)
    gn = gn_mine[...] + gn_core[...].astype(F32) + gn_far[...].astype(F32)
    xhat, rstd = norm(after[...])
    g_out = jnp.where(ids[0] == ids[1], g_home[...].astype(F32), g_cross[...].astype(F32))
    value = g_out + norm_back(gn, xhat, rstd, gains[1:2])
    grad_after[...] = value
    low = value.astype(BF)
    halves = value[:, :half], value[:, half:]
    ga_own[...] = jnp.where(ids[0] == 0, halves[0], halves[1]).astype(BF)
    ga_far[...] = jnp.where(ids[0] == 0, halves[1], halves[0]).astype(BF)
    sums[...] = jnp.concatenate(
        [
            jnp.sum(gn * xhat, axis=0, keepdims=True),
            jnp.sum(gn, axis=0, keepdims=True),
            jnp.sum(value, axis=0, keepdims=True),
            jnp.zeros((5, width), F32),
        ],
        0,
    )
    lay_keys(keys, values, kv_own, kv_other, rows, pitch, width)
    valid = key_mask(ids[1], rows, pitch, 0)
    scale = (width // HEADS) ** (-0.5)
    copies[0].wait()
    grad_mixed = dot(low, wp[...], (1, 1)).astype(BF)
    gk[...] = jnp.zeros_like(gk)
    gv[...] = jnp.zeros_like(gv)
    tiles = [jnp.zeros((rows, LANES), F32) for _ in range(width // LANES)]
    logs = log_total[...].T
    for h, start, stop, first, last in head_windows(width):
        mask = lane_mask(start, stop, first, last)
        low_mask = mask.astype(F32).astype(BF)
        mine = q[:, first:last] * low_mask
        gm = grad_mixed[:, first:last] * low_mask
        scores = jnp.where(valid, dot(keys[:, first:last], mine, (1, 1)) * scale, NEG_FILL)
        probs = jnp.exp(scores - logs[h : h + 1, :])
        gp = dot(values[:, first:last], gm, (1, 1))
        gs = (probs * (gp - jnp.sum(gp * probs, axis=0, keepdims=True))).astype(BF)
        part = dot(gs, keys[:, first:last], (0, 0))
        for t in range(first, last, LANES):
            tiles[t // LANES] = jnp.where(
                mask[:, t - first : t - first + LANES], part[:, t - first : t - first + LANES], tiles[t // LANES]
            )
        gk[:, first:last] += dot(gs, mine, (1, 0))
        gv[:, first:last] += dot(probs.astype(BF), gm, (1, 0))
    for t, tile in enumerate(tiles):
        grad_q[:, t * LANES : (t + 1) * LANES] = (tile * scale).astype(BF)
    gkv_own[:, :width] = gk[0:rows] * scale
    gkv_own[:, width:] = gv[0:rows]
    gk_other[...] = (gk[pitch : pitch + rows] * scale).astype(BF)
    gv_other[...] = gv[pitch : pitch + rows].astype(BF)


def lay_rows(buf, blocks):
    rows = blocks[0].shape[0]
    pitch = buf.shape[0] // len(blocks)
    if pitch > rows:
        buf[...] = jnp.zeros_like(buf)
    for i, block in enumerate(blocks):
        buf[i * pitch : i * pitch + rows] = block[...]


def lay_chosen(buf, flag, pairs):
    rows = pairs[0][0].shape[0]
    pitch = buf.shape[0] // len(pairs)
    buf[...] = jnp.zeros_like(buf)
    for way, chosen in enumerate((flag, jnp.logical_not(flag))):

        @pl.when(chosen)
        def _(way=way):
            for i, pair in enumerate(pairs):
                buf[i * pitch : i * pitch + rows] = pair[way][...]


def mlp_kernel(ids, n0, n1, g0a, g0b, g1a, g1b, w1, b1, w2, activ, grad_inner, n_all, g_all, gn_mine, gn_other, sums, inner_v, grad_v):
    rows, width = n0.shape
    units = w1.shape[1]
    lay_rows(n_all, (n0, n1))
    lay_chosen(g_all, ids[0] == ids[1], ((g0a, g0b), (g1a, g1b)))
    height = n_all.shape[0]
    pitch = height // 2
    step = 3 * LANES
    chunk = 48
    root = 0.5**0.5
    bell = (0.5 / jnp.pi) ** 0.5
    for j in range(units // step):
        cols = slice(j * step, (j + 1) * step)
        inner_v[...] = dot(n_all[...], w1[:, cols], (1, 0))
        grad_v[...] = dot(g_all[...], w2[cols, :], (1, 1))
        bias = b1[0:1, cols]

        def body(i, total):
            at = pl.ds(pl.multiple_of(i * chunk, chunk), chunk)
            x = inner_v[at] + bias
            cdf = 0.5 + 0.5 * lax.erf(x * root)
            activ[at, cols] = (x * cdf).astype(BF)
            g = grad_v[at] * (cdf + x * jnp.exp(-0.5 * x * x) * bell)
            grad_inner[at, cols] = g.astype(BF)
            return total + jnp.sum(g, axis=0, keepdims=True)

        sums[0:1, cols] = lax.fori_loop(0, height // chunk, body, jnp.zeros((1, step), F32), unroll=UNROLL)
    for j in range(width // step):
        cols = slice(j * step, (j + 1) * step)
        part = dot(grad_inner[...], w1[cols, :], (1, 1))
        gn_mine[:, cols] = part[:rows]
        gn_other[:, cols] = part[pitch : pitch + rows].astype(BF)


def mlp_out_kernel(activ_own, activ_far, w2, own, far, own_core, far_core):
    rows = own.shape[0]
    pitch = activ_own.shape[0] // 2
    step = 3 * LANES
    for activ, mine, other in ((activ_far, far, far_core), (activ_own, own, own_core)):
        for j in range(w2.shape[1] // step):
            cols = slice(j * step, (j + 1) * step)
            part = dot(activ[...], w2[:, cols], (1, 0))
            mine[:, cols] = part[:rows]
            other[:, cols] = part[pitch : pitch + rows].astype(BF)


def split_blocks(total, keep, sends, at, mine, stride):
    count = keep.shape[0]
    rows = total.shape[0] // (2 * count)
    slot = 0
    for i in range(2 * count):
        if i // stride % 2:
            continue
        a = total[i * rows : (i + 1) * rows]
        b = total[(i + stride) * rows : (i + stride + 1) * rows]
        keep[slot, at : at + rows] = jnp.where(mine == 0, a, b).astype(BF)
        per = sends[0].shape[0]
        sends[slot // per][slot % per, at : at + rows, : keep.shape[2]] = jnp.where(mine == 0, b, a).astype(BF)
        slot += 1


def outer_kernel(stride, bit, layout, pieces, ids, *refs):
    spots = iter(refs)
    operands = [
        [([(next(spots), *span) for span in left], (next(spots), right)) for left, right in parts] for parts in layout
    ]
    outs = [next(spots) for _ in range(1 + pieces if stride else len(layout))]
    at = 0
    for i, parts in enumerate(operands):
        total, left, right = next(spots), next(spots), next(spots)
        pitch = left.shape[0] // len(parts)
        cols = right.shape[1]
        for p, (lefts, (y, first)) in enumerate(parts):
            rows = lefts[0][0].shape[0]
            if pitch > rows:
                left[p * pitch : (p + 1) * pitch] = jnp.zeros((pitch, left.shape[1]), BF)
                right[p * pitch : (p + 1) * pitch] = jnp.zeros((pitch, cols), BF)
            right[p * pitch : p * pitch + rows] = y[:rows, first : first + cols]
            spot = 0
            for x, start, n in lefts:
                left[p * pitch : p * pitch + rows, spot : spot + n] = x[:, start : start + n]
                spot += n
        step = 3 * LANES
        for j in range(0, left.shape[1], step):
            span = slice(j, min(j + step, left.shape[1]))
            total[span, :] = dot(left[:, span], right[...], (0, 0))
        if stride:
            split_blocks(total, outs[0], outs[1:], at, ids[1 + bit], stride)
            at += left.shape[1] // (2 * outs[0].shape[0])
        else:
            outs[i][...] = total[...].astype(BF)


def combine_kernel(stride, bit, ids, keep, *refs):
    gots, kept, send = refs[:-2], refs[-2], refs[-1]
    slot = 0
    cols = keep.shape[2]
    per = gots[0].shape[0]

    def total(i):
        return keep[i].astype(F32) + gots[i // per][i % per, :, :cols].astype(F32)

    for i in range(keep.shape[0]):
        if i // stride % 2:
            continue
        a, b = total(i), total(i + stride)
        kept[slot] = jnp.where(ids[1 + bit] == 0, a, b).astype(BF)
        send[slot, :, :cols] = jnp.where(ids[1 + bit] == 0, b, a).astype(BF)
        slot += 1


def ride_outer_kernel(stride, bit, layout, pieces, ids, *refs):
    inputs = sum(len(left) + 1 for parts in layout for left, _ in parts)
    operands, small, outs, scratch = refs[:inputs], refs[inputs], refs[inputs + 1 : inputs + 3 + pieces], refs[inputs + 3 + pieces :]
    keep, sends, riding = outs[0], outs[1:-1], outs[-1]
    outer_kernel(stride, bit, layout, pieces, ids, *operands, keep, *sends, *scratch)
    far = operands[-1]
    total = small[...] + far[far.shape[0] - 16 :, :].astype(F32)
    cols = keep.shape[2]
    extra = sends[0].shape[2] - cols
    for j in range(small.shape[1] // extra):
        riding[12 * j : 12 * j + 12, :] = total[:12, extra * j : extra * (j + 1)]
    for send in sends:
        send[:, :, cols:] = jnp.zeros((send.shape[0], send.shape[1], extra), BF)
    sends[0][0, :, cols:] = riding[...].astype(BF)


def ride_combine_kernel(stride, bit, ids, keep, riding, *refs):
    gots, (kept, send, rode) = refs[:-3], refs[-3:]
    combine_kernel(stride, bit, ids, keep, *gots, kept, send)
    cols = keep.shape[2]
    total = riding[...] + gots[0][0, :, cols:].astype(F32)
    rode[...] = total
    if send.shape[0] > 1:
        send[1:, :, cols:] = jnp.zeros((send.shape[0] - 1, send.shape[1], send.shape[2] - cols), BF)
    send[0, :, cols:] = total.astype(BF)


def ride_ends_kernel(split, pieces, ids, keep, got, riding, proj, skip, gains, biases, units, buf, line):
    cols = keep.shape[2]
    total = keep[0].astype(F32) + got[0, :, :cols].astype(F32)
    proj[...] = total[:split]
    skip[...] = total[split:]
    extra = riding.shape[1]
    small = riding[...] + got[0, :, cols:].astype(F32)
    for j in range(buf.shape[1] // extra):
        buf[:12, extra * j : extra * (j + 1)] = small[12 * j : 12 * j + 12]
    gains[...] = buf[:2]
    biases[...] = buf[2:7]
    piece = buf.shape[1] // pieces
    for m in range(pieces):
        for i in range(4):
            at = (4 * m + i) * piece
            line[0:1, at : at + piece] = buf[7 + i : 8 + i, piece * m : piece * (m + 1)]
    for t in range(units.shape[0]):
        units[t : t + 1, :] = line[0:1, t * LANES : (t + 1) * LANES]


def add_kernel(ids, *refs):
    total = refs[0][...].astype(F32)
    for ref in refs[1:-1]:
        total += ref[...].astype(F32)
    refs[-1][...] = total.astype(refs[-1].dtype)


def project_kernel(blocks, ids, grad_q, gkv_own, gk_core, gv_core, gkv, own, late):
    total = gkv_own[...] + jnp.concatenate([gk_core[...], gv_core[...]], 1).astype(F32)
    gkv[...] = total.astype(BF)
    whole = jnp.concatenate([grad_q[...].astype(F32), total], 1)
    size = whole.shape[1] // (2 * blocks)
    parts = [
        jnp.concatenate([whole[:, (2 * j + s) * size : (2 * j + s + 1) * size] for j in range(blocks)], 1)
        for s in range(2)
    ]
    own[...] = jnp.where(ids[0] == 0, parts[0], parts[1]).astype(BF)
    late[...] = jnp.where(ids[0] == 0, parts[1], parts[0]).astype(BF)


def result_kernel(ids, biases, grad_hidden, back_a, *refs):
    total = biases[4:5]
    for ref in refs[:-1]:
        total = total + ref[...].astype(F32)
    width = grad_hidden.shape[1]
    refs[-1][:, :width] = total.astype(BF)
    refs[-1][:, width : 2 * width] = grad_hidden[...]
    refs[-1][:, 2 * width :] = back_a[...]


def half_kernel(ids, keep_two, got_two, keep_one, got_one, own, far):
    half = own.shape[2]
    for i, (keep, got) in enumerate(((keep_two, got_two), (keep_one, got_one))):
        total = keep[0].astype(F32) + got[0].astype(F32)
        left, right = total[:, :half], total[:, half:]
        own[i] = jnp.where(ids[0] == 0, left, right)
        far[i] = jnp.where(ids[0] == 0, right, left).astype(BF)


def join_ff_kernel(ids, own, far, *outs):
    rows = own.shape[1]
    for i, out in enumerate(outs):
        here, there = own[i], far[i].astype(F32)
        out[:rows] = jnp.where(ids[0] == 0, here, there)
        out[rows:] = jnp.where(ids[0] == 0, there, here)


def ends_kernel(split, ids, keep_two, got_two, proj, skip):
    total = keep_two[0].astype(F32) + got_two[0].astype(F32)
    proj[...] = total[:split]
    skip[...] = total[split:]


def third_half_kernel(ids, keep, got, own, far):
    half = own.shape[1]
    total = keep[0].astype(F32) + got[0].astype(F32)
    left, right = total[:, :half], total[:, half:]
    own[...] = jnp.where(ids[0] == 0, left, right)
    far[...] = jnp.where(ids[0] == 0, right, left).astype(BF)


def third_join_kernel(ids, own, far, out):
    here, there = own[...], far[...].astype(F32)
    rows = own.shape[0]
    out[:rows] = jnp.where(ids[0] == 0, here, there)
    out[rows:] = jnp.where(ids[0] == 0, there, here)


def home_kernel(ids, counts, back, back_b, output, grad_hidden, grad_skip):
    rows, width = output.shape
    grad_hidden[...] = back[:, width : 2 * width]
    seq = ids[0]
    spot = lax.broadcasted_iota(jnp.int32, (rows, 1), 0) + seq * rows
    live = jnp.logical_and(spot < 2 * rows - PADDED, counts[0] > 0)
    output[...] = jnp.where(live, back[:, :width].astype(F32), 0.0).astype(BF)
    a, b = back[:, 2 * width :].astype(F32), back_b[...].astype(F32)
    grad_skip[:rows] = jnp.where(seq == 0, a, b).astype(BF)
    grad_skip[rows:] = jnp.where(seq == 0, b, a).astype(BF)


def last_kernel(
    ids, grad_q, gkv, merged, grad_after, w_skip, w_qkv, gains, sums_two, sums_out, units_own, units_far, ga_far,
    gm_own, gm_far, grad_hidden, back_a, back_b, small,
):
    width = merged.shape[1]
    half = width // 2
    xhat, rstd = norm(merged[...])
    gn = dot(grad_q[...], w_qkv[:, :width], (1, 1))
    gn += dot(gkv[...], w_qkv[:, width:], (1, 1))
    value = grad_after[...] + norm_back(gn, xhat, rstd, gains[0:1])
    units = units_own[0:1] + units_far[0:1]
    spot = 2 * ids[1] + ids[0]
    sums = jnp.concatenate(
        [
            jnp.sum(gn * xhat, axis=0, keepdims=True),
            sums_two[0:1],
            jnp.sum(value, axis=0, keepdims=True),
            jnp.sum(gn, axis=0, keepdims=True),
            sums_two[2:3],
            sums_two[1:2],
            sums_out[0:1],
        ]
        + [jnp.where(spot == i, units, 0.0) for i in range(4)]
        + [jnp.zeros((5, width), F32)],
        0,
    )
    small[...] = sums
    halves = value[:, :half], value[:, half:]
    rows = value.shape[0]
    gm_own[...] = jnp.where(ids[0] == 0, halves[0], halves[1]).astype(BF)
    gm_far[:rows, :half] = ga_far[...]
    gm_far[:rows, half:] = jnp.where(ids[0] == 0, halves[1], halves[0]).astype(BF)
    gm_far[gm_far.shape[0] - 16 :] = sums.astype(BF)
    low = value.astype(BF)
    grad_hidden[...] = dot(low, w_skip[:width], (1, 1)).astype(BF)
    a = dot(low, w_skip[width : width + half], (1, 1))
    b = dot(low, w_skip[width + half :], (1, 1))
    back_a[...] = jnp.where(ids[1] == 0, a, b).astype(BF)
    back_b[...] = jnp.where(ids[1] == 0, b, a).astype(BF)


def shards(
    hidden_in,
    skip_in,
    cotangent,
    timesteps,
    counts,
    w_skip,
    w_qkv,
    w_proj,
    w_fc1,
    w_fc2,
    gains,
    biases,
    fc1_bias,
):
    rows, width = hidden_in.shape[1:]
    half = width // 2
    ff = w_fc1.shape[1]
    n_dp = lax.axis_size("dp")
    bits = n_dp.bit_length() - 1
    pairs = n_dp // 2
    place = lax.axis_index("dp")
    core = place % 2
    seq = lax.axis_index("seq")
    piece = ff // (4 * pairs)
    quarter = pairs * piece
    ids = jnp.stack([seq] + [(place >> b) & 1 for b in range(bits)]).astype(jnp.int32)
    ids = lax.optimization_barrier(ids)
    pitch = -(-rows // GAP) * GAP

    def flat(dp, s):
        return 2 * dp + s

    mirror_perm = [
        (flat(2 * k + c, s), flat(2 * k + s, c)) for k in range(pairs) for c in range(2) for s in range(2)
    ]
    turn = {(0, 0): (1, 0), (1, 0): (1, 1), (1, 1): (0, 1), (0, 1): (0, 0)}
    turn_perm = [
        (flat(2 * k + c, s), flat(2 * k + d[0], d[1])) for k in range(pairs) for (c, s), d in turn.items()
    ]
    turn_back_perm = [(b, a) for a, b in turn_perm]

    def mirror(x):
        return lax.ppermute(x, ("dp", "seq"), mirror_perm)

    def across_seq(x):
        return lax.ppermute(x, "seq", [(0, 1), (1, 0)])

    def across_bit(x, bit):
        return lax.ppermute(x, "dp", [(i, i ^ (1 << bit)) for i in range(n_dp)])

    def across_core(x):
        return across_bit(x, 0)

    def swap_if(flag, a, b, axis):
        return jnp.where(flag, jnp.concatenate([b, a], axis), jnp.concatenate([a, b], axis))

    def my_bit(bit):
        return (place >> bit) & 1

    marks = []

    def run(kernel, name, operands, outs, scratch, mib, flops, after=()):
        results = call(
            kernel,
            name,
            [(ids, IN_SMEM)] + [a if isinstance(a, tuple) else (a, IN_VMEM) for a in operands],
            outs,
            scratch,
            mib,
            flops,
            [*marks[-1:], *after],
        )
        marks.append(results[-1])
        return results[:-1]

    def tie(x, *others):
        return lax.optimization_barrier((x, *others))[0]

    def later(x):
        return lax.optimization_barrier((x, marks[-1]))[0]

    token = shape((rows, width), BF)
    token32 = shape((rows, width), F32)
    half_token = shape((rows, half), BF)
    wide_token = shape((rows, width + half), BF)
    sums = shape((8, width), F32)
    work = 2 * rows * width * width

    hidden = mirror(hidden_in[0])
    far_perm = [
        (flat(2 * k + c, s), flat(2 * k + s, 1 - c)) for k in range(pairs) for c in range(2) for s in range(2)
    ]
    hidden_far = lax.ppermute(hidden_in[0], ("dp", "seq"), far_perm)
    skip_a, skip_b = run(
        pack_kernel,
        "pack",
        [(skip_in[0], IN_ANY)],
        [half_token, half_token],
        [pltpu.VMEM((2 * rows, half), BF), pltpu.SemaphoreType.DMA((1,))],
        0,
        work // 100,
    )
    skip_a = mirror(skip_a)
    skip_b = lax.ppermute(skip_b, ("dp", "seq"), turn_perm)

    if piece % GAP == 0 and piece <= 2 * LANES - 7 * GAP:
        w1, w2, b1 = run(
            functools.partial(gather_kernel, pairs),
            "gather",
            [w_fc1, (w_fc2.reshape(4 * pairs, piece, width), IN_HBM), fc1_bias.reshape(ff // LANES, LANES)],
            [shape((width, quarter), BF), shape((pairs, piece, width), BF), shape((8, quarter), F32)],
            [pltpu.SemaphoreType.DMA((pairs,))],
            GATHER_MIB,
            work // 100,
        )
    else:
        w1 = pick(pick(w_fc1.reshape(width, pairs, 2, 2, piece), core, 2), seq, 2).reshape(width, quarter)
        b1 = pick(pick(fc1_bias.reshape(pairs, 2, 2, piece), core, 1), seq, 1).reshape(1, quarter)
        b1 = jnp.broadcast_to(b1, (8, quarter))
        w2 = pick(pick(w_fc2.reshape(pairs, 2, 2, piece, width), core, 1), seq, 1)
    w2 = w2.reshape(quarter, width)

    g_home, sum_grad_out = run(
        grad_out_kernel,
        "grad_out",
        [(timesteps, IN_SMEM), (counts, IN_SMEM), cotangent[0]],
        [token, sums],
        [],
        0,
        work // 100,
    )

    merged, skips, early, q, kv = run(
        first_kernel,
        "first",
        [hidden, skip_a, skip_b, w_skip, w_qkv, gains, biases],
        [token32, token, token, token, shape((rows, 2 * width), BF)],
        [],
        0,
        5 * work,
        (hidden_far,),

    )
    kv_other = across_core(kv)
    g_far = across_seq(g_home)
    g_other = across_core(g_home)

    key_buf = pltpu.VMEM((2 * pitch, width), BF)
    proj_buf = [pltpu.VMEM((width, width), BF), pltpu.SemaphoreType.DMA((1,))]
    early_a, early_b, after_attn, normed_two, log_total = run(
        attend_kernel,
        "attend",
        [q, kv, kv_other, merged, skips, early, (w_proj, IN_ANY), gains, biases],
        [wide_token, wide_token, token32, token, shape((rows, LANES), F32)],
        [key_buf, key_buf, *proj_buf],
        0,
        2 * work,
    )

    n_far = across_seq(normed_two)
    n_other = across_core(normed_two)
    g_other_far = across_core(later(g_far))

    def mlp(name, n0, n1, *g):
        tall = shape((2 * pitch, quarter), BF)
        wide = shape((2 * pitch, width), BF)
        return run(
            mlp_kernel,
            name,
            [n0, n1, *g, w1, b1, w2],
            [tall, tall, wide, wide, token32, token, shape((8, quarter), F32)],
            [pltpu.VMEM((2 * pitch, 3 * LANES), F32), pltpu.VMEM((2 * pitch, 3 * LANES), F32)],
            0,
            6 * 2 * rows * width * quarter,
        )

    act_own, gi_own, nn_own, gg_own, gn_own, gn_own_core, si_own = mlp(
        "mlp_own", normed_two, n_other, g_home, g_other_far, g_far, g_other
    )
    n_other_far = across_core(later(n_far))
    early_a_far = across_seq(tie(early_a, n_far))
    act_far, gi_far, nn_far, gg_far, gn_far, gn_far_core, si_far = mlp(
        "mlp_far", n_far, n_other_far, g_other, g_far, g_other_far, g_home
    )
    gn_far_core = across_core(gn_far_core)
    gn_own_core = across_core(gn_own_core)

    def outer(name, products, blocks, bit, shift, riding=None, after=()):
        pieces = PIECES if shift == 0 and n_dp // 2 % PIECES == 0 else 1
        lefts = [sum(n for _, _, n in parts[0][0]) for _, parts in products]
        rows_of = [n // blocks for n in lefts]
        inside = all(r % 4 == 0 for r in rows_of)
        cols = products[0][0]
        stride = (1 << (bit - shift)) if inside else 0
        scratch, operands = [], []
        for n, (c, parts) in zip(lefts, products):
            height = -(-parts[0][0][0][0].shape[0] // GAP) * GAP * len(parts)
            scratch += [pltpu.VMEM((n, c), F32), pltpu.VMEM((height, n), BF), pltpu.VMEM((height, c), BF)]
            for left, (right, _) in parts:
                operands += [x for x, _, _ in left] + [right]
        r = sum(rows_of)
        if inside:
            outs = [shape((blocks // 2, r, cols), BF)] + [shape((blocks // 2 // pieces, r, cols), BF)] * pieces
        else:
            outs = [shape((n, cols), BF) for n in lefts]
        layout = [[([span for _, *span in left], right[1]) for left, right in parts] for _, parts in products]
        if riding is not None:
            outs = [outs[0], *[shape((blocks // 2 // pieces, r, cols + extra), BF)] * pieces, shape((r, extra), F32)]
            operands.append(riding)
        results = run(
            functools.partial(outer_kernel if riding is None else ride_outer_kernel, stride, bit, layout, pieces),
            name,
            operands,
            outs,
            scratch,
            0,
            sum(2 * n * cols * 4 * rows for n in lefts),
            after,
        )
        if inside:
            return results[0], results[1 : 1 + pieces], results[1 + pieces :]
        whole = jnp.concatenate([x.reshape(blocks, r, cols) for x, r in zip(results, rows_of)], 1)
        whole = whole.reshape(blocks >> (bit - shift + 1), 2, 1 << (bit - shift), sum(rows_of), cols)
        flat_shape = (blocks // 2, sum(rows_of), cols)
        keep, send = [pick(whole, i, 1).reshape(flat_shape) for i in (my_bit(bit), 1 - my_bit(bit))]
        return keep, [send], []

    def combine(name, keep, gots, left, bit, riding=(), after=()):
        count, r, cols = keep.shape
        stride = 1 << left.index(bit)
        if r % 4 == 0:
            results = run(
                functools.partial(ride_combine_kernel if riding else combine_kernel, stride, bit),
                name,
                [keep, *riding, *gots],
                [shape((count // 2, r, cols), BF), shape((count // 2, r, gots[0].shape[2]), BF)]
                + [shape(x.shape, F32) for x in riding],
                [],
                0,
                work // 100,
                after,
            )
            return results[0], [results[1]], results[2:]
        both = (keep.astype(F32) + gots[0].astype(F32)).astype(BF).reshape(count // (2 * stride), 2, stride, r, cols)
        keep, send = [pick(both, i, 1).reshape(count // 2, r, cols) for i in (my_bit(bit), 1 - my_bit(bit))]
        return keep, [send], []

    class Chain:
        def __init__(self, name, order, parts):
            self.name, self.order = name, order
            self.keep, sends, self.riding = parts
            self.step = 0
            self.left = sorted(order[1:])
            self.got = [across_bit(send, order[0]) for send in sends]

        def advance(self, *after):
            self.step += 1
            if self.step >= len(self.order):
                return
            bit = self.order[self.step]
            self.keep, sends, self.riding = combine(
                f"{self.name}_{self.step}", self.keep, self.got, self.left, bit, self.riding, after
            )
            self.left.remove(bit)
            self.got = [across_bit(send, bit) for send in sends]

    def order_of(first):
        return first + list(range(4, bits))

    def add(name, out, *terms):
        return run(add_kernel, name, list(terms), [out], [], 0, work // 100)[0]

    fc2 = Chain(
        "fc2",
        order_of([1, 2, 3]),
        outer("outer_fc2", [(width, [([(act_own, 0, quarter)], (gg_own, 0)), ([(act_far, 0, quarter)], (gg_far, 0))])], pairs, 1, 1),
    )
    gn_far = across_seq(add("gn_add", token, gn_far, gn_far_core))
    fc1 = Chain(
        "fc1",
        order_of([2, 1, 3]),
        outer("outer_fc1", [(width, [([(gi_own, 0, quarter)], (nn_own, 0)), ([(gi_far, 0, quarter)], (nn_far, 0))])], pairs, 2, 1, None, (early_a_far,)),
    )

    split = width // n_dp
    extra = -half % LANES
    rides = 3 * split % 8 == 0 and extra and 3 * split * extra == 12 * width
    early_b_far = across_seq(tie(early_b, gn_far))
    grad_after, ga_own, ga_far, grad_q, gkv_own, gk_other, gv_other, sums_two = run(
        attend_back_kernel,
        "attend_back",
        [gn_own, gn_own_core, gn_far, g_home, g_other_far, after_attn, q, kv, kv_other, log_total]
        + [(w_proj, IN_ANY), gains],
        [token32, half_token, half_token, token]
        + [shape((rows, 2 * width), F32), token, token, sums],
        [key_buf, key_buf, proj_buf[0], pltpu.VMEM((2 * pitch, width), F32), pltpu.VMEM((2 * pitch, width), F32), proj_buf[1]],
        0,
        3 * work,
    )
    gk_core, gv_core = across_core(gk_other), across_core(gv_other)
    even = 3 * split % 8 == 0
    if even:
        gkv, project_own, late = run(
            functools.partial(project_kernel, n_dp),
            "project",
            [grad_q, gkv_own, gk_core, gv_core],
            [shape((rows, 2 * width), BF), wide_token, wide_token],
            [],
            0,
            work // 100,
        )
        third_cols, normed, normed_far = width, early_b, early_b_far
    else:
        gkv = (gkv_own + jnp.concatenate([gk_core, gv_core], 1).astype(F32)).astype(BF)
        project_own = jnp.concatenate([grad_q, gkv], 1)
        late = project_own
        third_cols = half
        normed, normed_far = [
            lax.dynamic_slice_in_dim(x, seq * half, half, 1) for x in (early_b, early_b_far)
        ]
    third_wide = project_own.shape[1]
    late_far = across_seq(late)
    gm_own, gm_far, grad_hidden, back_a, back_b, small = run(
        last_kernel,
        "last",
        [grad_q, gkv, merged, grad_after, w_skip, w_qkv, gains, sums_two, sum_grad_out, si_own, si_far, ga_far],
        [half_token, shape((pitch + 16, width), BF), token, half_token, half_token, shape((16, width), F32)],
        [],
        0,
        5 * work,
        (early_b_far,),
    )
    gm_far = across_seq(gm_far)

    fc2.advance()
    out_own, out_far, out_own_core, out_far_core = run(
        lambda ids, *refs: mlp_out_kernel(*refs),
        "mlp_out",
        [act_own, act_far, w2],
        [token32, token32, token, token],
        [],
        0,
        2 * 4 * rows * width * quarter,
    )
    out_own_core, out_far_core = across_core(out_own_core), across_core(out_far_core)
    fc1.advance()
    third = Chain(
        "third",
        order_of([0, 2, 1, 3]),
        outer(
            "outer_third",
            [
                (
                    third_cols,
                    [
                        ([(project_own, 0, third_wide)], (normed, 0)),
                        ([(late_far, 0, third_wide)], (normed_far, 0)),
                    ],
                )
            ],
            n_dp,
            0,
            0,
        ),
    )
    second = Chain(
        "second",
        order_of([0, 1, 2, 3]),
        outer(
            "outer_second",
            [
                (
                    half,
                    [
                        ([(early_a, width, half), (early_b, width, half)], (ga_own, 0)),
                        ([(early_a_far, width, half), (early_b_far, width, half)], (gm_far, 0)),
                    ],
                ),
                (
                    half,
                    [
                        ([(hidden, 0, width), (early_a, 0, width)], (gm_own, 0)),
                        ([(hidden_far, 0, width), (early_a_far, 0, width)], (gm_far, half)),
                    ],
                ),
            ],
            n_dp,
            0,
            0,
            small if rides else None,
        ),
    )
    third.advance()
    second.advance()
    fc2.advance()
    fc1.advance()
    out_far = across_seq(add("out_add", token, out_far, out_far_core))
    back = run(
        result_kernel,
        "result",
        [biases, grad_hidden, back_a, after_attn, out_own, out_own_core, out_far],
        [shape((rows, 2 * width + half), BF)],
        [],
        0,
        work // 100,
    )[0]
    back = mirror(back)
    back_b = lax.ppermute(later(back_b), ("dp", "seq"), turn_back_perm)
    if not rides:
        small = small[:12]
        small = small + across_seq(small)
        for bit in range(bits):
            small = small + across_bit(small, bit)
    third.advance()
    while fc2.step + 1 < len(fc2.order):
        fc2.advance()
        fc1.advance()
    own, far = run(
        half_kernel,
        "half",
        [fc2.keep, *fc2.got, fc1.keep, *fc1.got],
        [shape((2, piece, half), F32), shape((2, piece, half), BF)],
        [],
        0,
        work // 100,
    )
    far = across_seq(far)
    second.advance()
    output, grad_hidden, grad_skip = run(
        home_kernel,
        "home",
        [(counts, IN_SMEM), back, back_b],
        [token, token, shape((2 * rows, half), BF)],
        [],
        0,
        work // 100,
    )
    while third.step + 1 < len(third.order):
        third.advance()
    while second.step + 1 < len(second.order):
        second.advance()
    out_w_fc2, out_w_fc1 = run(
        join_ff_kernel,
        "join_ff",
        [own, far],
        [shape((2 * piece, half), F32)] * 2,
        [],
        0,
        work // 100,
    )
    if even:
        third_rows = 3 * split // 2
        third_own, third_far = run(
            third_half_kernel,
            "third_half",
            [third.keep, *third.got],
            [shape((third_rows, half), F32), shape((third_rows, half), BF)],
            [],
            0,
            work // 100,
        )
        third_far = across_seq(third_far)
    ends = [shape((split, half), F32), shape((2 * split, half), F32)]
    if rides:
        out_w_proj, out_w_skip, grad_gains, grad_biases, grad_fc1_bias = run(
            functools.partial(ride_ends_kernel, split, pairs),
            "ends",
            [second.keep, *second.got, *second.riding],
            ends + [shape((2, width), F32), shape((5, width), F32), shape((ff // LANES, LANES), F32)],
            [pltpu.VMEM((16, width), F32), pltpu.VMEM((8, ff), F32)],
            0,
            work // 100,
        )
        grad_fc1_bias = grad_fc1_bias.reshape(ff)
    else:
        out_w_proj, out_w_skip = run(
            functools.partial(ends_kernel, split), "ends", [second.keep, *second.got], ends, [], 0, work // 100
        )
        grad_gains, grad_biases = small[:2], small[2:7]
        grad_fc1_bias = small[7:11].reshape(2, 2, pairs, piece).transpose(2, 0, 1, 3).reshape(ff)
    if even:
        (out_w_qkv,) = run(
            third_join_kernel,
            "third_join",
            [third_own, third_far],
            [shape((2 * third_rows, half), F32)],
            [],
            0,
            work // 100,
        )
    else:
        out_w_qkv = (third.keep[0].astype(F32) + third.got[0][0].astype(F32)).T
    out_w_fc1 = out_w_fc1.T
    if even:
        out_w_qkv = out_w_qkv.T
    return (
        output[None],
        grad_hidden[None],
        grad_skip[None],
        out_w_skip,
        out_w_qkv,
        out_w_proj,
        out_w_fc1,
        out_w_fc2,
        grad_gains,
        grad_biases,
        grad_fc1_bias,
    )


def solution(mesh):
    return jax.shard_map(
        shards,
        mesh=mesh,
        in_specs=(
            P("dp", "seq", None),
            P("dp", None, "seq"),
            P("dp", "seq", None),
            P("dp"),
            P("dp"),
            P(),
            P(),
            P(),
            P(),
            P(),
            P(),
            P(),
            P(),
        ),
        out_specs=(
            P("dp", "seq", None),
            P("dp", "seq", None),
            P("dp", None, "seq"),
            P("dp", "seq"),
            P("seq", "dp"),
            P("dp", "seq"),
            P("seq", "dp"),
            P("dp", "seq"),
            P(),
            P(),
            P(),
        ),
        check_vma=False,
    )
```

```python
import functools

import jax
import jax.numpy as jnp
from jax import lax
from jax.experimental import pallas as pl
from jax.experimental.pallas import tpu as pltpu
from jax.sharding import PartitionSpec as P

HEADS = 16
PADDED = 2
TSTEPS = 1000

EPSILON = 1e-06
NEG_FILL = -1e30
BF = jnp.bfloat16
F32 = jnp.float32
MIB = 1 << 20
LANES = 128
GAP = 16


def dot(left, right, dims):
    return lax.dot_general(left, right, ((dims[:1], dims[1:]), ((), ())), preferred_element_type=F32)


def norm(value):
    center = value - jnp.mean(value, axis=-1, keepdims=True)
    rstd = lax.rsqrt(jnp.mean(center * center, axis=-1, keepdims=True) + EPSILON)
    return center * rstd, rstd


def norm_back(grad, xhat, rstd, gain):
    scaled = grad * gain
    return rstd * (
        scaled
        - jnp.mean(scaled, axis=-1, keepdims=True)
        - xhat * jnp.mean(scaled * xhat, axis=-1, keepdims=True)
    )


def pick(array, index, axis):
    return lax.dynamic_index_in_dim(array, index, axis, keepdims=False)


def shape(dims, dtype):
    return jax.ShapeDtypeStruct(dims, dtype)


def padded(dims, dtype):
    dims = (1,) * (2 - len(dims)) + tuple(dims)
    size = -(-dims[-2] // 16) * 16 * -(-dims[-1] // LANES) * LANES
    for dim in dims[:-2]:
        size *= dim
    return size * jnp.dtype(dtype).itemsize


COMPUTE = ("gather",)
PIECES = 1
UNROLL = True
GATHER_MIB = 34
SCALE = 0.3
TAKES = {
    "pack": 12.0,
    "gather": 8.0,
    "first": 4.4,
    "attend": 6.6,
    "mlp": 6.0,
    "outer": 3.2,
    "attend_back": 10.3,
    "last": 6.3,
    "outer_second": 0.3,
    "outer_third": 0.3,
    "third": 0.3,
    "second": 0.3,
    "fc1": 0.3,
    "fc2": 0.3,
}


IN_VMEM = pl.BlockSpec(memory_space=pltpu.VMEM)
IN_SMEM = pl.BlockSpec(memory_space=pltpu.SMEM)
IN_ANY = pl.BlockSpec(memory_space=pl.ANY)
IN_HBM = pl.BlockSpec(memory_space=pltpu.HBM)


def call(kernel, name, operands, outs, scratch, mib, flops, after=()):
    takes = TAKES.get(name, TAKES.get(name.split("_")[0], 1.0)) * SCALE
    outs = [*outs, shape((8, LANES), F32)]
    inputs = len(operands)
    marks = len(after)
    if not mib:
        need = sum(padded(a.shape, a.dtype) for a, spec in operands if spec is IN_VMEM)
        need += sum(padded(o.shape, o.dtype) for o in outs)
        need += sum(padded(b.shape, b.dtype) for b in scratch if b.memory_space == pltpu.VMEM)
        mib = need * 9 // 8 // MIB + 4

    def body(*refs):
        mark = refs[inputs + marks + len(outs) - 1]
        mark[...] = jnp.zeros_like(mark)
        kernel(*refs[:inputs], *refs[inputs + marks : inputs + marks + len(outs) - 1], *refs[inputs + marks + len(outs) :])

    return pl.pallas_call(
        body,
        out_shape=outs,
        in_specs=[spec for _, spec in operands] + [IN_ANY] * marks,
        out_specs=[IN_VMEM] * len(outs),
        scratch_shapes=scratch,
        compiler_params=pltpu.CompilerParams(vmem_limit_bytes=mib * MIB),
        cost_estimate=pl.CostEstimate(flops=int(takes * 1e9), bytes_accessed=1 if name in COMPUTE else int(takes * 3.6e6), transcendentals=0),
        name=name,
    )(*[a for a, _ in operands], *after)


def fetch(pairs, sems):
    copies = [pltpu.make_async_copy(src, dst, sems.at[i]) for i, (src, dst) in enumerate(pairs)]
    for copy in copies:
        copy.start()
    return copies


def gather_kernel(pieces, ids, w_fc1, w_fc2, bias, w1, w2, b1, sems):
    core, seq = ids[1], ids[0]
    piece_size = w1.shape[1] // pieces
    which = [4 * m + 2 * core + seq for m in range(pieces)]
    spots = [w * piece_size for w in which]
    copies = fetch([(w_fc2.at[w], w2.at[m]) for m, w in enumerate(which)], sems)
    lane = lax.broadcasted_iota(jnp.int32, (8, LANES), 1)
    for m in range(pieces):
        base, into = m * piece_size // LANES * LANES, m * piece_size % LANES
        window = [bias[pl.ds(spots[m] // LANES + i, 1), :] for i in range(2)]
        window = jnp.concatenate([jnp.broadcast_to(x, (8, LANES)) for x in window], 1)
        turn = (into - spots[m] % LANES + 2 * LANES) % (2 * LANES)
        window = pltpu.roll(window, turn, 1)
        left = window[:, :LANES]
        if into:
            left = jnp.where(lane >= into, left, b1[:, base : base + LANES])
        b1[:, base : base + LANES] = left
        b1[:, base + LANES : base + 2 * LANES] = window[:, LANES:]
    source = lax.broadcasted_iota(jnp.int32, (2 * LANES, 2 * LANES), 0)
    target = lax.broadcasted_iota(jnp.int32, (2 * LANES, 2 * LANES), 1)
    before = {}
    for m in range(pieces):
        base = m * piece_size // LANES * LANES
        column = target + (base - m * piece_size)
        take = jnp.logical_and(column >= 0, column < piece_size)
        take = jnp.logical_and(take, source == column + spots[m] % LANES)
        window = pl.ds(pl.multiple_of(spots[m] // LANES * LANES, LANES), 2 * LANES)
        part = dot(w_fc1[:, window], take.astype(F32).astype(BF), (1, 0))
        for at, half in ((base, part[:, :LANES]), (base + LANES, part[:, LANES:])):
            before[at] = before[at] + half if at in before else half
        for at in [x for x in before if x <= base]:
            w1[:, at : at + LANES] = before.pop(at).astype(BF)
    for at, half in before.items():
        w1[:, at : at + LANES] = half.astype(BF)
    for copy in copies:
        copy.wait()


def pack_kernel(ids, skip_in, skip_a, skip_b, skip, sems):
    rows = skip_a.shape[0]
    seq = ids[0]
    fetch([(skip_in, skip)], sems)[0].wait()
    whole = skip[...].astype(F32)
    top, bottom = whole[:rows], whole[rows:]
    skip_a[...] = jnp.where(seq == 0, top, bottom).astype(BF)
    skip_b[...] = jnp.where(seq == 0, bottom, top).astype(BF)


def grad_out_kernel(ids, timesteps, counts, cotangent, g_home, sums):
    rows, width = g_home.shape
    time = jnp.zeros((1, 1), F32) + timesteps[0].astype(F32)
    weight = jax.nn.sigmoid(12.0 * time / TSTEPS - 6.0)
    spot = lax.broadcasted_iota(jnp.int32, (rows, 1), 0) + ids[0] * rows
    live = jnp.logical_and(spot < 2 * rows - PADDED, counts[0] > 0)
    g = cotangent[...].astype(F32) * jnp.where(live, weight, 0.0)
    g_home[...] = g.astype(BF)
    sums[...] = jnp.concatenate([jnp.sum(g, axis=0, keepdims=True), jnp.zeros((7, width), F32)], 0)


def first_kernel(ids, hidden, skip_a, skip_b, w_skip, w_qkv, gains, biases, merged, early_a, early, q, kv):
    width = hidden.shape[1]
    half = width // 2
    core = ids[1]
    a, b = skip_a[...].astype(F32), skip_b[...].astype(F32)
    low = jnp.where(core == 0, a, b).astype(BF)
    high = jnp.where(core == 0, b, a).astype(BF)
    early_a[:, :half] = low
    early_a[:, half:] = high
    total = dot(hidden[...], w_skip[:width], (1, 0)) + biases[0:1]
    total += dot(low, w_skip[width : width + half], (1, 0))
    total += dot(high, w_skip[width + half :], (1, 0))
    merged[...] = total
    xhat, _ = norm(total)
    one = (xhat * gains[0:1] + biases[1:2]).astype(BF)
    early[...] = one
    kv[...] = dot(one, w_qkv[:, width:], (1, 0)).astype(BF)
    q[...] = dot(one, w_qkv[:, :width], (1, 0)).astype(BF)


def head_windows(width):
    size = width // HEADS
    spans = []
    for h in range(HEADS):
        low, high = h * size, (h + 1) * size
        t0, t1 = low // LANES, (high - 1) // LANES + 1
        spans.append((h, low, high, t0 * LANES, t1 * LANES))
    return spans


def lane_mask(low, high, first, last):
    lane = lax.broadcasted_iota(jnp.int32, (1, last - first), 1) + first
    return jnp.logical_and(lane >= low, lane < high)


def key_mask(core, rows, pitch, axis=1):
    spot = lax.broadcasted_iota(jnp.int32, (1, 2 * pitch) if axis else (2 * pitch, 1), axis)
    other = spot >= pitch
    here = jnp.where(other, spot - pitch, spot)
    last_half = jnp.where(other, 1 - core, core) == 1
    limit = jnp.where(last_half, rows - PADDED, rows)
    return here < limit


def lay_keys(keys, values, kv_own, kv_other, rows, pitch, width):
    for buf, at in ((keys, 0), (values, width)):
        buf[...] = jnp.zeros_like(buf)
        buf[0:rows] = kv_own[:, at : at + width]
        buf[pitch : pitch + rows] = kv_other[:, at : at + width]


def attend_kernel(ids, q, kv_own, kv_other, merged, skips, early, w_proj, gains, biases, early_a, early_b, after, normed, log_total, keys, values, wp, sems):
    rows, width = q.shape
    pitch = keys.shape[0] // 2
    copies = fetch([(w_proj, wp)], sems)
    lay_keys(keys, values, kv_own, kv_other, rows, pitch, width)
    valid = key_mask(ids[1], rows, pitch)
    scale = (width // HEADS) ** (-0.5)
    lane = lax.broadcasted_iota(jnp.int32, (rows, LANES), 1)
    tiles = [jnp.zeros((rows, LANES), F32) for _ in range(width // LANES)]
    logs = jnp.zeros((rows, LANES), F32)
    for h, low, high, first, last in head_windows(width):
        mask = lane_mask(low, high, first, last)
        mine = q[:, first:last] * mask.astype(F32).astype(BF)
        scores = jnp.where(valid, dot(mine, keys[:, first:last], (1, 1)) * scale, NEG_FILL)
        top = jnp.max(scores, axis=-1, keepdims=True)
        expo = jnp.exp(scores - top)
        total = jnp.sum(expo, axis=-1, keepdims=True)
        probs = (expo * (1.0 / total)).astype(BF)
        logs = jnp.where(lane == h, top + jnp.log(total), logs)
        part = dot(probs, values[:, first:last], (1, 0))
        for t in range(first, last, LANES):
            tiles[t // LANES] = jnp.where(
                mask[:, t - first : t - first + LANES], part[:, t - first : t - first + LANES], tiles[t // LANES]
            )
    log_total[...] = logs
    mixed = jnp.concatenate(tiles, 1)
    half = width // 2
    early_a[:, :width] = skips[...]
    early_a[:, width:] = mixed[:, :half].astype(BF)
    early_b[:, :width] = early[...]
    early_b[:, width:] = mixed[:, half:].astype(BF)
    mixed = mixed.astype(BF)
    copies[0].wait()
    value = merged[...] + dot(mixed, wp[...], (1, 0)) + biases[2:3]
    after[...] = value
    xhat, _ = norm(value)
    normed[...] = (xhat * gains[1:2] + biases[3:4]).astype(BF)


def attend_back_kernel(
    ids, gn_mine, gn_core, gn_far, g_home, g_cross, after, q, kv_own, kv_other, log_total, w_proj, gains,
    grad_after, ga_own, ga_far, grad_q, gkv_own, gk_other, gv_other, sums,
    keys, values, wp, gk, gv, sems,
):
    rows, width = q.shape
    half = width // 2
    pitch = keys.shape[0] // 2
    copies = fetch([(w_proj, wp)], sems)
    gn = gn_mine[...] + gn_core[...].astype(F32) + gn_far[...].astype(F32)
    xhat, rstd = norm(after[...])
    g_out = jnp.where(ids[0] == ids[1], g_home[...].astype(F32), g_cross[...].astype(F32))
    value = g_out + norm_back(gn, xhat, rstd, gains[1:2])
    grad_after[...] = value
    low = value.astype(BF)
    halves = value[:, :half], value[:, half:]
    ga_own[...] = jnp.where(ids[0] == 0, halves[0], halves[1]).astype(BF)
    ga_far[...] = jnp.where(ids[0] == 0, halves[1], halves[0]).astype(BF)
    sums[...] = jnp.concatenate(
        [
            jnp.sum(gn * xhat, axis=0, keepdims=True),
            jnp.sum(gn, axis=0, keepdims=True),
            jnp.sum(value, axis=0, keepdims=True),
            jnp.zeros((5, width), F32),
        ],
        0,
    )
    lay_keys(keys, values, kv_own, kv_other, rows, pitch, width)
    valid = key_mask(ids[1], rows, pitch, 0)
    scale = (width // HEADS) ** (-0.5)
    copies[0].wait()
    grad_mixed = dot(low, wp[...], (1, 1)).astype(BF)
    gk[...] = jnp.zeros_like(gk)
    gv[...] = jnp.zeros_like(gv)
    tiles = [jnp.zeros((rows, LANES), F32) for _ in range(width // LANES)]
    logs = log_total[...].T
    for h, start, stop, first, last in head_windows(width):
        mask = lane_mask(start, stop, first, last)
        low_mask = mask.astype(F32).astype(BF)
        mine = q[:, first:last] * low_mask
        gm = grad_mixed[:, first:last] * low_mask
        scores = jnp.where(valid, dot(keys[:, first:last], mine, (1, 1)) * scale, NEG_FILL)
        probs = jnp.exp(scores - logs[h : h + 1, :])
        gp = dot(values[:, first:last], gm, (1, 1))
        gs = (probs * (gp - jnp.sum(gp * probs, axis=0, keepdims=True))).astype(BF)
        part = dot(gs, keys[:, first:last], (0, 0))
        for t in range(first, last, LANES):
            tiles[t // LANES] = jnp.where(
                mask[:, t - first : t - first + LANES], part[:, t - first : t - first + LANES], tiles[t // LANES]
            )
        gk[:, first:last] += dot(gs, mine, (1, 0))
        gv[:, first:last] += dot(probs.astype(BF), gm, (1, 0))
    for t, tile in enumerate(tiles):
        grad_q[:, t * LANES : (t + 1) * LANES] = (tile * scale).astype(BF)
    gkv_own[:, :width] = gk[0:rows] * scale
    gkv_own[:, width:] = gv[0:rows]
    gk_other[...] = (gk[pitch : pitch + rows] * scale).astype(BF)
    gv_other[...] = gv[pitch : pitch + rows].astype(BF)


def lay_rows(buf, blocks):
    rows = blocks[0].shape[0]
    pitch = buf.shape[0] // len(blocks)
    if pitch > rows:
        buf[...] = jnp.zeros_like(buf)
    for i, block in enumerate(blocks):
        buf[i * pitch : i * pitch + rows] = block[...]


def lay_chosen(buf, flag, pairs):
    rows = pairs[0][0].shape[0]
    pitch = buf.shape[0] // len(pairs)
    buf[...] = jnp.zeros_like(buf)
    for way, chosen in enumerate((flag, jnp.logical_not(flag))):

        @pl.when(chosen)
        def _(way=way):
            for i, pair in enumerate(pairs):
                buf[i * pitch : i * pitch + rows] = pair[way][...]


def mlp_kernel(ids, n0, n1, g0a, g0b, g1a, g1b, w1, b1, w2, activ, grad_inner, n_all, g_all, gn_mine, gn_other, sums, inner_v, grad_v):
    rows, width = n0.shape
    units = w1.shape[1]
    lay_rows(n_all, (n0, n1))
    lay_chosen(g_all, ids[0] == ids[1], ((g0a, g0b), (g1a, g1b)))
    height = n_all.shape[0]
    pitch = height // 2
    step = 3 * LANES
    chunk = 48
    root = 0.5**0.5
    bell = (0.5 / jnp.pi) ** 0.5
    for j in range(units // step):
        cols = slice(j * step, (j + 1) * step)
        inner_v[...] = dot(n_all[...], w1[:, cols], (1, 0))
        grad_v[...] = dot(g_all[...], w2[cols, :], (1, 1))
        bias = b1[0:1, cols]

        def body(i, total):
            at = pl.ds(pl.multiple_of(i * chunk, chunk), chunk)
            x = inner_v[at] + bias
            cdf = 0.5 + 0.5 * lax.erf(x * root)
            activ[at, cols] = (x * cdf).astype(BF)
            g = grad_v[at] * (cdf + x * jnp.exp(-0.5 * x * x) * bell)
            grad_inner[at, cols] = g.astype(BF)
            return total + jnp.sum(g, axis=0, keepdims=True)

        sums[0:1, cols] = lax.fori_loop(0, height // chunk, body, jnp.zeros((1, step), F32), unroll=UNROLL)
    for j in range(width // step):
        cols = slice(j * step, (j + 1) * step)
        part = dot(grad_inner[...], w1[cols, :], (1, 1))
        gn_mine[:, cols] = part[:rows]
        gn_other[:, cols] = part[pitch : pitch + rows].astype(BF)


def mlp_out_kernel(activ_own, activ_far, w2, own, far, own_core, far_core):
    rows = own.shape[0]
    pitch = activ_own.shape[0] // 2
    step = 3 * LANES
    for activ, mine, other in ((activ_far, far, far_core), (activ_own, own, own_core)):
        for j in range(w2.shape[1] // step):
            cols = slice(j * step, (j + 1) * step)
            part = dot(activ[...], w2[:, cols], (1, 0))
            mine[:, cols] = part[:rows]
            other[:, cols] = part[pitch : pitch + rows].astype(BF)


def split_blocks(total, keep, sends, at, mine, stride):
    count = keep.shape[0]
    rows = total.shape[0] // (2 * count)
    cols = keep.shape[2]
    per = sends[0].shape[0]
    for way in range(2):

        @pl.when(mine == way)
        def _(way=way):
            slot = 0
            for i in range(2 * count):
                if i // stride % 2:
                    continue
                stay, go = (i, i + stride) if way == 0 else (i + stride, i)
                keep[slot, at : at + rows] = total[stay * rows : (stay + 1) * rows].astype(BF)
                sends[slot // per][slot % per, at : at + rows, :cols] = total[go * rows : (go + 1) * rows].astype(BF)
                slot += 1


def outer_kernel(stride, bit, layout, pieces, ids, *refs):
    spots = iter(refs)
    operands = [
        [([(next(spots), *span) for span in left], (next(spots), right)) for left, right in parts] for parts in layout
    ]
    outs = [next(spots) for _ in range(1 + pieces if stride else len(layout))]
    at = 0
    for i, parts in enumerate(operands):
        total, left, right = next(spots), next(spots), next(spots)
        pitch = left.shape[0] // len(parts)
        cols = right.shape[1]
        for p, (lefts, (y, first)) in enumerate(parts):
            rows = lefts[0][0].shape[0]
            if pitch > rows:
                left[p * pitch : (p + 1) * pitch] = jnp.zeros((pitch, left.shape[1]), BF)
                right[p * pitch : (p + 1) * pitch] = jnp.zeros((pitch, cols), BF)
            right[p * pitch : p * pitch + rows] = y[:rows, first : first + cols]
            spot = 0
            for x, start, n in lefts:
                left[p * pitch : p * pitch + rows, spot : spot + n] = x[:, start : start + n]
                spot += n
        step = 3 * LANES
        for j in range(0, left.shape[1], step):
            span = slice(j, min(j + step, left.shape[1]))
            total[span, :] = dot(left[:, span], right[...], (0, 0))
        if stride:
            split_blocks(total, outs[0], outs[1:], at, ids[1 + bit], stride)
            at += left.shape[1] // (2 * outs[0].shape[0])
        else:
            outs[i][...] = total[...].astype(BF)


def combine_kernel(stride, bit, ids, keep, *refs):
    gots, kept, send = refs[:-2], refs[-2], refs[-1]
    slot = 0
    cols = keep.shape[2]
    per = gots[0].shape[0]

    def total(i):
        return keep[i].astype(F32) + gots[i // per][i % per, :, :cols].astype(F32)

    for i in range(keep.shape[0]):
        if i // stride % 2:
            continue
        a, b = total(i), total(i + stride)
        kept[slot] = jnp.where(ids[1 + bit] == 0, a, b).astype(BF)
        send[slot, :, :cols] = jnp.where(ids[1 + bit] == 0, b, a).astype(BF)
        slot += 1


def ride_outer_kernel(stride, bit, layout, pieces, ids, *refs):
    inputs = sum(len(left) + 1 for parts in layout for left, _ in parts)
    operands, small, outs, scratch = refs[:inputs], refs[inputs], refs[inputs + 1 : inputs + 3 + pieces], refs[inputs + 3 + pieces :]
    keep, sends, riding = outs[0], outs[1:-1], outs[-1]
    outer_kernel(stride, bit, layout, pieces, ids, *operands, keep, *sends, *scratch)
    far = operands[-1]
    total = small[...] + far[far.shape[0] - 16 :, :].astype(F32)
    cols = keep.shape[2]
    extra = sends[0].shape[2] - cols
    for j in range(small.shape[1] // extra):
        riding[12 * j : 12 * j + 12, :] = total[:12, extra * j : extra * (j + 1)]
    for send in sends:
        send[:, :, cols:] = jnp.zeros((send.shape[0], send.shape[1], extra), BF)
    sends[0][0, :, cols:] = riding[...].astype(BF)


def ride_combine_kernel(stride, bit, ids, keep, riding, *refs):
    gots, (kept, send, rode) = refs[:-3], refs[-3:]
    combine_kernel(stride, bit, ids, keep, *gots, kept, send)
    cols = keep.shape[2]
    total = riding[...] + gots[0][0, :, cols:].astype(F32)
    rode[...] = total
    if send.shape[0] > 1:
        send[1:, :, cols:] = jnp.zeros((send.shape[0] - 1, send.shape[1], send.shape[2] - cols), BF)
    send[0, :, cols:] = total.astype(BF)


def ride_ends_kernel(split, pieces, ids, keep, got, riding, proj, skip, gains, biases, units, buf, line):
    cols = keep.shape[2]
    total = keep[0].astype(F32) + got[0, :, :cols].astype(F32)
    proj[...] = total[:split]
    skip[...] = total[split:]
    extra = riding.shape[1]
    small = riding[...] + got[0, :, cols:].astype(F32)
    for j in range(buf.shape[1] // extra):
        buf[:12, extra * j : extra * (j + 1)] = small[12 * j : 12 * j + 12]
    gains[...] = buf[:2]
    biases[...] = buf[2:7]
    piece = buf.shape[1] // pieces
    for m in range(pieces):
        for i in range(4):
            at = (4 * m + i) * piece
            line[0:1, at : at + piece] = buf[7 + i : 8 + i, piece * m : piece * (m + 1)]
    for t in range(units.shape[0]):
        units[t : t + 1, :] = line[0:1, t * LANES : (t + 1) * LANES]


def add_kernel(ids, *refs):
    total = refs[0][...].astype(F32)
    for ref in refs[1:-1]:
        total += ref[...].astype(F32)
    refs[-1][...] = total.astype(refs[-1].dtype)


def project_kernel(blocks, ids, grad_q, gkv_own, gk_core, gv_core, gkv, own, late):
    total = gkv_own[...] + jnp.concatenate([gk_core[...], gv_core[...]], 1).astype(F32)
    gkv[...] = total.astype(BF)
    whole = jnp.concatenate([grad_q[...].astype(F32), total], 1)
    size = whole.shape[1] // (2 * blocks)
    parts = [
        jnp.concatenate([whole[:, (2 * j + s) * size : (2 * j + s + 1) * size] for j in range(blocks)], 1)
        for s in range(2)
    ]
    own[...] = jnp.where(ids[0] == 0, parts[0], parts[1]).astype(BF)
    late[...] = jnp.where(ids[0] == 0, parts[1], parts[0]).astype(BF)


def result_kernel(ids, biases, grad_hidden, back_a, *refs):
    total = biases[4:5]
    for ref in refs[:-1]:
        total = total + ref[...].astype(F32)
    width = grad_hidden.shape[1]
    refs[-1][:, :width] = total.astype(BF)
    refs[-1][:, width : 2 * width] = grad_hidden[...]
    refs[-1][:, 2 * width :] = back_a[...]


def half_kernel(ids, keep_two, got_two, keep_one, got_one, own, far):
    half = own.shape[2]
    for i, (keep, got) in enumerate(((keep_two, got_two), (keep_one, got_one))):
        total = keep[0].astype(F32) + got[0].astype(F32)
        left, right = total[:, :half], total[:, half:]
        own[i] = jnp.where(ids[0] == 0, left, right)
        far[i] = jnp.where(ids[0] == 0, right, left).astype(BF)


def join_ff_kernel(ids, own, far, *outs):
    rows = own.shape[1]
    for i, out in enumerate(outs):
        here, there = own[i], far[i].astype(F32)
        out[:rows] = jnp.where(ids[0] == 0, here, there)
        out[rows:] = jnp.where(ids[0] == 0, there, here)


def ends_kernel(split, ids, keep_two, got_two, proj, skip):
    total = keep_two[0].astype(F32) + got_two[0].astype(F32)
    proj[...] = total[:split]
    skip[...] = total[split:]


def third_half_kernel(ids, keep, got, own, far):
    half = own.shape[1]
    total = keep[0].astype(F32) + got[0].astype(F32)
    left, right = total[:, :half], total[:, half:]
    own[...] = jnp.where(ids[0] == 0, left, right)
    far[...] = jnp.where(ids[0] == 0, right, left).astype(BF)


def third_join_kernel(ids, own, far, out):
    here, there = own[...], far[...].astype(F32)
    rows = own.shape[0]
    out[:rows] = jnp.where(ids[0] == 0, here, there)
    out[rows:] = jnp.where(ids[0] == 0, there, here)


def home_kernel(ids, counts, back, back_b, output, grad_hidden, grad_skip):
    rows, width = output.shape
    grad_hidden[...] = back[:, width : 2 * width]
    seq = ids[0]
    spot = lax.broadcasted_iota(jnp.int32, (rows, 1), 0) + seq * rows
    live = jnp.logical_and(spot < 2 * rows - PADDED, counts[0] > 0)
    output[...] = jnp.where(live, back[:, :width].astype(F32), 0.0).astype(BF)
    a, b = back[:, 2 * width :].astype(F32), back_b[...].astype(F32)
    grad_skip[:rows] = jnp.where(seq == 0, a, b).astype(BF)
    grad_skip[rows:] = jnp.where(seq == 0, b, a).astype(BF)


def last_kernel(
    ids, grad_q, gkv, merged, grad_after, w_skip, w_qkv, gains, sums_two, sums_out, units_own, units_far, ga_far,
    gm_own, gm_far, grad_hidden, back_a, back_b, small,
):
    width = merged.shape[1]
    half = width // 2
    xhat, rstd = norm(merged[...])
    gn = dot(grad_q[...], w_qkv[:, :width], (1, 1))
    gn += dot(gkv[...], w_qkv[:, width:], (1, 1))
    value = grad_after[...] + norm_back(gn, xhat, rstd, gains[0:1])
    units = units_own[0:1] + units_far[0:1]
    spot = 2 * ids[1] + ids[0]
    sums = jnp.concatenate(
        [
            jnp.sum(gn * xhat, axis=0, keepdims=True),
            sums_two[0:1],
            jnp.sum(value, axis=0, keepdims=True),
            jnp.sum(gn, axis=0, keepdims=True),
            sums_two[2:3],
            sums_two[1:2],
            sums_out[0:1],
        ]
        + [jnp.where(spot == i, units, 0.0) for i in range(4)]
        + [jnp.zeros((5, width), F32)],
        0,
    )
    small[...] = sums
    halves = value[:, :half], value[:, half:]
    rows = value.shape[0]
    gm_own[...] = jnp.where(ids[0] == 0, halves[0], halves[1]).astype(BF)
    gm_far[:rows, :half] = ga_far[...]
    gm_far[:rows, half:] = jnp.where(ids[0] == 0, halves[1], halves[0]).astype(BF)
    gm_far[gm_far.shape[0] - 16 :] = sums.astype(BF)
    low = value.astype(BF)
    grad_hidden[...] = dot(low, w_skip[:width], (1, 1)).astype(BF)
    a = dot(low, w_skip[width : width + half], (1, 1))
    b = dot(low, w_skip[width + half :], (1, 1))
    back_a[...] = jnp.where(ids[1] == 0, a, b).astype(BF)
    back_b[...] = jnp.where(ids[1] == 0, b, a).astype(BF)


def shards(
    hidden_in,
    skip_in,
    cotangent,
    timesteps,
    counts,
    w_skip,
    w_qkv,
    w_proj,
    w_fc1,
    w_fc2,
    gains,
    biases,
    fc1_bias,
):
    rows, width = hidden_in.shape[1:]
    half = width // 2
    ff = w_fc1.shape[1]
    n_dp = lax.axis_size("dp")
    bits = n_dp.bit_length() - 1
    pairs = n_dp // 2
    place = lax.axis_index("dp")
    core = place % 2
    seq = lax.axis_index("seq")
    piece = ff // (4 * pairs)
    quarter = pairs * piece
    ids = jnp.stack([seq] + [(place >> b) & 1 for b in range(bits)]).astype(jnp.int32)
    ids = lax.optimization_barrier(ids)
    pitch = -(-rows // GAP) * GAP

    def flat(dp, s):
        return 2 * dp + s

    mirror_perm = [
        (flat(2 * k + c, s), flat(2 * k + s, c)) for k in range(pairs) for c in range(2) for s in range(2)
    ]
    turn = {(0, 0): (1, 0), (1, 0): (1, 1), (1, 1): (0, 1), (0, 1): (0, 0)}
    turn_perm = [
        (flat(2 * k + c, s), flat(2 * k + d[0], d[1])) for k in range(pairs) for (c, s), d in turn.items()
    ]
    turn_back_perm = [(b, a) for a, b in turn_perm]

    def mirror(x):
        return lax.ppermute(x, ("dp", "seq"), mirror_perm)

    def across_seq(x):
        return lax.ppermute(x, "seq", [(0, 1), (1, 0)])

    def across_bit(x, bit):
        return lax.ppermute(x, "dp", [(i, i ^ (1 << bit)) for i in range(n_dp)])

    def across_core(x):
        return across_bit(x, 0)

    def swap_if(flag, a, b, axis):
        return jnp.where(flag, jnp.concatenate([b, a], axis), jnp.concatenate([a, b], axis))

    def my_bit(bit):
        return (place >> bit) & 1

    marks = []

    def run(kernel, name, operands, outs, scratch, mib, flops, after=()):
        results = call(
            kernel,
            name,
            [(ids, IN_SMEM)] + [a if isinstance(a, tuple) else (a, IN_VMEM) for a in operands],
            outs,
            scratch,
            mib,
            flops,
            [*marks[-1:], *after],
        )
        marks.append(results[-1])
        return results[:-1]

    def tie(x, *others):
        return lax.optimization_barrier((x, *others))[0]

    def later(x):
        return lax.optimization_barrier((x, marks[-1]))[0]

    token = shape((rows, width), BF)
    token32 = shape((rows, width), F32)
    half_token = shape((rows, half), BF)
    wide_token = shape((rows, width + half), BF)
    sums = shape((8, width), F32)
    work = 2 * rows * width * width

    hidden = mirror(hidden_in[0])
    far_perm = [
        (flat(2 * k + c, s), flat(2 * k + s, 1 - c)) for k in range(pairs) for c in range(2) for s in range(2)
    ]
    hidden_far = lax.ppermute(hidden_in[0], ("dp", "seq"), far_perm)
    skip_a, skip_b = run(
        pack_kernel,
        "pack",
        [(skip_in[0], IN_ANY)],
        [half_token, half_token],
        [pltpu.VMEM((2 * rows, half), BF), pltpu.SemaphoreType.DMA((1,))],
        0,
        work // 100,
    )
    skip_a = mirror(skip_a)
    skip_b = lax.ppermute(skip_b, ("dp", "seq"), turn_perm)

    if piece % GAP == 0 and piece <= 2 * LANES - 7 * GAP:
        w1, w2, b1 = run(
            functools.partial(gather_kernel, pairs),
            "gather",
            [w_fc1, (w_fc2.reshape(4 * pairs, piece, width), IN_HBM), fc1_bias.reshape(ff // LANES, LANES)],
            [shape((width, quarter), BF), shape((pairs, piece, width), BF), shape((8, quarter), F32)],
            [pltpu.SemaphoreType.DMA((pairs,))],
            GATHER_MIB,
            work // 100,
        )
    else:
        w1 = pick(pick(w_fc1.reshape(width, pairs, 2, 2, piece), core, 2), seq, 2).reshape(width, quarter)
        b1 = pick(pick(fc1_bias.reshape(pairs, 2, 2, piece), core, 1), seq, 1).reshape(1, quarter)
        b1 = jnp.broadcast_to(b1, (8, quarter))
        w2 = pick(pick(w_fc2.reshape(pairs, 2, 2, piece, width), core, 1), seq, 1)
    w2 = w2.reshape(quarter, width)

    g_home, sum_grad_out = run(
        grad_out_kernel,
        "grad_out",
        [(timesteps, IN_SMEM), (counts, IN_SMEM), cotangent[0]],
        [token, sums],
        [],
        0,
        work // 100,
    )

    merged, skips, early, q, kv = run(
        first_kernel,
        "first",
        [hidden, skip_a, skip_b, w_skip, w_qkv, gains, biases],
        [token32, token, token, token, shape((rows, 2 * width), BF)],
        [],
        0,
        5 * work,
        (hidden_far,),

    )
    kv_other = across_core(kv)
    g_far = across_seq(g_home)
    g_other = across_core(g_home)

    key_buf = pltpu.VMEM((2 * pitch, width), BF)
    proj_buf = [pltpu.VMEM((width, width), BF), pltpu.SemaphoreType.DMA((1,))]
    early_a, early_b, after_attn, normed_two, log_total = run(
        attend_kernel,
        "attend",
        [q, kv, kv_other, merged, skips, early, (w_proj, IN_ANY), gains, biases],
        [wide_token, wide_token, token32, token, shape((rows, LANES), F32)],
        [key_buf, key_buf, *proj_buf],
        0,
        2 * work,
    )

    n_far = across_seq(normed_two)
    n_other = across_core(normed_two)
    g_other_far = across_core(later(g_far))

    def mlp(name, n0, n1, *g):
        tall = shape((2 * pitch, quarter), BF)
        wide = shape((2 * pitch, width), BF)
        return run(
            mlp_kernel,
            name,
            [n0, n1, *g, w1, b1, w2],
            [tall, tall, wide, wide, token32, token, shape((8, quarter), F32)],
            [pltpu.VMEM((2 * pitch, 3 * LANES), F32), pltpu.VMEM((2 * pitch, 3 * LANES), F32)],
            0,
            6 * 2 * rows * width * quarter,
        )

    act_own, gi_own, nn_own, gg_own, gn_own, gn_own_core, si_own = mlp(
        "mlp_own", normed_two, n_other, g_home, g_other_far, g_far, g_other
    )
    n_other_far = across_core(later(n_far))
    early_a_far = across_seq(tie(early_a, n_far))
    act_far, gi_far, nn_far, gg_far, gn_far, gn_far_core, si_far = mlp(
        "mlp_far", n_far, n_other_far, g_other, g_far, g_other_far, g_home
    )
    gn_far_core = across_core(gn_far_core)
    gn_own_core = across_core(gn_own_core)

    def outer(name, products, blocks, bit, shift, riding=None, after=()):
        pieces = PIECES if shift == 0 and n_dp // 2 % PIECES == 0 else 1
        lefts = [sum(n for _, _, n in parts[0][0]) for _, parts in products]
        rows_of = [n // blocks for n in lefts]
        inside = all(r % 4 == 0 for r in rows_of)
        cols = products[0][0]
        stride = (1 << (bit - shift)) if inside else 0
        scratch, operands = [], []
        for n, (c, parts) in zip(lefts, products):
            height = -(-parts[0][0][0][0].shape[0] // GAP) * GAP * len(parts)
            scratch += [pltpu.VMEM((n, c), F32), pltpu.VMEM((height, n), BF), pltpu.VMEM((height, c), BF)]
            for left, (right, _) in parts:
                operands += [x for x, _, _ in left] + [right]
        r = sum(rows_of)
        if inside:
            outs = [shape((blocks // 2, r, cols), BF)] + [shape((blocks // 2 // pieces, r, cols), BF)] * pieces
        else:
            outs = [shape((n, cols), BF) for n in lefts]
        layout = [[([span for _, *span in left], right[1]) for left, right in parts] for _, parts in products]
        if riding is not None:
            outs = [outs[0], *[shape((blocks // 2 // pieces, r, cols + extra), BF)] * pieces, shape((r, extra), F32)]
            operands.append(riding)
        results = run(
            functools.partial(outer_kernel if riding is None else ride_outer_kernel, stride, bit, layout, pieces),
            name,
            operands,
            outs,
            scratch,
            0,
            sum(2 * n * cols * 4 * rows for n in lefts),
            after,
        )
        if inside:
            return results[0], results[1 : 1 + pieces], results[1 + pieces :]
        whole = jnp.concatenate([x.reshape(blocks, r, cols) for x, r in zip(results, rows_of)], 1)
        whole = whole.reshape(blocks >> (bit - shift + 1), 2, 1 << (bit - shift), sum(rows_of), cols)
        flat_shape = (blocks // 2, sum(rows_of), cols)
        keep, send = [pick(whole, i, 1).reshape(flat_shape) for i in (my_bit(bit), 1 - my_bit(bit))]
        return keep, [send], []

    def combine(name, keep, gots, left, bit, riding=(), after=()):
        count, r, cols = keep.shape
        stride = 1 << left.index(bit)
        if r % 4 == 0:
            results = run(
                functools.partial(ride_combine_kernel if riding else combine_kernel, stride, bit),
                name,
                [keep, *riding, *gots],
                [shape((count // 2, r, cols), BF), shape((count // 2, r, gots[0].shape[2]), BF)]
                + [shape(x.shape, F32) for x in riding],
                [],
                0,
                work // 100,
                after,
            )
            return results[0], [results[1]], results[2:]
        both = (keep.astype(F32) + gots[0].astype(F32)).astype(BF).reshape(count // (2 * stride), 2, stride, r, cols)
        keep, send = [pick(both, i, 1).reshape(count // 2, r, cols) for i in (my_bit(bit), 1 - my_bit(bit))]
        return keep, [send], []

    class Chain:
        def __init__(self, name, order, parts):
            self.name, self.order = name, order
            self.keep, sends, self.riding = parts
            self.step = 0
            self.left = sorted(order[1:])
            self.got = [across_bit(send, order[0]) for send in sends]

        def advance(self, *after):
            self.step += 1
            if self.step >= len(self.order):
                return
            bit = self.order[self.step]
            self.keep, sends, self.riding = combine(
                f"{self.name}_{self.step}", self.keep, self.got, self.left, bit, self.riding, after
            )
            self.left.remove(bit)
            self.got = [across_bit(send, bit) for send in sends]

    def order_of(first):
        return first + list(range(4, bits))

    def add(name, out, *terms):
        return run(add_kernel, name, list(terms), [out], [], 0, work // 100)[0]

    fc2 = Chain(
        "fc2",
        order_of([1, 2, 3]),
        outer("outer_fc2", [(width, [([(act_own, 0, quarter)], (gg_own, 0)), ([(act_far, 0, quarter)], (gg_far, 0))])], pairs, 1, 1),
    )
    gn_far = across_seq(add("gn_add", token, gn_far, gn_far_core))
    fc1 = Chain(
        "fc1",
        order_of([2, 1, 3]),
        outer("outer_fc1", [(width, [([(gi_own, 0, quarter)], (nn_own, 0)), ([(gi_far, 0, quarter)], (nn_far, 0))])], pairs, 2, 1, None, (early_a_far,)),
    )

    split = width // n_dp
    extra = -half % LANES
    rides = 3 * split % 8 == 0 and extra and 3 * split * extra == 12 * width
    early_b_far = across_seq(tie(early_b, gn_far))
    grad_after, ga_own, ga_far, grad_q, gkv_own, gk_other, gv_other, sums_two = run(
        attend_back_kernel,
        "attend_back",
        [gn_own, gn_own_core, gn_far, g_home, g_other_far, after_attn, q, kv, kv_other, log_total]
        + [(w_proj, IN_ANY), gains],
        [token32, half_token, half_token, token]
        + [shape((rows, 2 * width), F32), token, token, sums],
        [key_buf, key_buf, proj_buf[0], pltpu.VMEM((2 * pitch, width), F32), pltpu.VMEM((2 * pitch, width), F32), proj_buf[1]],
        0,
        3 * work,
    )
    gk_core, gv_core = across_core(gk_other), across_core(gv_other)
    even = 3 * split % 8 == 0
    if even:
        gkv, project_own, late = run(
            functools.partial(project_kernel, n_dp),
            "project",
            [grad_q, gkv_own, gk_core, gv_core],
            [shape((rows, 2 * width), BF), wide_token, wide_token],
            [],
            0,
            work // 100,
        )
        third_cols, normed, normed_far = width, early_b, early_b_far
    else:
        gkv = (gkv_own + jnp.concatenate([gk_core, gv_core], 1).astype(F32)).astype(BF)
        project_own = jnp.concatenate([grad_q, gkv], 1)
        late = project_own
        third_cols = half
        normed, normed_far = [
            lax.dynamic_slice_in_dim(x, seq * half, half, 1) for x in (early_b, early_b_far)
        ]
    third_wide = project_own.shape[1]
    late_far = across_seq(late)
    gm_own, gm_far, grad_hidden, back_a, back_b, small = run(
        last_kernel,
        "last",
        [grad_q, gkv, merged, grad_after, w_skip, w_qkv, gains, sums_two, sum_grad_out, si_own, si_far, ga_far],
        [half_token, shape((pitch + 16, width), BF), token, half_token, half_token, shape((16, width), F32)],
        [],
        0,
        5 * work,
        (early_b_far,),
    )
    gm_far = across_seq(gm_far)

    fc2.advance()
    out_own, out_far, out_own_core, out_far_core = run(
        lambda ids, *refs: mlp_out_kernel(*refs),
        "mlp_out",
        [act_own, act_far, w2],
        [token32, token32, token, token],
        [],
        0,
        2 * 4 * rows * width * quarter,
    )
    out_own_core, out_far_core = across_core(out_own_core), across_core(out_far_core)
    fc1.advance()
    third = Chain(
        "third",
        order_of([0, 2, 1, 3]),
        outer(
            "outer_third",
            [
                (
                    third_cols,
                    [
                        ([(project_own, 0, third_wide)], (normed, 0)),
                        ([(late_far, 0, third_wide)], (normed_far, 0)),
                    ],
                )
            ],
            n_dp,
            0,
            0,
        ),
    )
    second = Chain(
        "second",
        order_of([0, 1, 2, 3]),
        outer(
            "outer_second",
            [
                (
                    half,
                    [
                        ([(early_a, width, half), (early_b, width, half)], (ga_own, 0)),
                        ([(early_a_far, width, half), (early_b_far, width, half)], (gm_far, 0)),
                    ],
                ),
                (
                    half,
                    [
                        ([(hidden, 0, width), (early_a, 0, width)], (gm_own, 0)),
                        ([(hidden_far, 0, width), (early_a_far, 0, width)], (gm_far, half)),
                    ],
                ),
            ],
            n_dp,
            0,
            0,
            small if rides else None,
        ),
    )
    third.advance()
    second.advance()
    fc2.advance()
    fc1.advance()
    out_far = across_seq(add("out_add", token, out_far, out_far_core))
    back = run(
        result_kernel,
        "result",
        [biases, grad_hidden, back_a, after_attn, out_own, out_own_core, out_far],
        [shape((rows, 2 * width + half), BF)],
        [],
        0,
        work // 100,
    )[0]
    back = mirror(back)
    back_b = lax.ppermute(later(back_b), ("dp", "seq"), turn_back_perm)
    if not rides:
        small = small[:12]
        small = small + across_seq(small)
        for bit in range(bits):
            small = small + across_bit(small, bit)
    third.advance()
    while fc2.step + 1 < len(fc2.order):
        fc2.advance()
        fc1.advance()
    own, far = run(
        half_kernel,
        "half",
        [fc2.keep, *fc2.got, fc1.keep, *fc1.got],
        [shape((2, piece, half), F32), shape((2, piece, half), BF)],
        [],
        0,
        work // 100,
    )
    far = across_seq(far)
    second.advance()
    output, grad_hidden, grad_skip = run(
        home_kernel,
        "home",
        [(counts, IN_SMEM), back, back_b],
        [token, token, shape((2 * rows, half), BF)],
        [],
        0,
        work // 100,
    )
    while third.step + 1 < len(third.order):
        third.advance()
    while second.step + 1 < len(second.order):
        second.advance()
    out_w_fc2, out_w_fc1 = run(
        join_ff_kernel,
        "join_ff",
        [own, far],
        [shape((2 * piece, half), F32)] * 2,
        [],
        0,
        work // 100,
    )
    if even:
        third_rows = 3 * split // 2
        third_own, third_far = run(
            third_half_kernel,
            "third_half",
            [third.keep, *third.got],
            [shape((third_rows, half), F32), shape((third_rows, half), BF)],
            [],
            0,
            work // 100,
        )
        third_far = across_seq(third_far)
    ends = [shape((split, half), F32), shape((2 * split, half), F32)]
    if rides:
        out_w_proj, out_w_skip, grad_gains, grad_biases, grad_fc1_bias = run(
            functools.partial(ride_ends_kernel, split, pairs),
            "ends",
            [second.keep, *second.got, *second.riding],
            ends + [shape((2, width), F32), shape((5, width), F32), shape((ff // LANES, LANES), F32)],
            [pltpu.VMEM((16, width), F32), pltpu.VMEM((8, ff), F32)],
            0,
            work // 100,
        )
        grad_fc1_bias = grad_fc1_bias.reshape(ff)
    else:
        out_w_proj, out_w_skip = run(
            functools.partial(ends_kernel, split), "ends", [second.keep, *second.got], ends, [], 0, work // 100
        )
        grad_gains, grad_biases = small[:2], small[2:7]
        grad_fc1_bias = small[7:11].reshape(2, 2, pairs, piece).transpose(2, 0, 1, 3).reshape(ff)
    if even:
        (out_w_qkv,) = run(
            third_join_kernel,
            "third_join",
            [third_own, third_far],
            [shape((2 * third_rows, half), F32)],
            [],
            0,
            work // 100,
        )
    else:
        out_w_qkv = (third.keep[0].astype(F32) + third.got[0][0].astype(F32)).T
    out_w_fc1 = out_w_fc1.T
    if even:
        out_w_qkv = out_w_qkv.T
    return (
        output[None],
        grad_hidden[None],
        grad_skip[None],
        out_w_skip,
        out_w_qkv,
        out_w_proj,
        out_w_fc1,
        out_w_fc2,
        grad_gains,
        grad_biases,
        grad_fc1_bias,
    )


def solution(mesh):
    return jax.shard_map(
        shards,
        mesh=mesh,
        in_specs=(
            P("dp", "seq", None),
            P("dp", None, "seq"),
            P("dp", "seq", None),
            P("dp"),
            P("dp"),
            P(),
            P(),
            P(),
            P(),
            P(),
            P(),
            P(),
            P(),
        ),
        out_specs=(
            P("dp", "seq", None),
            P("dp", "seq", None),
            P("dp", None, "seq"),
            P("dp", "seq"),
            P("seq", "dp"),
            P("dp", "seq"),
            P("seq", "dp"),
            P("dp", "seq"),
            P(),
            P(),
            P(),
        ),
        check_vma=False,
    )
```
